32 devices in a mesh: section: 4 (over y, x), dp: 8 (over z, core).
Axes of the slice: x: 2, y: 2, z: 4, core: 2. Of those that a mesh axis runs over, the one named last changes fastest.
Arguments:
- starting_learned_vectors: bfloat16 [256, 32, 768], P('dp'), may hold values from -6 to 6
- frozen_picture_vectors: bfloat16 [96, 257, 1408], P('dp'), may hold values from -6 to 6
- texts_per_picture: int32 [8, 12], P('dp'), may hold values from 1 to 5, 32 in all within a row
- early_triple_matrix: bfloat16 [768, 2304], replicated, may hold values from -0.21875 to 0.21875
- early_mixing_exit_matrix: bfloat16 [768, 768], replicated, may hold values from -0.4375 to 0.4375
- picture_asker_matrix: bfloat16 [768, 768], replicated, may hold values from -0.21875 to 0.21875
- picture_pair_matrix: bfloat16 [1408, 1536], replicated, may hold values from -0.15625 to 0.15625
- picture_exit_matrix: bfloat16 [768, 768], replicated, may hold values from -0.4375 to 0.4375
- early_widen_matrix: bfloat16 [768, 3072], replicated, may hold values from -0.21875 to 0.21875
- early_narrow_matrix: bfloat16 [3072, 768], replicated, may hold values from -0.109375 to 0.109375
- later_triple_matrix: bfloat16 [768, 2304], replicated, may hold values from -0.21875 to 0.21875
- later_mixing_exit_matrix: bfloat16 [768, 768], replicated, may hold values from -0.4375 to 0.4375
- later_widen_matrix: bfloat16 [768, 3072], replicated, may hold values from -0.21875 to 0.21875
- later_narrow_matrix: bfloat16 [3072, 768], replicated, may hold values from -0.109375 to 0.109375
- standardizer_factors: float32 [5, 768], replicated, may hold values from 0.5 to 1.5
- picture_divisors: float32 [12], replicated, may hold values from 0.45 to 2.8
- closing_cotangent: bfloat16 [256, 32, 768], P('dp'), may hold values from -6 to 6
Outputs:
- final_states: float32 [256, 32, 768], P('dp', None, 'section')
- query_grad: float32 [256, 32, 768], P('dp', None, 'section')
- first_project_grad: float32 [768, 2304], P('dp', 'section')
- first_output_grad: float32 [768, 768], P('dp', 'section')
- image_query_grad: float32 [768, 768], P('dp', 'section')
- image_keyval_grad: float32 [1408, 1536], P('dp', 'section')
- image_output_grad: float32 [768, 768], P('dp', 'section')
- first_expand_grad: float32 [768, 3072], P('dp', 'section')
- first_reduce_grad: float32 [3072, 768], P('dp', 'section')
- second_project_grad: float32 [768, 2304], P('dp', 'section')
- second_output_grad: float32 [768, 768], P('dp', 'section')
- second_expand_grad: float32 [768, 3072], P('dp', 'section')
- second_reduce_grad: float32 [3072, 768], P('dp', 'section')
- norm_gains_grad: float32 [5, 768], replicated
- temperature_grad: float32 [12], replicated
The draws below stay inside these ranges and needn't reach their ends.
Inputs may be any that keep to these rules, and one draw needn't show every extreme that they name: `texts_per_picture`: row d holds the caption counts of the 12 images of index d of dp, in the order of their items, and sums to 32; every row has an image with 5 captions.
All inputs are finite; a program needn't handle non-finite values.
Results may differ from the reference program's by a relative error of at most 0.035.
The reference program's roundings to bfloat16 on the way count: a program that leaves them out, or rounds other values in their place, can miss the bound.
Values may be sent and summed in bfloat16 or wider, within the bound.
A program may use at most 832 MiB of HBM per device.

```python
import math
import jax
import jax.numpy as jnp
import numpy as np
from jax import lax

D = 768
FOCUS_UNITS = 12
PER_UNIT_WIDTH = 64
FF = 3072
Q = 32
P_SIZE = 257
F = 1408
ITEM_DEV = 32
IMG_DEV = 12
ITEMS = 256
IMAGES = 96
N_DP = 8


def block_levels(rng, extent, split, least, top_value):
    def one(dim, blocks):
        steps = jax.random.uniform(jax.random.fold_in(jax.random.fold_in(rng, 6), dim), (blocks,), jnp.float32, least / len(split), top_value / len(split))
        return jnp.repeat(jnp.exp(steps), extent[dim] // blocks).reshape((-1,) + (1,) * (len(extent) - dim - 1))

    loudness = one(*split[0])
    for cut in split[1:]:
        loudness = loudness * one(*cut)
    return loudness


def split_up(count, total, bound, slope):
    weights = [(1 << 20) // math.isqrt(standing ** slope) + 1 for standing in range(2, count + 1)]
    surplus, holding = total - bound - (count - 1), [1] * (count - 1)
    while surplus > 0:
        candidates = [i for i in range(count - 1) if holding[i] < bound]
        whole, left = sum([weights[i] for i in candidates]), surplus
        for i in candidates:
            extra = min(bound - holding[i], max(1, left * weights[i] // whole), surplus)
            holding[i] = holding[i] + extra
            surplus = surplus - extra
    return np.array([bound] + holding)


def ragged(key, amount, total, bound, lean):
    if amount == 2:
        one = jax.random.randint(key, (), max(1, total - bound), min(bound, total - 1) + 1)
        return jnp.stack([one, total - one])
    lengths = jnp.asarray(split_up(amount, total, bound, lean), jnp.int32)
    twos = (amount - 1) // 2
    donor, taker = lengths[1:1 + 2 * twos:2], lengths[2:2 + 2 * twos:2]
    room = jnp.minimum(donor - 1, bound - taker)
    shifted = jax.random.randint(jax.random.fold_in(key, 1), (twos,), 0, 1 << 20) % (room + 1)
    lengths = lengths.at[1:1 + 2 * twos:2].set(donor - shifted).at[2:2 + 2 * twos:2].set(taker + shifted)
    return lengths[jax.random.permutation(jax.random.fold_in(key, 2), amount)]


def normal_values(rng, shape, scale, bound, pieces=(), kind=jnp.bfloat16):
    drawn = scale * jax.random.normal(rng, shape, jnp.float32)
    if pieces:
        drawn = drawn * block_levels(rng, shape, pieces, -0.22, 0.18)
    return jnp.clip(drawn, -bound, bound).astype(kind)


def setup_inputs(seed: int = 0) -> dict:
    key_list = jax.random.split(jax.random.key(seed), 18)
    return {
        "starting_learned_vectors": normal_values(key_list[0], (ITEMS, Q, D), 1.0, 6.0, ((0, 8),)),
        "frozen_picture_vectors": normal_values(key_list[1], (IMAGES, P_SIZE, F), 1.0, 6.0, ((0, 8),)),
        "texts_per_picture": jax.vmap(lambda own: ragged(own, IMG_DEV, ITEM_DEV, 5, 2))(jax.random.split(key_list[2], N_DP)).reshape((N_DP, IMG_DEV)).astype(jnp.int32),
        "early_triple_matrix": normal_values(key_list[3], (D, 3 * D), D ** -0.5, 0.21875),
        "early_mixing_exit_matrix": normal_values(key_list[4], (D, D), (D // 4) ** -0.5, 0.4375),
        "picture_asker_matrix": normal_values(key_list[5], (D, D), D ** -0.5, 0.21875),
        "picture_pair_matrix": normal_values(key_list[6], (F, 2 * D), F ** -0.5, 0.15625),
        "picture_exit_matrix": normal_values(key_list[7], (D, D), (D // 4) ** -0.5, 0.4375),
        "early_widen_matrix": normal_values(key_list[8], (D, FF), D ** -0.5, 0.21875),
        "early_narrow_matrix": normal_values(key_list[9], (FF, D), FF ** -0.5, 0.109375),
        "later_triple_matrix": normal_values(key_list[10], (D, 3 * D), D ** -0.5, 0.21875),
        "later_mixing_exit_matrix": normal_values(key_list[11], (D, D), (D // 4) ** -0.5, 0.4375),
        "later_widen_matrix": normal_values(key_list[12], (D, FF), D ** -0.5, 0.21875),
        "later_narrow_matrix": normal_values(key_list[13], (FF, D), FF ** -0.5, 0.109375),
        "standardizer_factors": jnp.clip(1.0 + 0.1 * jax.random.normal(key_list[14], (5, D), jnp.float32), 0.5, 1.5),
        "picture_divisors": jnp.clip(jnp.exp(jax.random.uniform(key_list[15], (FOCUS_UNITS,), jnp.float32, math.log(0.45), math.log(2.8))), 0.45, 2.8),
        "closing_cotangent": normal_values(key_list[16], (ITEMS, Q, D), 1.0, 6.0, ((0, 8),)),
    }


@jax.custom_vjp
def low(v):
    return lax.optimization_barrier(v.astype(jnp.bfloat16)).astype(jnp.float32)

@jax.custom_vjp
def low_back(v):
    return v

def low_keep(v):
    return (low(v), None)

def low_pass(kept, grad):
    return (grad,)

def back_keep(v):
    return (v, None)

def back_low(kept, grad):
    return (low(grad),)
low.defvjp(low_keep, low_pass)
low_back.defvjp(back_keep, back_low)
EPSILON = 1e-06
HIGHEST_PRECISION = lax.Precision.HIGHEST

def product(left_side, right_side):
    return jnp.dot(left_side, right_side, precision=HIGHEST_PRECISION)

def layer_norm(summed_in, standardizer_factor):
    mean_row = lax.optimization_barrier(jnp.mean(summed_in, axis=-1, keepdims=True))
    centred = summed_in - mean_row
    spread = lax.optimization_barrier(jnp.mean(centred * centred, axis=-1, keepdims=True))
    return centred * lax.rsqrt(spread + EPSILON) * standardizer_factor

def self_block(entries_given, w_project, exit_matrix, standardizer_factor):
    row_count = entries_given.shape[0]
    item_count = row_count // Q
    joined = low_back(low(product(low(entries_given), w_project))).reshape(item_count, Q, 3, FOCUS_UNITS, PER_UNIT_WIDTH)
    queries, key_part, value_part = (joined[:, :, 0], joined[:, :, 1], joined[:, :, 2])
    raw_scores = low_back(jnp.einsum('iqhd,ikhd->ihqk', queries, key_part, precision=HIGHEST_PRECISION))
    softened = low(jax.nn.softmax(raw_scores * PER_UNIT_WIDTH ** (-0.5), axis=-1))
    mixed_heads = low_back(low(jnp.einsum('ihqk,ikhd->iqhd', softened, value_part, precision=HIGHEST_PRECISION)))
    branch = low_back(product(mixed_heads.reshape(row_count, D), exit_matrix))
    return layer_norm(entries_given + branch, standardizer_factor)

def picture_mixing_step(entries_given, paired_entries, asker_matrix, exit_matrix, standardizer_factor, exponent_divisor):
    row_count = entries_given.shape[0]
    item_count = row_count // Q
    queries = low_back(low(product(low(entries_given), asker_matrix))).reshape(item_count, Q, FOCUS_UNITS, PER_UNIT_WIDTH)
    keyval_pairs = paired_entries.reshape(item_count, P_SIZE, 2, FOCUS_UNITS, PER_UNIT_WIDTH)
    raw_scores = low_back(jnp.einsum('iqhd,iphd->ihqp', queries, keyval_pairs[:, :, 0], precision=HIGHEST_PRECISION))
    multiplier = PER_UNIT_WIDTH ** (-0.5) / jnp.clip(exponent_divisor, 0.5, 2.0)
    softened = low(jax.nn.softmax(raw_scores * multiplier[None, :, None, None], axis=-1))
    mixed_heads = low_back(low(jnp.einsum('ihqp,iphd->iqhd', softened, keyval_pairs[:, :, 1], precision=HIGHEST_PRECISION)))
    branch = low_back(product(mixed_heads.reshape(row_count, D), exit_matrix))
    return layer_norm(entries_given + branch, standardizer_factor)

def hidden_block(entries_given, w_expand, w_reduce, standardizer_factor):
    hidden = low_back(low(product(low(entries_given), w_expand)))
    active = low(jax.nn.gelu(hidden, approximate=False))
    branch = low_back(product(active, w_reduce))
    return layer_norm(entries_given + branch, standardizer_factor)

def reference(starting_learned_vectors, frozen_picture_vectors, texts_per_picture, early_triple_matrix, early_mixing_exit_matrix, picture_asker_matrix, picture_pair_matrix, picture_exit_matrix, early_widen_matrix, early_narrow_matrix, later_triple_matrix, later_mixing_exit_matrix, later_widen_matrix, later_narrow_matrix, standardizer_factors, picture_divisors, closing_cotangent):
    count_ends = jnp.cumsum(texts_per_picture, axis=1).astype(jnp.int32)
    positions = jnp.arange(ITEM_DEV, dtype=jnp.int32)
    local_image = lax.optimization_barrier(jnp.sum((count_ends[:, None, :] <= positions[None, :, None]).astype(jnp.int32), axis=2))
    image_of = (local_image + (jnp.arange(N_DP, dtype=jnp.int32) * IMG_DEV)[:, None]).astype(jnp.int32)
    features = frozen_picture_vectors.astype(jnp.float32)

    def evaluate_model(hidden_vectors, early_triple, early_mixing_exit, picture_asker, picture_pair, picture_exit, early_widen, early_narrow, later_triple, later_mixing_exit, later_widen, later_narrow, scale_factors, exponent_divisor):
        paired_matrix = low_back(low(jnp.einsum('npf,fc->npc', features, picture_pair, precision=HIGHEST_PRECISION)))

        def group(pair):
            block_states, selected_entry = pair
            rows_in = block_states.reshape(ITEM_DEV * Q, D)
            hidden_between = self_block(rows_in, early_triple, early_mixing_exit, scale_factors[0])
            hidden_between = picture_mixing_step(hidden_between, jnp.take(paired_matrix, selected_entry, axis=0), picture_asker, picture_exit, scale_factors[1], exponent_divisor)
            hidden_between = hidden_block(hidden_between, early_widen, early_narrow, scale_factors[2])
            hidden_between = self_block(hidden_between, later_triple, later_mixing_exit, scale_factors[3])
            hidden_between = hidden_block(hidden_between, later_widen, later_narrow, scale_factors[4])
            return hidden_between.reshape(ITEM_DEV, Q, D)
        outputs = lax.map(jax.checkpoint(group), (hidden_vectors.reshape(N_DP, ITEM_DEV, Q, D), image_of))
        return outputs.reshape(ITEMS, Q, D)
    parameter_bundle = [early_triple_matrix, early_mixing_exit_matrix, picture_asker_matrix, picture_pair_matrix, picture_exit_matrix, early_widen_matrix, early_narrow_matrix, later_triple_matrix, later_mixing_exit_matrix, later_widen_matrix, later_narrow_matrix]
    evaluation_inputs = [starting_learned_vectors.astype(jnp.float32)] + [lone_matrix.astype(jnp.float32) for lone_matrix in parameter_bundle] + [standardizer_factors.astype(jnp.float32), picture_divisors.astype(jnp.float32)]
    final_states, pullback = jax.vjp(evaluate_model, *evaluation_inputs)
    grads = pullback(closing_cotangent.astype(jnp.float32))
    return (final_states, grads[0], grads[1], grads[2], grads[3], grads[4], grads[5], grads[6], grads[7], grads[8], grads[9], grads[10], grads[11], grads[12], grads[13])
```

```python
import math

import jax
import jax.numpy as jnp
from jax import lax
from jax.sharding import PartitionSpec as P

EPSILON = 1e-06
BF = jnp.bfloat16
F32 = jnp.float32


def mm(left, right):
    return jnp.dot(left, right, preferred_element_type=F32)


def mm_tn(left, right):
    return lax.dot_general(left, right, (((0,), (0,)), ((), ())), preferred_element_type=F32)


def mm_nt(left, right):
    return lax.dot_general(left, right, (((1,), (1,)), ((), ())), preferred_element_type=F32)


def layer_norm(z, gain):
    centred = z - jnp.mean(z, axis=-1, keepdims=True)
    inverse = lax.rsqrt(jnp.mean(centred * centred, axis=-1, keepdims=True) + EPSILON)
    normed = centred * inverse
    return normed * gain, normed, inverse


def norm_back(dout, gain, normed, inverse):
    dn = dout * gain
    dgain = jnp.sum(dout * normed, axis=0)
    dz = inverse * (
        dn
        - jnp.mean(dn, axis=-1, keepdims=True)
        - normed * jnp.mean(dn * normed, axis=-1, keepdims=True)
    )
    return dz, dgain


def gelu(u):
    return u * (1.0 + lax.erf(u * (0.5**0.5))) * 0.5


def gelu_slope(u):
    return 0.5 * (1.0 + lax.erf(u * (0.5**0.5))) + u * jnp.exp(-0.5 * u * u) * (
        1.0 / math.sqrt(2.0 * math.pi)
    )


def swap(value, axis, bit):
    size = lax.axis_size(axis)
    return lax.ppermute(value, axis, [(i, i ^ bit) for i in range(size)])


def pick(value, index, axis):
    return lax.dynamic_index_in_dim(value, index, axis, keepdims=False)


def add_low(left, right):
    return (left.astype(F32) + right.astype(F32)).astype(BF)


def section_blocks(value):
    rows, width = value.shape
    parts = lax.axis_size("section")
    return value.reshape(rows, parts, width // parts).transpose(1, 0, 2)


def exchange(blocks):
    me = lax.axis_index("section")
    parts = lax.axis_size("section")
    out = blocks
    for bit in range(1, parts):
        got = swap(pick(blocks, me ^ bit, 0), "section", bit)
        out = lax.dynamic_update_index_in_dim(out, got, me ^ bit, 0)
    return out


def cols_to_section(value):
    return exchange(section_blocks(value))


def rows_from_section(blocks):
    got = exchange(blocks)
    parts, rows, width = got.shape
    return got.transpose(1, 0, 2).reshape(rows, parts * width)


def line_sum(blocks):
    n = blocks.shape[0]
    p = lax.axis_index("dp") // 2
    size = lax.axis_size("dp")
    kept = blocks
    for k in range(n - 1):
        up_at = jnp.clip(n - 1 - k + p, 0, n - 1)
        down_at = jnp.clip(p - (n - 1 - k), 0, n - 1)
        up_pairs = [(2 * q + c, 2 * q + 2 + c) for q in range(min(k, n - 2) + 1) for c in (0, 1)]
        down_pairs = [
            (2 * q + c, 2 * q - 2 + c) for q in range(max(n - 1 - k, 1), n) for c in (0, 1)
        ]
        up = lax.ppermute(pick(kept, up_at, 0), "dp", up_pairs)
        down = lax.ppermute(pick(kept, down_at, 0), "dp", down_pairs)
        up_to = jnp.clip(n - 2 - k + p, 0, n - 1)
        down_to = jnp.clip(p + 1 - (n - 1 - k), 0, n - 1)
        kept = lax.dynamic_update_index_in_dim(kept, add_low(pick(kept, up_to, 0), up), up_to, 0)
        kept = lax.dynamic_update_index_in_dim(
            kept, add_low(pick(kept, down_to, 0), down), down_to, 0
        )
    del size
    return pick(kept, p, 0)


def core_sum(unit):
    parts, dp, r, w = unit.shape
    c = lax.axis_index("dp") % 2
    pairs = unit.reshape(parts, dp // 2, 2, r, w)
    return add_low(pick(pairs, c, 2), swap(pick(pairs, 1 - c, 2), "dp", 1))


def plane_sum(unit):
    parts, n, r, w = unit.shape
    me = lax.axis_index("section")
    low, high = me % 2, me // 2
    square = unit.reshape(2, 2, n, r, w)
    a, b = square[:, :, :, : r // 2], square[:, :, :, r // 2 :]
    a = add_low(pick(a, low, 1), swap(pick(a, 1 - low, 1), "section", 1))
    b = add_low(pick(b, high, 0), swap(pick(b, 1 - high, 0), "section", 2))
    a = add_low(pick(a, high, 0), swap(pick(a, 1 - high, 0), "section", 2))
    b = add_low(pick(b, low, 0), swap(pick(b, 1 - low, 0), "section", 1))
    return jnp.concatenate([a, b], axis=1)


def home(unit):
    return line_sum(plane_sum(core_sum(unit)))


def unit_of(grad, dp, sections):
    rows, cols = grad.shape
    return (
        grad.astype(BF)
        .reshape(dp, rows // dp, sections, cols // sections)
        .transpose(2, 0, 1, 3)
    )


def all_sum(value):
    for axis in ("dp", "section"):
        bit = 1
        while bit < lax.axis_size(axis):
            value = value + swap(value, axis, bit)
            bit *= 2
    return value


def self_parts(joined, items, query_count, heads):
    rows = joined.shape[0]
    width = joined.shape[1] // 3
    parts = joined.reshape(items, query_count, 3, heads, width // heads)
    return parts[:, :, 0], parts[:, :, 1], parts[:, :, 2]


def self_forward(x, w_project, w_exit, gain, query_count, heads):
    rows, width = x.shape
    items = rows // query_count
    low = x.astype(BF)
    joined = mm(low, w_project).astype(BF)
    q, k, v = self_parts(joined, items, query_count, heads)
    scale = 1.0 / math.sqrt(width // heads)
    t = jnp.einsum("iqhd,ikhd->ihqk", q, k, preferred_element_type=F32)
    p = jax.nn.softmax(t * scale, axis=-1)
    mixed = (
        jnp.einsum("ihqk,ikhd->iqhd", p.astype(BF), v, preferred_element_type=F32)
        .astype(BF)
        .reshape(rows, width)
    )
    out, normed, inverse = layer_norm(x + mm(mixed, w_exit), gain)
    return out, (low, joined, p, mixed, normed, inverse)


def self_backward(dout, w_project, w_exit, gain, saved, query_count, heads):
    low, joined, p, mixed, normed, inverse = saved
    rows, width = mixed.shape
    items = rows // query_count
    q, k, v = self_parts(joined, items, query_count, heads)
    scale = 1.0 / math.sqrt(width // heads)
    dz, dgain = norm_back(dout, gain, normed, inverse)
    da = dz.astype(BF)
    d_exit = mm_tn(mixed, da)
    do = mm_nt(da, w_exit).astype(BF).reshape(items, query_count, heads, width // heads)
    dp = jnp.einsum("iqhd,ikhd->ihqk", do, v, preferred_element_type=F32)
    dv = jnp.einsum("ihqk,iqhd->ikhd", p.astype(BF), do, preferred_element_type=F32)
    ds = p * (dp - jnp.sum(p * dp, axis=-1, keepdims=True))
    dt = (ds * scale).astype(BF)
    dq = jnp.einsum("ihqk,ikhd->iqhd", dt, k, preferred_element_type=F32)
    dk = jnp.einsum("ihqk,iqhd->ikhd", dt, q, preferred_element_type=F32)
    djoined = jnp.stack([dq, dk, dv], axis=2).astype(BF).reshape(rows, 3 * width)
    d_project = mm_tn(low, djoined)
    return dz + mm_nt(djoined, w_project), dgain, d_project, d_exit


def hidden_forward(x, w_expand, w_reduce, gain):
    low = x.astype(BF)
    u = mm(low, w_expand).astype(BF)
    m = gelu(u.astype(F32)).astype(BF)
    out, normed, inverse = layer_norm(x + mm(m, w_reduce), gain)
    return out, (low, u, m, normed, inverse)


def hidden_backward(dout, w_expand, w_reduce, gain, saved):
    low, u, m, normed, inverse = saved
    dz, dgain = norm_back(dout, gain, normed, inverse)
    da = dz.astype(BF)
    d_reduce = mm_tn(m, da)
    du = (mm_nt(da, w_reduce) * gelu_slope(u.astype(F32))).astype(BF)
    d_expand = mm_tn(low, du)
    return dz + mm_nt(du, w_expand), dgain, d_expand, d_reduce


def body(
    starting_learned_vectors,
    frozen_picture_vectors,
    texts_per_picture,
    early_triple_matrix,
    early_mixing_exit_matrix,
    picture_asker_matrix,
    picture_pair_matrix,
    picture_exit_matrix,
    early_widen_matrix,
    early_narrow_matrix,
    later_triple_matrix,
    later_mixing_exit_matrix,
    later_widen_matrix,
    later_narrow_matrix,
    standardizer_factors,
    picture_divisors,
    closing_cotangent,
):
    sections = lax.axis_size("section")
    dp = lax.axis_size("dp")
    me = lax.axis_index("section")
    item_count, query_count, width = starting_learned_vectors.shape
    heads = picture_divisors.shape[0]
    images, patches, feat = frozen_picture_vectors.shape
    own_items = item_count // sections
    rows = own_items * query_count
    own_heads = heads // sections
    head_size = width // heads
    own_width = width // sections
    gains = standardizer_factors

    ends = jnp.cumsum(texts_per_picture[0])
    positions = jnp.arange(item_count, dtype=jnp.int32)
    image_of = jnp.sum((ends[None, :] <= positions[:, None]).astype(jnp.int32), axis=1)
    onehot = (image_of[:, None] == jnp.arange(images)[None, :]).astype(F32)

    def own_rows(value):
        part = lax.dynamic_slice_in_dim(value, me * own_items, own_items, 0)
        return part.reshape(rows, width).astype(F32)

    w_pair = jnp.concatenate(
        [
            lax.dynamic_slice_in_dim(picture_pair_matrix, me * own_width, own_width, 1),
            lax.dynamic_slice_in_dim(picture_pair_matrix, width + me * own_width, own_width, 1),
        ],
        axis=1,
    )
    keyval = jnp.einsum(
        "npf,fc->npc", frozen_picture_vectors, w_pair, preferred_element_type=F32
    ).astype(BF)

    x0 = own_rows(starting_learned_vectors)
    h1, saved_self1 = self_forward(
        x0, early_triple_matrix, early_mixing_exit_matrix, gains[0], query_count, heads
    )
    low1 = h1.astype(BF)
    q_cols = cols_to_section(mm(low1, picture_asker_matrix).astype(BF))
    q = q_cols.reshape(item_count, query_count, own_heads, head_size)
    chosen = jnp.take(keyval, image_of, axis=0).reshape(
        item_count, patches, 2, own_heads, head_size
    )
    k, v = chosen[:, :, 0], chosen[:, :, 1]
    clamped = jnp.clip(picture_divisors, 0.5, 2.0)
    scale_all = 1.0 / math.sqrt(head_size) / clamped
    scale = lax.dynamic_slice_in_dim(scale_all, me * own_heads, own_heads, 0)
    t = jnp.einsum("iqhd,iphd->ihqp", q, k, preferred_element_type=F32)
    p = jax.nn.softmax(t * scale[None, :, None, None], axis=-1)
    p_low = p.astype(BF)
    o = jnp.einsum("ihqp,iphd->iqhd", p_low, v, preferred_element_type=F32).astype(BF)
    mixed = rows_from_section(o.reshape(sections, rows, own_width))
    h2, normed2, inverse2 = layer_norm(h1 + mm(mixed, picture_exit_matrix), gains[1])

    h3, saved_ff1 = hidden_forward(h2, early_widen_matrix, early_narrow_matrix, gains[2])
    h4, saved_self2 = self_forward(
        h3, later_triple_matrix, later_mixing_exit_matrix, gains[3], query_count, heads
    )
    h5, saved_ff2 = hidden_forward(h4, later_widen_matrix, later_narrow_matrix, gains[4])
    final_part = cols_to_section(h5.astype(BF)).astype(F32)
    final_part = final_part.reshape(item_count, query_count, own_width)

    def unit(grad):
        return unit_of(grad, dp, sections)

    def fold(blocks):
        parts, n, r, w = blocks.shape
        return blocks.reshape(parts, n, 4, r // 4, w).transpose(0, 1, 3, 2, 4).reshape(
            parts, n, r // 4, 4 * w
        )

    def unfold(block):
        r, w = block.shape
        return block.reshape(r, 4, w // 4).transpose(1, 0, 2).reshape(4 * r, w // 4)

    dout = own_rows(closing_cotangent)
    d5, dg4, d_expand2, d_reduce2 = hidden_backward(
        dout, later_widen_matrix, later_narrow_matrix, gains[4], saved_ff2
    )
    expand2 = home(unit(d_expand2))
    reduce2 = unfold(home(fold(unit(d_reduce2))))
    d4, dg3, d_project2, d_out2 = self_backward(
        d5, later_triple_matrix, later_mixing_exit_matrix, gains[3], saved_self2, query_count, heads
    )
    self2 = home(jnp.concatenate([unit(d_project2), unit(d_out2)], axis=3))
    d3, dg2, d_expand1, d_reduce1 = hidden_backward(
        d4, early_widen_matrix, early_narrow_matrix, gains[2], saved_ff1
    )
    expand1 = home(unit(d_expand1))
    reduce1 = unfold(home(fold(unit(d_reduce1))))

    dz2, dg1 = norm_back(d3, gains[1], normed2, inverse2)
    da2 = dz2.astype(BF)
    d_exit = mm_tn(mixed, da2)
    do = cols_to_section(mm_nt(da2, picture_exit_matrix).astype(BF))
    do = do.reshape(item_count, query_count, own_heads, head_size)
    dpr = jnp.einsum("iqhd,iphd->ihqp", do, v, preferred_element_type=F32)
    dv = jnp.einsum("ihqp,iqhd->iphd", p_low, do, preferred_element_type=F32)
    ds = p * (dpr - jnp.sum(p * dpr, axis=-1, keepdims=True))
    d_temper = jnp.sum(ds * t, axis=(0, 2, 3))
    dt = (ds * scale[None, :, None, None]).astype(BF)
    dq = jnp.einsum("ihqp,iphd->iqhd", dt, k, preferred_element_type=F32).astype(BF)
    dk = jnp.einsum("ihqp,iqhd->iphd", dt, q, preferred_element_type=F32)
    dkv = jnp.stack([dk, dv], axis=2).reshape(item_count, patches, 2 * own_width)
    dkv = jnp.einsum("bj,bpc->jpc", onehot, dkv, precision=lax.Precision.HIGHEST).astype(BF)
    d_pair = jnp.einsum("npf,npc->fc", frozen_picture_vectors, dkv, preferred_element_type=F32)
    pair_block = line_sum(
        core_sum(d_pair.astype(BF).reshape(1, dp, feat // dp, 2 * own_width))[0]
    )
    dq_rows = rows_from_section(dq.reshape(sections, rows, own_width))
    d_asker = mm_tn(low1, dq_rows)
    d2 = dz2 + mm_nt(dq_rows, picture_asker_matrix)
    image_units = home(jnp.concatenate([unit(d_asker), unit(d_exit)], axis=3))

    d1, dg0, d_project1, d_out1 = self_backward(
        d2, early_triple_matrix, early_mixing_exit_matrix, gains[0], saved_self1, query_count, heads
    )
    self1 = home(jnp.concatenate([unit(d_project1), unit(d_out1)], axis=3))
    grad_part = cols_to_section(d1.astype(BF)).astype(F32)
    grad_part = grad_part.reshape(item_count, query_count, own_width)

    pair_rows = pair_block.shape[0]
    half = sections // 2
    pair_halves = pair_block.reshape(pair_rows, 2, own_width).transpose(1, 0, 2)
    key_home, val_home = me // 2, half + me // 2
    sent = jnp.zeros((sections, pair_rows, own_width), BF)
    sent = lax.dynamic_update_index_in_dim(sent, pair_halves[0], key_home, 0)
    sent = lax.dynamic_update_index_in_dim(sent, pair_halves[1], val_home, 0)
    got = exchange(sent)
    first = (me % half) * 2
    pair_part = lax.dynamic_slice_in_dim(got, first, 2, 0)
    pair_part = pair_part.transpose(1, 0, 2).reshape(pair_rows, 2 * own_width).astype(F32)

    interior = ((picture_divisors > 0.5) & (picture_divisors < 2.0)).astype(F32)
    spread = jnp.zeros((heads,), F32)
    spread = lax.dynamic_update_slice_in_dim(spread, d_temper, me * own_heads, 0)
    spread = spread * (-scale_all / clamped) * interior
    small = jnp.concatenate([jnp.stack([dg0, dg1, dg2, dg3, dg4]).reshape(-1), spread])
    small = all_sum(small)
    gains_grad = small[: 5 * width].reshape(5, width)
    temper_grad = small[5 * width :]

    def f(block):
        return block.astype(F32)

    third = 3 * own_width
    return (
        final_part,
        grad_part,
        f(self1[:, :third]),
        f(self1[:, third:]),
        f(image_units[:, :own_width]),
        pair_part,
        f(image_units[:, own_width:]),
        f(expand1),
        f(reduce1),
        f(self2[:, :third]),
        f(self2[:, third:]),
        f(expand2),
        f(reduce2),
        gains_grad,
        temper_grad,
    )


def solution(mesh):
    return jax.shard_map(
        body,
        mesh=mesh,
        in_specs=(P("dp", None, None), P("dp", None, None), P("dp", None))
        + (P(),) * 13
        + (P("dp", None, None),),
        out_specs=(P("dp", None, "section"),) * 2 + (P("dp", "section"),) * 11 + (P(), P()),
        check_vma=False,
    )
```

```python
import functools
import math

import jax
import jax.numpy as jnp
from jax import lax
from jax.experimental import pallas as pl
from jax.experimental.pallas import tpu as pltpu
from jax.sharding import PartitionSpec as P

EPSILON = 1e-06
BF = jnp.bfloat16
F32 = jnp.float32


def mm(left, right):
    return jnp.dot(left, right, preferred_element_type=F32)


def mm_tn(left, right):
    return lax.dot_general(left, right, (((0,), (0,)), ((), ())), preferred_element_type=F32)


def mm_nt(left, right):
    return lax.dot_general(left, right, (((1,), (1,)), ((), ())), preferred_element_type=F32)


def layer_norm(z, gain):
    centred = z - jnp.mean(z, axis=-1, keepdims=True)
    inverse = lax.rsqrt(jnp.mean(centred * centred, axis=-1, keepdims=True) + EPSILON)
    normed = centred * inverse
    return normed * gain, normed, inverse


def norm_back(dout, gain, normed, inverse):
    dn = dout * gain
    dgain = jnp.sum(dout * normed, axis=0)
    dz = inverse * (
        dn
        - jnp.mean(dn, axis=-1, keepdims=True)
        - normed * jnp.mean(dn * normed, axis=-1, keepdims=True)
    )
    return dz, dgain


def gelu_both(u):
    x = jnp.abs(u) * (0.5**0.5)
    e = jnp.exp(-0.5 * u * u)
    s = 1.0 / (1.0 + 0.3275911 * x)
    poly = s * (
        0.254829592
        + s * (-0.284496736 + s * (1.421413741 + s * (-1.453152027 + s * 1.061405429)))
    )
    tail = 0.5 * poly * e
    cdf = jnp.where(u < 0.0, tail, 1.0 - tail)
    return u * cdf, cdf + u * e * (1.0 / math.sqrt(2.0 * math.pi))


def swap(value, axis, bit):
    size = lax.axis_size(axis)
    return lax.ppermute(value, axis, [(i, i ^ bit) for i in range(size)])


def pick(value, index, axis):
    return lax.dynamic_index_in_dim(value, index, axis, keepdims=False)


def add_low(left, right):
    return (left.astype(F32) + right.astype(F32)).astype(BF)


def section_blocks(value):
    rows, width = value.shape
    parts = lax.axis_size("section")
    return value.reshape(rows, parts, width // parts).transpose(1, 0, 2)


def exchange(blocks):
    me = lax.axis_index("section")
    parts = lax.axis_size("section")
    out = blocks
    for bit in range(1, parts):
        got = swap(pick(blocks, me ^ bit, 0), "section", bit)
        out = lax.dynamic_update_index_in_dim(out, got, me ^ bit, 0)
    return out


def cols_to_section(value):
    return exchange(section_blocks(value))


def rows_from_section(blocks):
    got = exchange(blocks)
    parts, rows, width = got.shape
    return got.transpose(1, 0, 2).reshape(rows, parts * width)


def line_sum(blocks):
    n = blocks.shape[0]
    p = lax.axis_index("dp") // 2
    size = lax.axis_size("dp")
    kept = blocks
    for k in range(n - 1):
        up_at = jnp.clip(n - 1 - k + p, 0, n - 1)
        down_at = jnp.clip(p - (n - 1 - k), 0, n - 1)
        up_pairs = [(2 * q + c, 2 * q + 2 + c) for q in range(min(k, n - 2) + 1) for c in (0, 1)]
        down_pairs = [
            (2 * q + c, 2 * q - 2 + c) for q in range(max(n - 1 - k, 1), n) for c in (0, 1)
        ]
        up = lax.ppermute(pick(kept, up_at, 0), "dp", up_pairs)
        down = lax.ppermute(pick(kept, down_at, 0), "dp", down_pairs)
        up_to = jnp.clip(n - 2 - k + p, 0, n - 1)
        down_to = jnp.clip(p + 1 - (n - 1 - k), 0, n - 1)
        kept = lax.dynamic_update_index_in_dim(kept, add_low(pick(kept, up_to, 0), up), up_to, 0)
        kept = lax.dynamic_update_index_in_dim(
            kept, add_low(pick(kept, down_to, 0), down), down_to, 0
        )
    del size
    return pick(kept, p, 0)


def core_sum(unit):
    parts, dp, r, w = unit.shape
    c = lax.axis_index("dp") % 2
    pairs = unit.reshape(parts, dp // 2, 2, r, w)
    return add_low(pick(pairs, c, 2), swap(pick(pairs, 1 - c, 2), "dp", 1))


def plane_sum(unit):
    parts, n, r, w = unit.shape
    me = lax.axis_index("section")
    low, high = me % 2, me // 2
    square = unit.reshape(2, 2, n, r, w)
    a, b = square[:, :, :, : r // 2], square[:, :, :, r // 2 :]
    a = add_low(pick(a, low, 1), swap(pick(a, 1 - low, 1), "section", 1))
    b = add_low(pick(b, high, 0), swap(pick(b, 1 - high, 0), "section", 2))
    a = add_low(pick(a, high, 0), swap(pick(a, 1 - high, 0), "section", 2))
    b = add_low(pick(b, low, 0), swap(pick(b, 1 - low, 0), "section", 1))
    return jnp.concatenate([a, b], axis=1)


def home(unit):
    return line_sum(plane_sum(core_sum(unit)))


def unit_of(grad, dp, sections):
    rows, cols = grad.shape
    return (
        grad.astype(BF)
        .reshape(dp, rows // dp, sections, cols // sections)
        .transpose(2, 0, 1, 3)
    )


def all_sum(value):
    for axis in ("dp", "section"):
        bit = 1
        while bit < lax.axis_size(axis):
            value = value + swap(value, axis, bit)
            bit *= 2
    return value


VMEM = pltpu.MemorySpace.VMEM
SMEM = pltpu.MemorySpace.SMEM
LIMIT = 60 * 1024 * 1024
GROUP = 128


def whole(space=VMEM):
    return pl.BlockSpec(memory_space=space)


def head_lanes(shape, head, head_size):
    return lax.broadcasted_iota(jnp.int32, shape, len(shape) - 1) // head_size == head


def same_item(query_count):
    shape = (GROUP, GROUP)
    left = lax.broadcasted_iota(jnp.int32, shape, 0) // query_count
    right = lax.broadcasted_iota(jnp.int32, shape, 1) // query_count
    return left == right


def soft(t, mask, scale):
    t = jnp.where(mask, t * scale, -1e30)
    e = jnp.exp(t - jnp.max(t, axis=-1, keepdims=True))
    return e / jnp.sum(e, axis=-1, keepdims=True)


def masked(value, head, head_size):
    return jnp.where(head_lanes(value.shape, head, head_size), value, jnp.zeros_like(value))


def attend_self(joined_ref, mixed_ref, query_count, head_size):
    rows, width = mixed_ref.shape
    pair = 2 * head_size
    scale = 1.0 / math.sqrt(head_size)
    mask = same_item(query_count)

    def step(i, _):
        col = pl.multiple_of(i * pair, pair)
        for g in range(rows // GROUP):
            at = pl.ds(g * GROUP, GROUP)
            q = joined_ref[at, pl.ds(col, pair)]
            k = joined_ref[at, pl.ds(width + col, pair)]
            v = joined_ref[at, pl.ds(2 * width + col, pair)]
            o = jnp.zeros((GROUP, pair), F32)
            for h in range(2):
                p = soft(mm_nt(masked(q, h, head_size), k), mask, scale).astype(BF)
                o = o + mm(p, masked(v, h, head_size))
            mixed_ref[at, pl.ds(col, pair)] = o.astype(BF)
        return 0

    lax.fori_loop(0, width // pair, step, 0)


def attend_self_back(joined_ref, do_ref, djoined_ref, query_count, head_size):
    rows, width = do_ref.shape
    pair = 2 * head_size
    scale = 1.0 / math.sqrt(head_size)
    mask = same_item(query_count)

    def step(i, _):
        col = pl.multiple_of(i * pair, pair)
        for g in range(rows // GROUP):
            at = pl.ds(g * GROUP, GROUP)
            q = joined_ref[at, pl.ds(col, pair)]
            k = joined_ref[at, pl.ds(width + col, pair)]
            v = joined_ref[at, pl.ds(2 * width + col, pair)]
            do = do_ref[at, pl.ds(col, pair)]
            dq = jnp.zeros((GROUP, pair), F32)
            dk = jnp.zeros((GROUP, pair), F32)
            dv = jnp.zeros((GROUP, pair), F32)
            for h in range(2):
                qh, kh = masked(q, h, head_size), masked(k, h, head_size)
                doh = masked(do, h, head_size)
                p = soft(mm_nt(qh, k), mask, scale)
                dp = mm_nt(doh, v)
                ds = p * (dp - jnp.sum(p * dp, axis=-1, keepdims=True))
                dt = (ds * scale).astype(BF)
                dv = dv + mm_tn(p.astype(BF), doh)
                dq = dq + mm(dt, kh)
                dk = dk + mm_tn(dt, qh)
            djoined_ref[at, pl.ds(col, pair)] = dq.astype(BF)
            djoined_ref[at, pl.ds(width + col, pair)] = dk.astype(BF)
            djoined_ref[at, pl.ds(2 * width + col, pair)] = dv.astype(BF)
        return 0

    lax.fori_loop(0, width // pair, step, 0)


def project_into(out_ref, low, w_ref, block=768):
    for at in range(0, w_ref.shape[1], block):
        out_ref[:, at : at + block] = mm(low, w_ref[:, at : at + block]).astype(BF)


def back_through(dy_ref, w_ref, block=768):
    total = None
    for at in range(0, w_ref.shape[1], block):
        term = mm_nt(dy_ref[:, at : at + block], w_ref[:, at : at + block])
        total = term if total is None else total + term
    return total


def hidden_forward(low, w_expand_ref, w_reduce_ref, m_ref, slope_ref, block=512):
    total = None
    for at in range(0, w_expand_ref.shape[1], block):
        u = mm(low, w_expand_ref[:, at : at + block]).astype(BF).astype(F32)
        m, slope = gelu_both(u)
        m = m.astype(BF)
        m_ref[:, at : at + block] = m
        slope_ref[:, at : at + block] = slope
        term = mm(m, w_reduce_ref[at : at + block, :])
        total = term if total is None else total + term
    return total


def hidden_backward(da, w_expand_ref, w_reduce_ref, slope_ref, du_ref, block=512):
    total = None
    for at in range(0, w_expand_ref.shape[1], block):
        dm = mm_nt(da, w_reduce_ref[at : at + block, :])
        du = (dm * slope_ref[:, at : at + block]).astype(BF)
        du_ref[:, at : at + block] = du
        term = mm_nt(du, w_expand_ref[:, at : at + block])
        total = term if total is None else total + term
    return total


def norm_into(z, gain, n_ref, r_ref):
    out, n, r = layer_norm(z, gain)
    n_ref[...] = n
    r_ref[...] = r
    return out


def put_blocks(out_ref, value):
    parts, _, wide = out_ref.shape
    own = value.shape[1] // parts
    for t in range(parts):
        out_ref[t, :, :own] = value[:, t * own : (t + 1) * own]
        if wide > own:
            out_ref[t, :, own:] = jnp.zeros((value.shape[0], wide - own), out_ref.dtype)


def take_blocks(in_ref, own):
    return jnp.concatenate([in_ref[t, :, :own] for t in range(in_ref.shape[0])], axis=1)


def front_kernel(
    query_count, head_size, x_ref, wp_ref, wo_ref, wq_ref, g_ref,
    h_ref, n_ref, r_ref, joined_ref, mixed_ref, q_ref,
):
    low = x_ref[...]
    project_into(joined_ref, low, wp_ref)
    attend_self(joined_ref, mixed_ref, query_count, head_size)
    z = low.astype(F32) + mm(mixed_ref[...], wo_ref[...])
    h = norm_into(z, g_ref[0:1, :], n_ref, r_ref)
    h_ref[...] = h
    put_blocks(q_ref, mm(h.astype(BF), wq_ref[...]).astype(BF))


def keyval_kernel(x_ref, w_ref, out_ref):
    patches = x_ref.shape[1]
    padded = out_ref.shape[1]
    full = patches // 16 * 16
    out_ref[0, full:, :] = jnp.zeros((padded - full, out_ref.shape[2]), BF)
    out_ref[0, :patches, :] = mm(x_ref[0], w_ref[...]).astype(BF)


def stacked(value, own_heads, head_size):
    return jnp.concatenate([masked(value, h, head_size) for h in range(own_heads)], axis=0)


def unstacked(value, own_heads, head_size):
    rows = value.shape[0] // own_heads
    total = None
    for h in range(own_heads):
        part = masked(value[h * rows : (h + 1) * rows], h, head_size)
        total = part if total is None else total + part
    return total


def row_scales(scale_ref, own_heads, query_count):
    return jnp.concatenate(
        [jnp.full((query_count, 1), scale_ref[0, h], F32) for h in range(own_heads)], axis=0
    )


def attend_image_kernel(
    patches, own_heads, head_size, query_count, together,
    image_ref, scale_ref, q_ref, kv_ref, o_ref,
):
    wide = q_ref.shape[1]
    items = q_ref.shape[0] // query_count
    padded = kv_ref.shape[1]
    scales = row_scales(scale_ref, own_heads, query_count)
    mask = lax.broadcasted_iota(jnp.int32, (1, padded), 1) < patches

    def step(i, _):
        for b in range(together):
            item = i * together + b
            at = pl.ds(pl.multiple_of(item * query_count, query_count), query_count)
            j = image_ref[0, item]
            q = stacked(q_ref[at, :], own_heads, head_size)
            p = soft(mm_nt(q, kv_ref[j, :, :wide]), mask, scales)
            o = mm(p.astype(BF), kv_ref[j, :, wide:])
            o_ref[at, :] = unstacked(o, own_heads, head_size).astype(BF)
        return 0

    lax.fori_loop(0, items // together, step, 0)


def attend_image_back_kernel(
    patches, own_heads, head_size, query_count, together,
    image_ref, scale_ref, q_ref, do_ref, kv_ref, dq_ref, dkv_ref, temper_ref, total_ref,
):
    wide = q_ref.shape[1]
    items = q_ref.shape[0] // query_count
    padded = kv_ref.shape[1]
    scales = row_scales(scale_ref, own_heads, query_count)
    mask = lax.broadcasted_iota(jnp.int32, (1, padded), 1) < patches
    total_ref[...] = jnp.zeros_like(total_ref)
    temper_ref[...] = jnp.zeros_like(temper_ref)

    def step(i, _):
        temper = None
        for b in range(together):
            item = i * together + b
            at = pl.ds(pl.multiple_of(item * query_count, query_count), query_count)
            j = image_ref[0, item]
            q = stacked(q_ref[at, :], own_heads, head_size)
            do = stacked(do_ref[at, :], own_heads, head_size)
            k, v = kv_ref[j, :, :wide], kv_ref[j, :, wide:]
            t = mm_nt(q, k)
            p = soft(t, mask, scales)
            dp = mm_nt(do, v)
            ds = p * (dp - jnp.sum(p * dp, axis=-1, keepdims=True))
            term = jnp.sum(ds * t, axis=-1, keepdims=True)
            temper = term if temper is None else temper + term
            dt = (ds * scales).astype(BF)
            dq_ref[at, :] = unstacked(mm(dt, k), own_heads, head_size).astype(BF)
            total_ref[j, :, :wide] += mm_tn(dt, q)
            total_ref[j, :, wide:] += mm_tn(p.astype(BF), do)
        temper_ref[...] += temper
        return 0

    lax.fori_loop(0, items // together, step, 0)
    dkv_ref[...] = total_ref[...].astype(BF)


def keyval_grad_kernel(x_ref, dkv_ref, out_ref, total_ref):
    @pl.when(pl.program_id(0) == 0)
    def _():
        total_ref[...] = jnp.zeros_like(total_ref)

    patches = x_ref.shape[1]
    total_ref[...] += mm_tn(dkv_ref[0, :patches, :], x_ref[0])

    @pl.when(pl.program_id(0) == pl.num_programs(0) - 1)
    def _():
        own = out_ref.shape[1] // 2
        wide = total_ref.shape[0] // 2
        out_ref[...] = jnp.concatenate(
            [total_ref[:own, :].T, total_ref[wide : wide + own, :].T], axis=1
        ).astype(BF)


def middle_kernel(
    query_count, head_size,
    h1_ref, mixed1_ref, dout_ref, g_ref,
    wx_hbm, we1_hbm, wr1_hbm, wp_hbm, wo_hbm, we2_hbm, wr2_hbm,
    final_ref, low2_ref, m1_ref, du1_ref, da3_ref, low3_ref, mixed2_ref, djoined_ref, da4_ref,
    low4_ref, m2_ref, du2_ref, da5_ref, da2_ref, do_ref, dz2_ref, dg_ref,
    wx, we1, wr1, wp, wo, we2, wr2, sems,
    slope1, slope2, joined, do2, n2, r2, n3, r3, n4, r4, n5, r5,
):
    copies = [
        pltpu.make_async_copy(src, dst, sems.at[i])
        for i, (src, dst) in enumerate(
            zip((wx_hbm, we1_hbm, wr1_hbm, wp_hbm, wo_hbm, we2_hbm, wr2_hbm),
                (wx, we1, wr1, wp, wo, we2, wr2))
        )
    ]
    for copy in copies:
        copy.start()
    own = mixed1_ref.shape[2]
    own = wx.shape[0] // mixed1_ref.shape[0]
    mixed1 = take_blocks(mixed1_ref, own)
    copies[0].wait()
    h2 = norm_into(h1_ref[...] + mm(mixed1, wx[...]), g_ref[1:2, :], n2, r2)
    low2_ref[...] = h2.astype(BF)
    copies[1].wait()
    copies[2].wait()
    a = hidden_forward(low2_ref[...], we1, wr1, m1_ref, slope1)
    h3 = norm_into(n2[...] * g_ref[1:2, :] + a, g_ref[2:3, :], n3, r3)
    low3_ref[...] = h3.astype(BF)
    copies[3].wait()
    project_into(joined, low3_ref[...], wp)
    attend_self(joined, mixed2_ref, query_count, head_size)
    copies[4].wait()
    a = mm(mixed2_ref[...], wo[...])
    h4 = norm_into(n3[...] * g_ref[2:3, :] + a, g_ref[3:4, :], n4, r4)
    low4_ref[...] = h4.astype(BF)
    copies[5].wait()
    copies[6].wait()
    a = hidden_forward(low4_ref[...], we2, wr2, m2_ref, slope2)
    h5 = norm_into(n4[...] * g_ref[3:4, :] + a, g_ref[4:5, :], n5, r5)
    put_blocks(final_ref, h5.astype(BF))

    dz, dg4 = norm_back(dout_ref[...].astype(F32), g_ref[4:5, :], n5[...], r5[...])
    da5_ref[...] = dz.astype(BF)
    d4 = dz + hidden_backward(da5_ref[...], we2, wr2, slope2, du2_ref)

    dz, dg3 = norm_back(d4, g_ref[3:4, :], n4[...], r4[...])
    da4_ref[...] = dz.astype(BF)
    do2[...] = mm_nt(da4_ref[...], wo[...]).astype(BF)
    attend_self_back(joined, do2, djoined_ref, query_count, head_size)
    d3 = dz + back_through(djoined_ref, wp)

    dz, dg2 = norm_back(d3, g_ref[2:3, :], n3[...], r3[...])
    da3_ref[...] = dz.astype(BF)
    d2 = dz + hidden_backward(da3_ref[...], we1, wr1, slope1, du1_ref)

    dz, dg1 = norm_back(d2, g_ref[1:2, :], n2[...], r2[...])
    dz2_ref[...] = dz
    da2_ref[...] = dz.astype(BF)
    put_blocks(do_ref, mm_nt(da2_ref[...], wx[...]).astype(BF))
    dg_ref[...] = jnp.concatenate([d[None, :] for d in (dg1, dg2, dg3, dg4)], axis=0)


def last_kernel(
    query_count, head_size, dz2_ref, dq_ref, wq_ref, n_ref, r_ref, g_ref, wo_ref, joined_ref, wp_ref,
    dqr_ref, da_ref, djoined_ref, dx_ref, dg_ref, do,
):
    own = wq_ref.shape[1] // dq_ref.shape[0]
    dqr_ref[...] = take_blocks(dq_ref, own)
    d1 = dz2_ref[...] + mm_nt(dqr_ref[...], wq_ref[...])
    dz, dg = norm_back(d1, g_ref[0:1, :], n_ref[...], r_ref[...])
    dg_ref[...] = dg[None, :]
    da_ref[...] = dz.astype(BF)
    do[...] = mm_nt(da_ref[...], wo_ref[...]).astype(BF)
    attend_self_back(joined_ref, do, djoined_ref, query_count, head_size)
    put_blocks(dx_ref, (dz + back_through(djoined_ref, wp_ref)).astype(BF))


def weight_kernel(x_ref, dy_ref, out_ref):
    out_ref[0] = mm_tn(x_ref[...], dy_ref[...]).astype(BF)


def pair_weight_kernel(x_ref, dy_ref, y_ref, dz_ref, out_ref):
    parts = out_ref.shape[0]
    own_a, own_b = dy_ref.shape[1] // parts, dz_ref.shape[1] // parts
    for t in range(parts):
        a = mm_tn(x_ref[...], dy_ref[:, t * own_a : (t + 1) * own_a]).astype(BF)
        b = mm_tn(y_ref[...], dz_ref[:, t * own_b : (t + 1) * own_b]).astype(BF)
        out_ref[t] = jnp.concatenate([a, b], axis=1)


def turned_weight_kernel(dy_ref, x_ref, out_ref):
    _, dp, own, wide = out_ref.shape
    r = mm_tn(dy_ref[...], x_ref[...]).astype(BF)
    for d in range(dp):
        out_ref[0, d] = r[:, d * wide : (d + 1) * wide]


def shape(dims, dtype):
    return jax.ShapeDtypeStruct(tuple(dims), dtype)


def call(kernel, outs, *args, in_specs=None, scratch=(), flops=0):
    return pl.pallas_call(
        kernel,
        out_shape=outs,
        in_specs=in_specs or [whole()] * len(args),
        out_specs=jax.tree.map(lambda _: whole(), outs),
        scratch_shapes=list(scratch),
        compiler_params=pltpu.CompilerParams(vmem_limit_bytes=LIMIT),
        cost_estimate=pl.CostEstimate(
            flops=flops, bytes_accessed=int(flops) // 400, transcendentals=0
        ),
    )(*args)


def expand_grad(low, du, parts):
    rows, width = low.shape
    own = du.shape[1] // parts
    return pl.pallas_call(
        weight_kernel,
        out_shape=shape((parts, width, own), BF),
        grid=(parts,),
        in_specs=[
            pl.BlockSpec((rows, width), lambda t: (0, 0)),
            pl.BlockSpec((rows, own), lambda t: (0, t)),
        ],
        out_specs=pl.BlockSpec((1, width, own), lambda t: (t, 0, 0)),
        compiler_params=pltpu.CompilerParams(vmem_limit_bytes=LIMIT),
    )(low, du)


def reduce_grad(da, m, parts, dp):
    rows, width = da.shape
    wide = m.shape[1] // dp
    own = width // parts
    per = 4 if dp % 4 == 0 and (dp // 4 * wide) % 128 == 0 else 1
    blocks = dp // per
    return pl.pallas_call(
        functools.partial(turned_weight_all_kernel, parts),
        out_shape=shape((parts, dp, own, wide), BF),
        grid=(per,),
        in_specs=[
            pl.BlockSpec((rows, width), lambda b: (0, 0)),
            pl.BlockSpec((rows, blocks * wide), lambda b: (0, b)),
        ],
        out_specs=pl.BlockSpec((parts, blocks, own, wide), lambda b: (0, b, 0, 0)),
        compiler_params=pltpu.CompilerParams(vmem_limit_bytes=LIMIT),
    )(da, m)


def turned_weight_all_kernel(parts, dy_ref, x_ref, out_ref):
    _, blocks, own, wide = out_ref.shape
    r = mm_tn(dy_ref[...], x_ref[...]).astype(BF)
    for t in range(parts):
        for d in range(blocks):
            out_ref[t, d] = r[t * own : (t + 1) * own, d * wide : (d + 1) * wide]


MESH = pl.DeviceIdType.MESH


def device_of(section, z, core):
    return (section, z * 2 + core)


class Home:
    def __init__(self, unit, kept, from_x, from_y, then_x, then_y, from_z, sends, recvs):
        self.unit, self.kept = unit, kept
        self.from_x, self.from_y = from_x, from_y
        self.then_x, self.then_y = then_x, then_y
        self.from_z = from_z
        self.sends, self.recvs = sends, recvs
        self.s, d = lax.axis_index("section"), lax.axis_index("dp")
        self.sx, self.sy = self.s % 2, self.s // 2
        self.z, self.c = d // 2, d % 2
        self.half = kept.shape[2] // 2

    def copy(self, i, src, dst, device):
        return pltpu.make_async_remote_copy(
            src_ref=src, dst_ref=dst, send_sem=self.sends.at[i], recv_sem=self.recvs.at[i],
            device_id=device, device_id_type=MESH,
        )

    def mine(self):
        return self.s if self.kept.shape[0] > 1 else 0

    def cores(self):
        return [
            self.copy(
                0, self.unit.at[:, :, 1 - self.c], self.kept, device_of(self.s, self.z, 1 - self.c)
            )
        ]

    def first(self):
        s, sx, sy, z, c, half = self.s, self.sx, self.sy, self.z, self.c, self.half
        out = []
        for i in range(2):
            out.append(self.copy(
                1 + i, self.kept.at[2 * i + 1 - sx, :, :half], self.from_x.at[i],
                device_of(s + 1 - 2 * sx, z, c),
            ))
            out.append(self.copy(
                3 + i, self.kept.at[2 * (1 - sy) + i, :, half:], self.from_y.at[i],
                device_of(s + 2 - 4 * sy, z, c),
            ))
        return out

    def second(self):
        s, sx, sy, z, c, half = self.s, self.sx, self.sy, self.z, self.c, self.half
        return [
            self.copy(
                5, self.kept.at[2 * (1 - sy) + sx, :, :half], self.then_y,
                device_of(s + 2 - 4 * sy, z, c),
            ),
            self.copy(
                6, self.kept.at[2 * sy + 1 - sx, :, half:], self.then_x,
                device_of(s + 1 - 2 * sx, z, c),
            ),
        ]

    def along(self):
        n = self.kept.shape[1]
        out = []
        for k in range(1, n):
            to = (self.z + k) % n
            out.append(self.copy(
                6 + k, self.kept.at[self.mine(), to], self.from_z.at[k - 1],
                device_of(self.s, to, self.c),
            ))
        return out

    def add_cores(self):
        n = self.kept.shape[1]

        def step(i, _):
            t, z = i // n, i % n
            self.kept[t, z] = self.kept[t, z] + self.unit[t, z, self.c]
            return 0

        lax.fori_loop(0, self.kept.shape[0] * n, step, 0)

    def add_first(self):
        n, half = self.kept.shape[1], self.half

        def step(i, _):
            t, z = i // n, i % n
            x, y = 2 * t + self.sx, 2 * self.sy + t
            self.kept[x, z, :half] = self.kept[x, z, :half] + self.from_x[t, z]
            self.kept[y, z, half:] = self.kept[y, z, half:] + self.from_y[t, z]
            return 0

        lax.fori_loop(0, 2 * n, step, 0)

    def add_second(self):
        n, half = self.kept.shape[1], self.half

        def step(z, _):
            self.kept[self.s, z, :half] = self.kept[self.s, z, :half] + self.then_y[z]
            self.kept[self.s, z, half:] = self.kept[self.s, z, half:] + self.then_x[z]
            return 0

        lax.fori_loop(0, n, step, 0)

    def total(self):
        total = self.kept[self.mine(), self.z].astype(F32)
        for k in range(self.from_z.shape[0]):
            total = total + self.from_z[k].astype(F32)
        return total


def start(copies):
    for copy in copies:
        copy.start()


def wait(copies):
    for copy in copies:
        copy.wait()


def greet():
    s, d = lax.axis_index("section"), lax.axis_index("dp")
    sections, dp = lax.axis_size("section"), lax.axis_size("dp")
    n = dp // 2
    z, c = d // 2, d % 2
    barrier = pltpu.get_barrier_semaphore()
    near = [device_of(s, z, 1 - c)]
    for bit in range(1, sections):
        near.append(device_of(s ^ bit, z, c))
    for k in range(1, n):
        near.append(device_of(s, (z + k) % n, c))
    for device in near:
        pl.semaphore_signal(barrier, inc=1, device_id=device, device_id_type=MESH)
    pl.semaphore_wait(barrier, len(near))


def fill_expand(unit, low, du):
    parts, n, two, r, w = unit.shape
    for t in range(parts):
        g = mm_tn(low[...], du[:, t * w : (t + 1) * w]).astype(BF)
        for d in range(2 * n):
            unit[t, d // 2, d % 2] = g[d * r : (d + 1) * r]


def fill_reduce(unit, da, m):
    parts, n, two, r, w = unit.shape
    own = w // 2
    for z in range(n):
        g = mm_tn(da[...], m[:, 2 * z * own : 2 * (z + 1) * own]).astype(BF)
        for c in range(2):
            for t in range(parts):
                for i in range(2):
                    at = (2 * t + i) * r
                    unit[t, z, c, :, i * own : (i + 1) * own] = g[
                        at : at + r, c * own : (c + 1) * own
                    ]


def fill_pair(unit, x, dy, y, dz):
    parts, n, two, r, w = unit.shape
    own_a, own_b = dy.shape[1] // parts, dz.shape[1] // parts
    for t in range(parts):
        a = mm_tn(x[...], dy[:, t * own_a : (t + 1) * own_a]).astype(BF)
        b = mm_tn(y[...], dz[:, t * own_b : (t + 1) * own_b]).astype(BF)
        g = jnp.concatenate([a, b], axis=1)
        for d in range(2 * n):
            unit[t, d // 2, d % 2] = g[d * r : (d + 1) * r]


def home_kernel(kinds, *refs):
    refs = list(refs)

    def take(count):
        out = refs[:count]
        del refs[:count]
        return out

    count = len(kinds)
    factors = [take({"expand": 2, "reduce": 2, "pair": 4, "made": 1}[kind]) for kind in kinds]
    results = [take({"expand": 1, "reduce": 1, "pair": 2, "made": 1}[kind]) for kind in kinds]
    buffers = [take(2 if kind == "made" else 6) for kind in kinds]
    wide, narrow, sends, recvs, slots_a, slots_b, slots_c, slots_d, loads = take(9)
    slots = (slots_a, slots_b, slots_c, slots_d)
    homes = []
    turns = 0
    for i, kind in enumerate(kinds):
        if kind == "made":
            kept, from_z = buffers[i]
            homes.append(Home(factors[i][0], kept, None, None, None, None, from_z,
                              sends.at[i], recvs.at[i]))
            continue
        if buffers[i][0].shape[3] == wide.shape[5]:
            unit = wide.at[turns % 2]
            turns += 1
        else:
            unit = narrow
        homes.append(Home(unit, *buffers[i], sends.at[i], recvs.at[i]))
    made = [i for i in range(count) if kinds[i] != "made"]

    def held(i):
        turn = made.index(i) % 2
        return [
            slots[j].at[turn, :, : source.shape[1]] for j, source in enumerate(factors[i])
        ]

    def fetch(i):
        return [
            pltpu.make_async_copy(source, target, loads.at[i, j])
            for j, (source, target) in enumerate(zip(factors[i], held(i)))
        ]

    start(fetch(made[0]))
    greet()

    def make(i):
        kind, unit = kinds[i], homes[i].unit
        if kind != "made":
            wait(fetch(i))
            later = made.index(i) + 1
            if later < len(made):
                start(fetch(made[later]))
        if kind == "expand":
            fill_expand(unit, *held(i))
        elif kind == "reduce":
            fill_reduce(unit, *held(i))
        elif kind == "pair":
            fill_pair(unit, *held(i))
        start(homes[i].cores())

    def finish(i):
        wait(homes[i].along())
        total = homes[i].total()
        out = results[i]
        if kinds[i] == "reduce":
            own = total.shape[1] // 2
            out[0][...] = jnp.concatenate([total[:, :own].T, total[:, own:].T], axis=1)
        elif kinds[i] == "pair":
            own = out[0].shape[1]
            out[0][...] = total[:, :own]
            out[1][...] = total[:, own:]
        else:
            out[0][...] = total

    for turn in range(count + 4):
        i = turn - 1
        if 0 <= i < count:
            wait(homes[i].cores())
            homes[i].add_cores()
            start(homes[i].along() if kinds[i] == "made" else homes[i].first())
        if turn < count:
            make(turn)
        i = turn - 2
        if 0 <= i < count and kinds[i] != "made":
            wait(homes[i].first())
            homes[i].add_first()
            start(homes[i].second())
        i = turn - 3
        if 0 <= i < count and kinds[i] != "made":
            wait(homes[i].second())
            homes[i].add_second()
            start(homes[i].along())
        i = turn - 4
        if 0 <= i < count:
            finish(i)


def bring_home(items, sections, dp, width):
    n = dp // 2
    kinds, factors, results, buffers = [], [], [], []
    widest = 0
    rows = items[0][1][0].shape[0]
    most = max(given[1].shape[1] for kind, given, _ in items if kind != "made")
    for kind, given, columns in items:
        kinds.append(kind)
        if kind == "made":
            r, w = given[0].shape[3:]
            results.append([shape((r, w), F32)])
            buffers.append([pltpu.VMEM((1, n, r, w), BF), pltpu.VMEM((n - 1, r, w), BF)])
            factors.append(list(given))
            continue
        r = width // dp
        if kind == "reduce":
            w = 2 * given[1].shape[1] // dp
            results.append([shape((w // 2, 2 * r), F32)])
        else:
            w = sum(columns)
            results.append([shape((r, one), F32) for one in columns])
        widest = max(widest, w)
        factors.append(list(given))
        buffers.append([
            pltpu.VMEM((sections, n, r, w), BF),
            pltpu.VMEM((2, n, r // 2, w), BF), pltpu.VMEM((2, n, r // 2, w), BF),
            pltpu.VMEM((n, r // 2, w), BF), pltpu.VMEM((n, r // 2, w), BF),
            pltpu.VMEM((n - 1, r, w), BF),
        ])
    r = width // dp
    count = len(items)
    flat = lambda lists: [one for part in lists for one in part]
    outs = pl.pallas_call(
        functools.partial(home_kernel, tuple(kinds)),
        out_shape=flat(results),
        in_specs=[
            whole() if kind == "made" else whole(pl.ANY)
            for kind, given in zip(kinds, factors)
            for _ in given
        ],
        out_specs=[whole()] * len(flat(results)),
        scratch_shapes=flat(buffers)
        + [
            pltpu.VMEM((2, sections, n, 2, r, widest), BF),
            pltpu.VMEM((sections, n, 2, r, widest // 2), BF),
            pltpu.SemaphoreType.DMA((count, 10)),
            pltpu.SemaphoreType.DMA((count, 10)),
            pltpu.VMEM((2, rows, width), BF),
            pltpu.VMEM((2, rows, most), BF),
            pltpu.VMEM((2, rows, width), BF),
            pltpu.VMEM((2, rows, width), BF),
            pltpu.SemaphoreType.DMA((count, 4)),
        ],
        compiler_params=pltpu.CompilerParams(
            vmem_limit_bytes=LIMIT, collective_id=0, has_side_effects=True
        ),
    )(*flat(factors))
    outs = list(outs)
    split = []
    for part in results:
        split.append(outs[: len(part)])
        del outs[: len(part)]
    return split


def body(
    starting_learned_vectors,
    frozen_picture_vectors,
    texts_per_picture,
    early_triple_matrix,
    early_mixing_exit_matrix,
    picture_asker_matrix,
    picture_pair_matrix,
    picture_exit_matrix,
    early_widen_matrix,
    early_narrow_matrix,
    later_triple_matrix,
    later_mixing_exit_matrix,
    later_widen_matrix,
    later_narrow_matrix,
    standardizer_factors,
    picture_divisors,
    closing_cotangent,
):
    sections = lax.axis_size("section")
    dp = lax.axis_size("dp")
    me = lax.axis_index("section")
    item_count, query_count, width = starting_learned_vectors.shape
    heads = picture_divisors.shape[0]
    images, patches, feat = frozen_picture_vectors.shape
    own_items = item_count // sections
    rows = own_items * query_count
    own_heads = heads // sections
    head_size = width // heads
    own_width = width // sections
    wide = -(-own_width // 128) * 128
    padded = -(-patches // 16) * 16
    hidden = early_widen_matrix.shape[1]
    gains = standardizer_factors

    ends = jnp.cumsum(texts_per_picture[0])
    positions = jnp.arange(item_count, dtype=jnp.int32)
    image_of = jnp.sum((ends[None, :] <= positions[:, None]).astype(jnp.int32), axis=1)[None, :]
    clamped = jnp.clip(picture_divisors, 0.5, 2.0)
    scale_all = 1.0 / math.sqrt(head_size) / clamped
    scale = lax.dynamic_slice_in_dim(scale_all, me * own_heads, own_heads, 0)[None, :]

    def own_rows(value):
        part = lax.dynamic_slice_in_dim(value, me * own_items, own_items, 0)
        return part.reshape(rows, width)

    def heads_to_sections(blocks):
        return exchange(blocks)

    x0 = own_rows(starting_learned_vectors)
    h1, n1, r1, joined1, mixed_self1, q_blocks = call(
        functools.partial(front_kernel, query_count, head_size),
        (
            shape((rows, width), F32),
            shape((rows, width), F32),
            shape((rows, 1), F32),
            shape((rows, 3 * width), BF),
            shape((rows, width), BF),
            shape((sections, rows, wide), BF),
        ),
        x0, early_triple_matrix, early_mixing_exit_matrix, picture_asker_matrix, gains,
    )
    q = exchange(q_blocks).reshape(sections * rows, wide)

    gap = jnp.zeros((feat, wide - own_width), BF)
    w_pair = jnp.concatenate(
        [
            lax.dynamic_slice_in_dim(picture_pair_matrix, me * own_width, own_width, 1),
            gap,
            lax.dynamic_slice_in_dim(picture_pair_matrix, width + me * own_width, own_width, 1),
            gap,
        ],
        axis=1,
    )
    keyval = pl.pallas_call(
        keyval_kernel,
        out_shape=shape((images, padded, 2 * wide), BF),
        grid=(images,),
        in_specs=[
            pl.BlockSpec((1, patches, feat), lambda j: (j, 0, 0)),
            pl.BlockSpec((feat, 2 * wide), lambda j: (0, 0)),
        ],
        out_specs=pl.BlockSpec((1, padded, 2 * wide), lambda j: (j, 0, 0)),
        compiler_params=pltpu.CompilerParams(vmem_limit_bytes=LIMIT),
    )(frozen_picture_vectors, w_pair)

    static = (patches, own_heads, head_size, query_count)
    o = call(
        functools.partial(attend_image_kernel, *static, 4),
        shape((sections * rows, wide), BF),
        image_of, scale, q, keyval,
        in_specs=[whole(SMEM), whole(SMEM), whole(), whole()],
    )
    mixed1 = exchange(o.reshape(sections, rows, wide))

    def act(*dims, dtype=BF):
        return shape((rows,) + dims, dtype)

    weights = (
        picture_exit_matrix, early_widen_matrix, early_narrow_matrix, later_triple_matrix,
        later_mixing_exit_matrix, later_widen_matrix, later_narrow_matrix,
    )
    (
        final_blocks, low2, m1, du1, da3, low3, mixed2, djoined2, da4,
        low4, m2, du2, da5, da2, do_blocks, dz2, dg_mid,
    ) = call(
        functools.partial(middle_kernel, query_count, head_size),
        (
            shape((sections, rows, wide), BF),
            act(width), act(hidden), act(hidden), act(width),
            act(width), act(width), act(3 * width), act(width),
            act(width), act(hidden), act(hidden), act(width),
            act(width), shape((sections, rows, wide), BF), act(width, dtype=F32),
            shape((4, width), F32),
        ),
        h1, mixed1, own_rows(closing_cotangent), gains, *weights,
        in_specs=[whole()] * 4 + [whole(pl.ANY)] * len(weights),
        scratch=[pltpu.VMEM(w.shape, BF) for w in weights]
        + [pltpu.SemaphoreType.DMA((len(weights),))]
        + [pltpu.VMEM((rows, hidden), F32)] * 2
        + [pltpu.VMEM((rows, 3 * width), BF), pltpu.VMEM((rows, width), BF)]
        + [pltpu.VMEM((rows, width), F32), pltpu.VMEM((rows, 1), F32)] * 4,
    )

    do = exchange(do_blocks).reshape(sections * rows, wide)
    dq, dkv, temper_rows = call(
        functools.partial(attend_image_back_kernel, *static, 2),
        (
            shape((sections * rows, wide), BF),
            shape((images, padded, 2 * wide), BF),
            shape((own_heads * query_count, 1), F32),
        ),
        image_of, scale, q, do, keyval,
        in_specs=[whole(SMEM), whole(SMEM), whole(), whole(), whole()],
        scratch=[pltpu.VMEM((images, padded, 2 * wide), F32)],
    )
    dq_blocks = exchange(dq.reshape(sections, rows, wide))

    d_pair = pl.pallas_call(
        keyval_grad_kernel,
        out_shape=shape((feat, 2 * own_width), BF),
        grid=(images,),
        in_specs=[
            pl.BlockSpec((1, patches, feat), lambda j: (j, 0, 0)),
            pl.BlockSpec((1, padded, 2 * wide), lambda j: (j, 0, 0)),
        ],
        out_specs=pl.BlockSpec((feat, 2 * own_width), lambda j: (0, 0)),
        scratch_shapes=[pltpu.VMEM((2 * wide, feat), F32)],
        compiler_params=pltpu.CompilerParams(vmem_limit_bytes=LIMIT),
    )(frozen_picture_vectors, dkv)

    dq_rows, da1, djoined1, dx_blocks, dg0 = call(
        functools.partial(last_kernel, query_count, head_size),
        (
            act(width), act(width), act(3 * width),
            shape((sections, rows, wide), BF), shape((1, width), F32),
        ),
        dz2, dq_blocks, picture_asker_matrix, n1, r1, gains, early_mixing_exit_matrix, joined1,
        early_triple_matrix,
        scratch=[pltpu.VMEM((rows, width), BF)],
    )

    def block_unit(grad):
        parts, k, own = grad.shape
        return grad.reshape(parts, dp, k // dp, own)

    def pair_grad(x, dy, y, dz):
        own = (dy.shape[1] + dz.shape[1]) // sections
        return block_unit(
            call(pair_weight_kernel, shape((sections, x.shape[1], own), BF), x, dy, y, dz)
        )

    mixed1_rows = mixed1[:, :, :own_width].transpose(1, 0, 2).reshape(rows, width)
    low1 = h1.astype(BF)
    if width // dp % 32 == 0:
        (
            (expand2,), (reduce2,), (project2, out2), (expand1,), (reduce1,),
            (pair_block,), (asker, image_out), (project1, out1),
        ) = bring_home(
            [
                ("expand", (low4, du2), (hidden // sections,)),
                ("reduce", (da5, m2), ()),
                ("pair", (low3, djoined2, mixed2, da4), (3 * own_width, own_width)),
                ("expand", (low2, du1), (hidden // sections,)),
                ("reduce", (da3, m1), ()),
                ("made", (d_pair.reshape(1, dp // 2, 2, feat // dp, 2 * own_width),), ()),
                ("pair", (low1, dq_rows, mixed1_rows, da2), (own_width, own_width)),
                ("pair", (x0, djoined1, mixed_self1, da1), (3 * own_width, own_width)),
            ],
            sections, dp, width,
        )
    else:
        expand2 = home(block_unit(expand_grad(low4, du2, sections)))
        reduce2 = home(reduce_grad(da5, m2, sections, dp)).T
        self2 = home(pair_grad(low3, djoined2, mixed2, da4))
        expand1 = home(block_unit(expand_grad(low2, du1, sections)))
        reduce1 = home(reduce_grad(da3, m1, sections, dp)).T
        pair_block = line_sum(
            core_sum(d_pair.reshape(1, dp, feat // dp, 2 * own_width))[0]
        )
        image_units = home(pair_grad(low1, dq_rows, mixed1_rows, da2))
        self1 = home(pair_grad(x0, djoined1, mixed_self1, da1))
        third = 3 * own_width
        project2, out2 = self2[:, :third], self2[:, third:]
        project1, out1 = self1[:, :third], self1[:, third:]
        asker, image_out = image_units[:, :own_width], image_units[:, own_width:]

    def home_states(blocks):
        got = exchange(blocks).reshape(item_count, query_count, wide)
        return got[:, :, :own_width].astype(F32)

    final_part = home_states(final_blocks)
    grad_part = home_states(dx_blocks)

    pair_rows = pair_block.shape[0]
    half = sections // 2
    pair_halves = pair_block.astype(BF).reshape(pair_rows, 2, own_width).transpose(1, 0, 2)
    key_home, val_home = me // 2, half + me // 2
    sent = jnp.zeros((sections, pair_rows, own_width), BF)
    sent = lax.dynamic_update_index_in_dim(sent, pair_halves[0], key_home, 0)
    sent = lax.dynamic_update_index_in_dim(sent, pair_halves[1], val_home, 0)
    got = exchange(sent)
    first = (me % half) * 2
    pair_part = lax.dynamic_slice_in_dim(got, first, 2, 0)
    pair_part = pair_part.transpose(1, 0, 2).reshape(pair_rows, 2 * own_width).astype(F32)

    interior = ((picture_divisors > 0.5) & (picture_divisors < 2.0)).astype(F32)
    d_temper = jnp.sum(temper_rows.reshape(own_heads, query_count), axis=1)
    spread = jnp.zeros((heads,), F32)
    spread = lax.dynamic_update_slice_in_dim(spread, d_temper, me * own_heads, 0)
    spread = spread * (-scale_all / clamped) * interior
    small = jnp.concatenate([dg0.reshape(-1), dg_mid.reshape(-1), spread])
    small = all_sum(small)
    gains_grad = small[: 5 * width].reshape(5, width)
    temper_grad = small[5 * width :]

    def f(block):
        return block.astype(F32)

    return (
        final_part,
        grad_part,
        f(project1),
        f(out1),
        f(asker),
        pair_part,
        f(image_out),
        f(expand1),
        f(reduce1),
        f(project2),
        f(out2),
        f(expand2),
        f(reduce2),
        gains_grad,
        temper_grad,
    )


def solution(mesh):
    return jax.shard_map(
        body,
        mesh=mesh,
        in_specs=(P("dp", None, None), P("dp", None, None), P("dp", None))
        + (P(),) * 13
        + (P("dp", None, None),),
        out_specs=(P("dp", None, "section"),) * 2 + (P("dp", "section"),) * 11 + (P(), P()),
        check_vma=False,
    )
```

```python
import functools
import math

import jax
import jax.numpy as jnp
from jax import lax
from jax.experimental import pallas as pl
from jax.experimental.pallas import tpu as pltpu
from jax.sharding import PartitionSpec as P

EPSILON = 1e-06
BF = jnp.bfloat16
F32 = jnp.float32


def mm(left, right):
    return jnp.dot(left, right, preferred_element_type=F32)


def mm_tn(left, right):
    return lax.dot_general(left, right, (((0,), (0,)), ((), ())), preferred_element_type=F32)


def mm_nt(left, right):
    return lax.dot_general(left, right, (((1,), (1,)), ((), ())), preferred_element_type=F32)


def layer_norm(z, gain):
    centred = z - jnp.mean(z, axis=-1, keepdims=True)
    inverse = lax.rsqrt(jnp.mean(centred * centred, axis=-1, keepdims=True) + EPSILON)
    normed = centred * inverse
    return normed * gain, normed, inverse


def norm_back(dout, gain, normed, inverse):
    dn = dout * gain
    dgain = jnp.sum(dout * normed, axis=0)
    dz = inverse * (
        dn
        - jnp.mean(dn, axis=-1, keepdims=True)
        - normed * jnp.mean(dn * normed, axis=-1, keepdims=True)
    )
    return dz, dgain


def gelu_both(u):
    x = jnp.abs(u) * (0.5**0.5)
    e = jnp.exp(-0.5 * u * u)
    s = 1.0 / (1.0 + 0.3275911 * x)
    poly = s * (
        0.254829592
        + s * (-0.284496736 + s * (1.421413741 + s * (-1.453152027 + s * 1.061405429)))
    )
    tail = 0.5 * poly * e
    cdf = jnp.where(u < 0.0, tail, 1.0 - tail)
    return u * cdf, cdf + u * e * (1.0 / math.sqrt(2.0 * math.pi))


def swap(value, axis, bit):
    size = lax.axis_size(axis)
    return lax.ppermute(value, axis, [(i, i ^ bit) for i in range(size)])


def pick(value, index, axis):
    return lax.dynamic_index_in_dim(value, index, axis, keepdims=False)


def add_low(left, right):
    return (left.astype(F32) + right.astype(F32)).astype(BF)


def section_blocks(value):
    rows, width = value.shape
    parts = lax.axis_size("section")
    return value.reshape(rows, parts, width // parts).transpose(1, 0, 2)


def exchange(blocks):
    me = lax.axis_index("section")
    parts = lax.axis_size("section")
    out = blocks
    for bit in range(1, parts):
        got = swap(pick(blocks, me ^ bit, 0), "section", bit)
        out = lax.dynamic_update_index_in_dim(out, got, me ^ bit, 0)
    return out


def cols_to_section(value):
    return exchange(section_blocks(value))


def rows_from_section(blocks):
    got = exchange(blocks)
    parts, rows, width = got.shape
    return got.transpose(1, 0, 2).reshape(rows, parts * width)


def line_sum(blocks):
    n = blocks.shape[0]
    p = lax.axis_index("dp") // 2
    size = lax.axis_size("dp")
    kept = blocks
    for k in range(n - 1):
        up_at = jnp.clip(n - 1 - k + p, 0, n - 1)
        down_at = jnp.clip(p - (n - 1 - k), 0, n - 1)
        up_pairs = [(2 * q + c, 2 * q + 2 + c) for q in range(min(k, n - 2) + 1) for c in (0, 1)]
        down_pairs = [
            (2 * q + c, 2 * q - 2 + c) for q in range(max(n - 1 - k, 1), n) for c in (0, 1)
        ]
        up = lax.ppermute(pick(kept, up_at, 0), "dp", up_pairs)
        down = lax.ppermute(pick(kept, down_at, 0), "dp", down_pairs)
        up_to = jnp.clip(n - 2 - k + p, 0, n - 1)
        down_to = jnp.clip(p + 1 - (n - 1 - k), 0, n - 1)
        kept = lax.dynamic_update_index_in_dim(kept, add_low(pick(kept, up_to, 0), up), up_to, 0)
        kept = lax.dynamic_update_index_in_dim(
            kept, add_low(pick(kept, down_to, 0), down), down_to, 0
        )
    del size
    return pick(kept, p, 0)


def core_sum(unit):
    parts, dp, r, w = unit.shape
    c = lax.axis_index("dp") % 2
    pairs = unit.reshape(parts, dp // 2, 2, r, w)
    return add_low(pick(pairs, c, 2), swap(pick(pairs, 1 - c, 2), "dp", 1))


def plane_sum(unit):
    parts, n, r, w = unit.shape
    me = lax.axis_index("section")
    low, high = me % 2, me // 2
    square = unit.reshape(2, 2, n, r, w)
    a, b = square[:, :, :, : r // 2], square[:, :, :, r // 2 :]
    a = add_low(pick(a, low, 1), swap(pick(a, 1 - low, 1), "section", 1))
    b = add_low(pick(b, high, 0), swap(pick(b, 1 - high, 0), "section", 2))
    a = add_low(pick(a, high, 0), swap(pick(a, 1 - high, 0), "section", 2))
    b = add_low(pick(b, low, 0), swap(pick(b, 1 - low, 0), "section", 1))
    return jnp.concatenate([a, b], axis=1)


def home(unit):
    return line_sum(plane_sum(core_sum(unit)))


def unit_of(grad, dp, sections):
    rows, cols = grad.shape
    return (
        grad.astype(BF)
        .reshape(dp, rows // dp, sections, cols // sections)
        .transpose(2, 0, 1, 3)
    )


def all_sum(value):
    for axis in ("dp", "section"):
        bit = 1
        while bit < lax.axis_size(axis):
            value = value + swap(value, axis, bit)
            bit *= 2
    return value


VMEM = pltpu.MemorySpace.VMEM
SMEM = pltpu.MemorySpace.SMEM
LIMIT = 60 * 1024 * 1024
GROUP = 128


def whole(space=VMEM):
    return pl.BlockSpec(memory_space=space)


def head_lanes(shape, head, head_size):
    return lax.broadcasted_iota(jnp.int32, shape, len(shape) - 1) // head_size == head


def same_item(query_count):
    shape = (GROUP, GROUP)
    left = lax.broadcasted_iota(jnp.int32, shape, 0) // query_count
    right = lax.broadcasted_iota(jnp.int32, shape, 1) // query_count
    return left == right


def soft(t, mask, scale):
    t = jnp.where(mask, t * scale, -1e30)
    e = jnp.exp(t - jnp.max(t, axis=-1, keepdims=True))
    return e / jnp.sum(e, axis=-1, keepdims=True)


def masked(value, head, head_size):
    return jnp.where(head_lanes(value.shape, head, head_size), value, jnp.zeros_like(value))


def attend_self(joined_ref, mixed_ref, query_count, head_size):
    rows, width = mixed_ref.shape
    pair = 2 * head_size
    scale = 1.0 / math.sqrt(head_size)
    mask = same_item(query_count)

    def step(i, _):
        col = pl.multiple_of(i * pair, pair)
        for g in range(rows // GROUP):
            at = pl.ds(g * GROUP, GROUP)
            q = joined_ref[at, pl.ds(col, pair)]
            k = joined_ref[at, pl.ds(width + col, pair)]
            v = joined_ref[at, pl.ds(2 * width + col, pair)]
            o = jnp.zeros((GROUP, pair), F32)
            for h in range(2):
                p = soft(mm_nt(masked(q, h, head_size), k), mask, scale).astype(BF)
                o = o + mm(p, masked(v, h, head_size))
            mixed_ref[at, pl.ds(col, pair)] = o.astype(BF)
        return 0

    lax.fori_loop(0, width // pair, step, 0)


def attend_self_back(joined_ref, do_ref, djoined_ref, query_count, head_size):
    rows, width = do_ref.shape
    pair = 2 * head_size
    scale = 1.0 / math.sqrt(head_size)
    mask = same_item(query_count)

    def step(i, _):
        col = pl.multiple_of(i * pair, pair)
        for g in range(rows // GROUP):
            at = pl.ds(g * GROUP, GROUP)
            q = joined_ref[at, pl.ds(col, pair)]
            k = joined_ref[at, pl.ds(width + col, pair)]
            v = joined_ref[at, pl.ds(2 * width + col, pair)]
            do = do_ref[at, pl.ds(col, pair)]
            dq = jnp.zeros((GROUP, pair), F32)
            dk = jnp.zeros((GROUP, pair), F32)
            dv = jnp.zeros((GROUP, pair), F32)
            for h in range(2):
                qh, kh = masked(q, h, head_size), masked(k, h, head_size)
                doh = masked(do, h, head_size)
                p = soft(mm_nt(qh, k), mask, scale)
                dp = mm_nt(doh, v)
                ds = p * (dp - jnp.sum(p * dp, axis=-1, keepdims=True))
                dt = (ds * scale).astype(BF)
                dv = dv + mm_tn(p.astype(BF), doh)
                dq = dq + mm(dt, kh)
                dk = dk + mm_tn(dt, qh)
            djoined_ref[at, pl.ds(col, pair)] = dq.astype(BF)
            djoined_ref[at, pl.ds(width + col, pair)] = dk.astype(BF)
            djoined_ref[at, pl.ds(2 * width + col, pair)] = dv.astype(BF)
        return 0

    lax.fori_loop(0, width // pair, step, 0)


def project_into(out_ref, low, w_ref, block=768):
    for at in range(0, w_ref.shape[1], block):
        out_ref[:, at : at + block] = mm(low, w_ref[:, at : at + block]).astype(BF)


def back_through(dy_ref, w_ref, block=768):
    total = None
    for at in range(0, w_ref.shape[1], block):
        term = mm_nt(dy_ref[:, at : at + block], w_ref[:, at : at + block])
        total = term if total is None else total + term
    return total


def hidden_forward(low, w_expand_ref, w_reduce_ref, m_ref, slope_ref, block=512):
    total = None
    for at in range(0, w_expand_ref.shape[1], block):
        u = mm(low, w_expand_ref[:, at : at + block]).astype(BF).astype(F32)
        m, slope = gelu_both(u)
        m = m.astype(BF)
        m_ref[:, at : at + block] = m
        slope_ref[:, at : at + block] = slope
        term = mm(m, w_reduce_ref[at : at + block, :])
        total = term if total is None else total + term
    return total


def hidden_backward(da, w_expand_ref, w_reduce_ref, slope_ref, du_ref, block=512):
    total = None
    for at in range(0, w_expand_ref.shape[1], block):
        dm = mm_nt(da, w_reduce_ref[at : at + block, :])
        du = (dm * slope_ref[:, at : at + block]).astype(BF)
        du_ref[:, at : at + block] = du
        term = mm_nt(du, w_expand_ref[:, at : at + block])
        total = term if total is None else total + term
    return total


def norm_into(z, gain, n_ref, r_ref):
    out, n, r = layer_norm(z, gain)
    n_ref[...] = n
    r_ref[...] = r
    return out


def put_blocks(out_ref, value):
    parts, _, wide = out_ref.shape
    own = value.shape[1] // parts
    for t in range(parts):
        out_ref[t, :, :own] = value[:, t * own : (t + 1) * own]
        if wide > own:
            out_ref[t, :, own:] = jnp.zeros((value.shape[0], wide - own), out_ref.dtype)


def take_blocks(in_ref, own):
    return jnp.concatenate([in_ref[t, :, :own] for t in range(in_ref.shape[0])], axis=1)


def front_kernel(
    query_count, head_size, x_ref, wp_ref, wo_ref, wq_ref, g_ref,
    h_ref, low_ref, n_ref, r_ref, joined_ref, mixed_ref, q_ref,
):
    low = x_ref[...]
    project_into(joined_ref, low, wp_ref)
    attend_self(joined_ref, mixed_ref, query_count, head_size)
    z = low.astype(F32) + mm(mixed_ref[...], wo_ref[...])
    h = norm_into(z, g_ref[0:1, :], n_ref, r_ref)
    h_ref[...] = h
    low_ref[...] = h.astype(BF)
    put_blocks(q_ref, mm(low_ref[...], wq_ref[...]).astype(BF))


def keyval_kernel(x_ref, w_ref, out_ref):
    patches = x_ref.shape[1]
    padded = out_ref.shape[1]
    full = patches // 16 * 16
    out_ref[0, full:, :] = jnp.zeros((padded - full, out_ref.shape[2]), BF)
    out_ref[0, :patches, :] = mm(x_ref[0], w_ref[...]).astype(BF)


def stacked(value, own_heads, head_size):
    return jnp.concatenate([masked(value, h, head_size) for h in range(own_heads)], axis=0)


def unstacked(value, own_heads, head_size):
    rows = value.shape[0] // own_heads
    total = None
    for h in range(own_heads):
        part = masked(value[h * rows : (h + 1) * rows], h, head_size)
        total = part if total is None else total + part
    return total


def row_scales(scale_ref, own_heads, query_count):
    return jnp.concatenate(
        [jnp.full((query_count, 1), scale_ref[0, h], F32) for h in range(own_heads)], axis=0
    )


def attend_image_kernel(
    patches, own_heads, head_size, query_count, together,
    image_ref, scale_ref, q_ref, kv_ref, o_ref,
):
    wide = q_ref.shape[1]
    items = q_ref.shape[0] // query_count
    padded = kv_ref.shape[1]
    scales = row_scales(scale_ref, own_heads, query_count)
    mask = lax.broadcasted_iota(jnp.int32, (1, padded), 1) < patches

    def step(i, _):
        for b in range(together):
            item = i * together + b
            at = pl.ds(pl.multiple_of(item * query_count, query_count), query_count)
            j = image_ref[0, item]
            q = stacked(q_ref[at, :], own_heads, head_size)
            p = soft(mm_nt(q, kv_ref[j, :, :wide]), mask, scales)
            o = mm(p.astype(BF), kv_ref[j, :, wide:])
            o_ref[at, :] = unstacked(o, own_heads, head_size).astype(BF)
        return 0

    lax.fori_loop(0, items // together, step, 0)


def attend_image_back_kernel(
    patches, own_heads, head_size, query_count, together,
    image_ref, scale_ref, q_ref, do_ref, kv_ref, dq_ref, dkv_ref, temper_ref, total_ref,
):
    wide = q_ref.shape[1]
    items = q_ref.shape[0] // query_count
    padded = kv_ref.shape[1]
    scales = row_scales(scale_ref, own_heads, query_count)
    mask = lax.broadcasted_iota(jnp.int32, (1, padded), 1) < patches
    total_ref[...] = jnp.zeros_like(total_ref)
    temper_ref[...] = jnp.zeros_like(temper_ref)

    def step(i, _):
        temper = None
        for b in range(together):
            item = i * together + b
            at = pl.ds(pl.multiple_of(item * query_count, query_count), query_count)
            j = image_ref[0, item]
            q = stacked(q_ref[at, :], own_heads, head_size)
            do = stacked(do_ref[at, :], own_heads, head_size)
            k, v = kv_ref[j, :, :wide], kv_ref[j, :, wide:]
            t = mm_nt(q, k)
            p = soft(t, mask, scales)
            dp = mm_nt(do, v)
            ds = p * (dp - jnp.sum(p * dp, axis=-1, keepdims=True))
            term = jnp.sum(ds * t, axis=-1, keepdims=True)
            temper = term if temper is None else temper + term
            dt = (ds * scales).astype(BF)
            dq_ref[at, :] = unstacked(mm(dt, k), own_heads, head_size).astype(BF)
            total_ref[j, :, :wide] += mm_tn(dt, q)
            total_ref[j, :, wide:] += mm_tn(p.astype(BF), do)
        temper_ref[...] += temper
        return 0

    lax.fori_loop(0, items // together, step, 0)
    dkv_ref[...] = total_ref[...].astype(BF)


def keyval_grad_kernel(x_ref, dkv_ref, out_ref, total_ref):
    @pl.when(pl.program_id(0) == 0)
    def _():
        total_ref[...] = jnp.zeros_like(total_ref)

    patches = x_ref.shape[1]
    total_ref[...] += mm_tn(dkv_ref[0, :patches, :], x_ref[0])

    @pl.when(pl.program_id(0) == pl.num_programs(0) - 1)
    def _():
        own = out_ref.shape[1] // 2
        wide = total_ref.shape[0] // 2
        out_ref[...] = jnp.concatenate(
            [total_ref[:own, :].T, total_ref[wide : wide + own, :].T], axis=1
        ).astype(BF)


def middle_kernel(
    query_count, head_size,
    h1_ref, mixed1_ref, dout_ref, g_ref,
    wx_hbm, we1_hbm, wr1_hbm, wp_hbm, wo_hbm, we2_hbm, wr2_hbm,
    final_ref, low2_ref, m1_ref, du1_ref, da3_ref, low3_ref, mixed2_ref, djoined_ref, da4_ref,
    low4_ref, m2_ref, du2_ref, da5_ref, mixed1_out, da2_ref, do_ref, dz2_ref, dg_ref,
    wx, we1, wr1, wp, wo, we2, wr2, sems,
    slope1, slope2, joined, do2, n2, r2, n3, r3, n4, r4, n5, r5,
):
    copies = [
        pltpu.make_async_copy(src, dst, sems.at[i])
        for i, (src, dst) in enumerate(
            zip((wx_hbm, we1_hbm, wr1_hbm, wp_hbm, wo_hbm, we2_hbm, wr2_hbm),
                (wx, we1, wr1, wp, wo, we2, wr2))
        )
    ]
    for copy in copies:
        copy.start()
    own = wx.shape[0] // mixed1_ref.shape[0]
    mixed1_out[...] = take_blocks(mixed1_ref, own)
    copies[0].wait()
    h2 = norm_into(h1_ref[...] + mm(mixed1_out[...], wx[...]), g_ref[1:2, :], n2, r2)
    low2_ref[...] = h2.astype(BF)
    copies[1].wait()
    copies[2].wait()
    a = hidden_forward(low2_ref[...], we1, wr1, m1_ref, slope1)
    h3 = norm_into(n2[...] * g_ref[1:2, :] + a, g_ref[2:3, :], n3, r3)
    low3_ref[...] = h3.astype(BF)
    copies[3].wait()
    project_into(joined, low3_ref[...], wp)
    attend_self(joined, mixed2_ref, query_count, head_size)
    copies[4].wait()
    a = mm(mixed2_ref[...], wo[...])
    h4 = norm_into(n3[...] * g_ref[2:3, :] + a, g_ref[3:4, :], n4, r4)
    low4_ref[...] = h4.astype(BF)
    copies[5].wait()
    copies[6].wait()
    a = hidden_forward(low4_ref[...], we2, wr2, m2_ref, slope2)
    h5 = norm_into(n4[...] * g_ref[3:4, :] + a, g_ref[4:5, :], n5, r5)
    put_blocks(final_ref, h5.astype(BF))

    dz, dg4 = norm_back(dout_ref[...].astype(F32), g_ref[4:5, :], n5[...], r5[...])
    da5_ref[...] = dz.astype(BF)
    d4 = dz + hidden_backward(da5_ref[...], we2, wr2, slope2, du2_ref)

    dz, dg3 = norm_back(d4, g_ref[3:4, :], n4[...], r4[...])
    da4_ref[...] = dz.astype(BF)
    do2[...] = mm_nt(da4_ref[...], wo[...]).astype(BF)
    attend_self_back(joined, do2, djoined_ref, query_count, head_size)
    d3 = dz + back_through(djoined_ref, wp)

    dz, dg2 = norm_back(d3, g_ref[2:3, :], n3[...], r3[...])
    da3_ref[...] = dz.astype(BF)
    d2 = dz + hidden_backward(da3_ref[...], we1, wr1, slope1, du1_ref)

    dz, dg1 = norm_back(d2, g_ref[1:2, :], n2[...], r2[...])
    dz2_ref[...] = dz
    da2_ref[...] = dz.astype(BF)
    put_blocks(do_ref, mm_nt(da2_ref[...], wx[...]).astype(BF))
    dg_ref[...] = jnp.concatenate([d[None, :] for d in (dg1, dg2, dg3, dg4)], axis=0)


def last_kernel(
    query_count, head_size, dz2_ref, dq_ref, wq_ref, n_ref, r_ref, g_ref, wo_ref, joined_ref, wp_ref,
    dqr_ref, da_ref, djoined_ref, dx_ref, dg_ref, do,
):
    own = wq_ref.shape[1] // dq_ref.shape[0]
    dqr_ref[...] = take_blocks(dq_ref, own)
    d1 = dz2_ref[...] + mm_nt(dqr_ref[...], wq_ref[...])
    dz, dg = norm_back(d1, g_ref[0:1, :], n_ref[...], r_ref[...])
    dg_ref[...] = dg[None, :]
    da_ref[...] = dz.astype(BF)
    do[...] = mm_nt(da_ref[...], wo_ref[...]).astype(BF)
    attend_self_back(joined_ref, do, djoined_ref, query_count, head_size)
    put_blocks(dx_ref, (dz + back_through(djoined_ref, wp_ref)).astype(BF))


def weight_kernel(x_ref, dy_ref, out_ref):
    out_ref[0] = mm_tn(x_ref[...], dy_ref[...]).astype(BF)


def pair_weight_kernel(x_ref, dy_ref, y_ref, dz_ref, out_ref):
    parts = out_ref.shape[0]
    own_a, own_b = dy_ref.shape[1] // parts, dz_ref.shape[1] // parts
    for t in range(parts):
        a = mm_tn(x_ref[...], dy_ref[:, t * own_a : (t + 1) * own_a]).astype(BF)
        b = mm_tn(y_ref[...], dz_ref[:, t * own_b : (t + 1) * own_b]).astype(BF)
        out_ref[t] = jnp.concatenate([a, b], axis=1)


def turned_weight_kernel(dy_ref, x_ref, out_ref):
    _, dp, own, wide = out_ref.shape
    r = mm_tn(dy_ref[...], x_ref[...]).astype(BF)
    for d in range(dp):
        out_ref[0, d] = r[:, d * wide : (d + 1) * wide]


def shape(dims, dtype):
    return jax.ShapeDtypeStruct(tuple(dims), dtype)


def call(kernel, outs, *args, in_specs=None, scratch=(), flops=0):
    return pl.pallas_call(
        kernel,
        out_shape=outs,
        in_specs=in_specs or [whole()] * len(args),
        out_specs=jax.tree.map(lambda _: whole(), outs),
        scratch_shapes=list(scratch),
        compiler_params=pltpu.CompilerParams(vmem_limit_bytes=LIMIT),
        cost_estimate=pl.CostEstimate(
            flops=flops, bytes_accessed=int(flops) // 400, transcendentals=0
        ),
    )(*args)


def expand_grad(low, du, parts):
    rows, width = low.shape
    own = du.shape[1] // parts
    return pl.pallas_call(
        weight_kernel,
        out_shape=shape((parts, width, own), BF),
        grid=(parts,),
        in_specs=[
            pl.BlockSpec((rows, width), lambda t: (0, 0)),
            pl.BlockSpec((rows, own), lambda t: (0, t)),
        ],
        out_specs=pl.BlockSpec((1, width, own), lambda t: (t, 0, 0)),
        compiler_params=pltpu.CompilerParams(vmem_limit_bytes=LIMIT),
    )(low, du)


def reduce_grad(da, m, parts, dp):
    rows, width = da.shape
    wide = m.shape[1] // dp
    own = width // parts
    per = 4 if dp % 4 == 0 and (dp // 4 * wide) % 128 == 0 else 1
    blocks = dp // per
    return pl.pallas_call(
        functools.partial(turned_weight_all_kernel, parts),
        out_shape=shape((parts, dp, own, wide), BF),
        grid=(per,),
        in_specs=[
            pl.BlockSpec((rows, width), lambda b: (0, 0)),
            pl.BlockSpec((rows, blocks * wide), lambda b: (0, b)),
        ],
        out_specs=pl.BlockSpec((parts, blocks, own, wide), lambda b: (0, b, 0, 0)),
        compiler_params=pltpu.CompilerParams(vmem_limit_bytes=LIMIT),
    )(da, m)


def turned_weight_all_kernel(parts, dy_ref, x_ref, out_ref):
    _, blocks, own, wide = out_ref.shape
    r = mm_tn(dy_ref[...], x_ref[...]).astype(BF)
    for t in range(parts):
        for d in range(blocks):
            out_ref[t, d] = r[t * own : (t + 1) * own, d * wide : (d + 1) * wide]


MESH = pl.DeviceIdType.MESH


def device_of(section, z, core):
    return (section, z * 2 + core)


class Home:
    def __init__(self, unit, kept, from_x, from_y, then_x, then_y, from_z, sends, recvs):
        self.unit, self.kept = unit, kept
        self.from_x, self.from_y = from_x, from_y
        self.then_x, self.then_y = then_x, then_y
        self.from_z = from_z
        self.sends, self.recvs = sends, recvs
        self.s, d = lax.axis_index("section"), lax.axis_index("dp")
        self.sx, self.sy = self.s % 2, self.s // 2
        self.z, self.c = d // 2, d % 2
        self.half = kept.shape[2] // 2

    def copy(self, i, src, dst, device):
        return pltpu.make_async_remote_copy(
            src_ref=src, dst_ref=dst, send_sem=self.sends.at[i], recv_sem=self.recvs.at[i],
            device_id=device, device_id_type=MESH,
        )

    def mine(self):
        return self.s if self.kept.shape[0] > 1 else 0

    def cores(self):
        return [
            self.copy(
                0, self.unit.at[:, :, 1 - self.c], self.kept, device_of(self.s, self.z, 1 - self.c)
            )
        ]

    def first(self):
        s, sx, sy, z, c, half = self.s, self.sx, self.sy, self.z, self.c, self.half
        out = []
        for i in range(2):
            out.append(self.copy(
                1 + i, self.kept.at[2 * i + 1 - sx, :, :half], self.from_x.at[i],
                device_of(s + 1 - 2 * sx, z, c),
            ))
            out.append(self.copy(
                3 + i, self.kept.at[2 * (1 - sy) + i, :, half:], self.from_y.at[i],
                device_of(s + 2 - 4 * sy, z, c),
            ))
        return out

    def second(self):
        s, sx, sy, z, c, half = self.s, self.sx, self.sy, self.z, self.c, self.half
        return [
            self.copy(
                5, self.kept.at[2 * (1 - sy) + sx, :, :half], self.then_y,
                device_of(s + 2 - 4 * sy, z, c),
            ),
            self.copy(
                6, self.kept.at[2 * sy + 1 - sx, :, half:], self.then_x,
                device_of(s + 1 - 2 * sx, z, c),
            ),
        ]

    def along(self):
        n = self.kept.shape[1]
        out = []
        for k in range(1, n):
            to = (self.z + k) % n
            out.append(self.copy(
                6 + k, self.kept.at[self.mine(), to], self.from_z.at[k - 1],
                device_of(self.s, to, self.c),
            ))
        return out

    def add_cores(self):
        n = self.kept.shape[1]

        def step(i, _):
            t, z = i // n, i % n
            self.kept[t, z] = self.kept[t, z] + self.unit[t, z, self.c]
            return 0

        lax.fori_loop(0, self.kept.shape[0] * n, step, 0)

    def add_first(self):
        n, half = self.kept.shape[1], self.half

        def step(i, _):
            t, z = i // n, i % n
            x, y = 2 * t + self.sx, 2 * self.sy + t
            self.kept[x, z, :half] = self.kept[x, z, :half] + self.from_x[t, z]
            self.kept[y, z, half:] = self.kept[y, z, half:] + self.from_y[t, z]
            return 0

        lax.fori_loop(0, 2 * n, step, 0)

    def add_second(self):
        n, half = self.kept.shape[1], self.half

        def step(z, _):
            self.kept[self.s, z, :half] = self.kept[self.s, z, :half] + self.then_y[z]
            self.kept[self.s, z, half:] = self.kept[self.s, z, half:] + self.then_x[z]
            return 0

        lax.fori_loop(0, n, step, 0)

    def total(self):
        total = self.kept[self.mine(), self.z].astype(F32)
        for k in range(self.from_z.shape[0]):
            total = total + self.from_z[k].astype(F32)
        return total


def start(copies):
    for copy in copies:
        copy.start()


def wait(copies):
    for copy in copies:
        copy.wait()


def greet():
    s, d = lax.axis_index("section"), lax.axis_index("dp")
    sections, dp = lax.axis_size("section"), lax.axis_size("dp")
    n = dp // 2
    z, c = d // 2, d % 2
    barrier = pltpu.get_barrier_semaphore()
    near = [device_of(s, z, 1 - c)]
    for bit in range(1, sections):
        near.append(device_of(s ^ bit, z, c))
    for k in range(1, n):
        near.append(device_of(s, (z + k) % n, c))
    for device in near:
        pl.semaphore_signal(barrier, inc=1, device_id=device, device_id_type=MESH)
    pl.semaphore_wait(barrier, len(near))


def fill_expand(unit, low, du):
    parts, n, two, r, w = unit.shape
    for t in range(parts):
        g = mm_tn(low[...], du[:, t * w : (t + 1) * w]).astype(BF)
        for d in range(2 * n):
            unit[t, d // 2, d % 2] = g[d * r : (d + 1) * r]


def fill_reduce(unit, da, m):
    parts, n, two, r, w = unit.shape
    own = w // 2
    for z in range(n):
        g = mm_tn(da[...], m[:, 2 * z * own : 2 * (z + 1) * own]).astype(BF)
        for c in range(2):
            for t in range(parts):
                for i in range(2):
                    at = (2 * t + i) * r
                    unit[t, z, c, :, i * own : (i + 1) * own] = g[
                        at : at + r, c * own : (c + 1) * own
                    ]


def fill_pair(unit, x, dy, y, dz):
    parts, n, two, r, w = unit.shape
    own_a, own_b = dy.shape[1] // parts, dz.shape[1] // parts
    for t in range(parts):
        a = mm_tn(x[...], dy[:, t * own_a : (t + 1) * own_a]).astype(BF)
        b = mm_tn(y[...], dz[:, t * own_b : (t + 1) * own_b]).astype(BF)
        g = jnp.concatenate([a, b], axis=1)
        for d in range(2 * n):
            unit[t, d // 2, d % 2] = g[d * r : (d + 1) * r]


def exchange_copies(source, target, sends, recvs):
    s, d = lax.axis_index("section"), lax.axis_index("dp")
    out = []
    for bit in range(1, lax.axis_size("section")):
        to = s ^ bit
        out.append(pltpu.make_async_remote_copy(
            src_ref=source.at[to], dst_ref=target.at[s], send_sem=sends.at[bit],
            recv_sem=recvs.at[bit], device_id=(to, d), device_id_type=MESH,
        ))
    out.append(pltpu.make_async_copy(source.at[s], target.at[s], sends.at[0]))
    return out


def tail_kernel(query_count, head_size, *refs):
    refs = list(refs)

    def take(count):
        out = refs[:count]
        del refs[:count]
        return out

    final_blocks, dq_blocks = take(2)
    low4, du2, da5, m2 = take(4)
    low3, djoined2, mixed2, da4 = take(4)
    low2, du1, da3, m1 = take(4)
    low1, mixed1, da2, x0, mixed_self1 = take(5)
    images, dkv, wq_hbm, wo_hbm, wp_hbm = take(5)
    dz2, n1, r1, gains, joined1, dg_mid, temper_rows = take(7)
    final_got, dx_got, small = take(3)
    expand2, reduce2, project2, out2, expand1, reduce1, asker, image_out, project1, out1 = take(10)
    pair_out = take(1)[0]
    units = ("expand2", "reduce2", "self1", "self2", "expand1", "reduce1", "image")
    buffers = {name: take(6) for name in units}
    pair_unit, pair_kept, pair_from_z, pair_low, pair_got = take(5)
    wide, sends, recvs, slots_a, slots_b, slots_c, slots_d, loads = take(8)
    slots = (slots_a, slots_b, slots_c, slots_d)
    dq_got, dqr, da1, djoined1, dx_blocks, sums, state_sends, state_recvs, local = take(9)
    own_heads = temper_rows.shape[0] // query_count

    s, d = lax.axis_index("section"), lax.axis_index("dp")
    z, c = d // 2, d % 2

    homes = {}
    for i, name in enumerate(units):
        unit = wide.at[:, :, :, :, : buffers[name][0].shape[3]]
        homes[name] = Home(unit, *buffers[name], sends.at[i], recvs.at[i])
    homes["pair"] = Home(
        pair_unit, pair_kept, None, None, None, None, pair_from_z,
        sends.at[len(units)], recvs.at[len(units)],
    )
    factors = {
        "expand2": (low4, du2), "reduce2": (da5, m2), "self2": (low3, djoined2, mixed2, da4),
        "expand1": (low2, du1), "reduce1": (da3, m1), "image": (low1, dqr, mixed1, da2),
        "self1": (x0, djoined1, mixed_self1, da1),
    }
    results = {
        "expand2": (expand2,), "reduce2": (reduce2,), "self2": (project2, out2),
        "expand1": (expand1,), "reduce1": (reduce1,), "image": (asker, image_out),
        "self1": (project1, out1),
    }

    def held(name):
        return [
            slots[j].at[:, : source.shape[1]] for j, source in enumerate(factors[name])
        ]

    def fetch(name):
        return [
            pltpu.make_async_copy(source, target, loads.at[units.index(name), j])
            for j, (source, target) in enumerate(zip(factors[name], held(name)))
        ]

    def make(name):
        wait(fetch(name))
        if name.startswith("expand"):
            fill_expand(homes[name].unit, *held(name))
        elif name.startswith("reduce"):
            fill_reduce(homes[name].unit, *held(name))
        else:
            fill_pair(homes[name].unit, *held(name))
        start(homes[name].cores())

    def finish(name):
        wait(homes[name].along())
        total = homes[name].total()
        out = results[name]
        if name.startswith("reduce"):
            own = total.shape[1] // 2
            out[0][...] = jnp.concatenate([total[:, :own].T, total[:, own:].T], axis=1)
        elif name.startswith("expand"):
            out[0][...] = total
        else:
            own = out[0].shape[1]
            out[0][...] = total[:, :own]
            out[1][...] = total[:, own:]

    steps = [("dp", 1), ("section", 1), ("section", 2)]
    bit = 2
    while bit < lax.axis_size("dp"):
        steps.append(("dp", bit))
        bit *= 2

    def small_copy(k):
        axis, bit = steps[k]
        to = (s ^ bit, d) if axis == "section" else (s, d ^ bit)
        return [pltpu.make_async_remote_copy(
            src_ref=small, dst_ref=sums.at[k], send_sem=state_sends.at[8 + k],
            recv_sem=state_recvs.at[8 + k], device_id=to, device_id_type=MESH,
        )]

    def small_step(k):
        if k > 0:
            wait(small_copy(k - 1))
            small[...] = small[...] + sums[k - 1]
        if k < len(steps):
            start(small_copy(k))

    finals = exchange_copies(final_blocks, final_got, state_sends.at[pl.ds(0, 4)], state_recvs.at[pl.ds(0, 4)])
    dqs = exchange_copies(dq_blocks, dq_got, state_sends.at[pl.ds(4, 4)], state_recvs.at[pl.ds(4, 4)])
    dxs = exchange_copies(dx_blocks, dx_got, state_sends.at[pl.ds(16, 4)], state_recvs.at[pl.ds(16, 4)])

    def rest_of_states(wq, wo, wp, do):
        own = wq.shape[1] // dq_got.shape[0]
        wait(dqs)
        wait([pltpu.make_async_copy(*one) for one in
              ((wq_hbm, wq, local.at[0]), (wo_hbm, wo, local.at[1]), (wp_hbm, wp, local.at[2]))])
        dqr[...] = take_blocks(dq_got, own)
        d1 = dz2[...] + mm_nt(dqr[...], wq[...])
        dz, dg = norm_back(d1, gains[0:1, :], n1[...], r1[...])
        da1[...] = dz.astype(BF)
        do[...] = mm_nt(da1[...], wo[...]).astype(BF)
        attend_self_back(joined1, do, djoined1, query_count, head_size)
        put_blocks(dx_blocks, (dz + back_through(djoined1, wp)).astype(BF))
        start(dxs)
        width = small.shape[1]
        lane = lax.broadcasted_iota(jnp.int32, (1, width), 1)
        row = jnp.zeros((1, width), F32)
        for h in range(own_heads):
            one = jnp.sum(temper_rows[h * query_count : (h + 1) * query_count, :], keepdims=True)
            row = row + jnp.where(lane == s * own_heads + h, one, 0.0)
        small[...] = jnp.concatenate(
            [dg[None, :], dg_mid[...], row, jnp.zeros((2, width), F32)], axis=0
        )

    def image_block(j, slot, blocks):
        return pltpu.make_async_copy(
            images.at[j], blocks.at[slot], local.at[4 + slot]
        )

    def pair_gradient(blocks, kv, total):
        patches = images.shape[1]
        copy = pltpu.make_async_copy(dkv, kv, local.at[3])
        copy.start()
        image_block(0, 0, blocks).start()
        total[...] = jnp.zeros_like(total)
        copy.wait()
        for j in range(images.shape[0]):
            image_block(j, j % 2, blocks).wait()
            if j + 1 < images.shape[0]:
                image_block(j + 1, (j + 1) % 2, blocks).start()
            total[...] += mm_tn(kv[j, :patches, :], blocks[j % 2])
        own = pair_unit.shape[4] // 2
        half = total.shape[0] // 2
        turned = jnp.concatenate(
            [total[:own, :].T, total[half : half + own, :].T], axis=1
        ).astype(BF)
        r = pair_unit.shape[3]
        for i in range(2 * pair_unit.shape[1]):
            pair_unit[0, i // 2, i % 2] = turned[i * r : (i + 1) * r]
        start(homes["pair"].cores())

    def pair_copy(half):
        to = 2 * half + s // 2
        return to, pltpu.make_async_remote_copy(
            src_ref=pair_low.at[half], dst_ref=pair_got.at[s % 2],
            send_sem=state_sends.at[20 + half], recv_sem=state_recvs.at[20 + s % 2],
            device_id=(to, d), device_id_type=MESH,
        )

    def send_pair():
        wait(homes["pair"].along())
        total = homes["pair"].total().astype(BF)
        own = total.shape[1] // 2
        for half in range(2):
            pair_low[half] = total[:, half * own : (half + 1) * own]
            to, copy = pair_copy(half)

            @pl.when(to != s)
            def _(copy=copy):
                copy.start()

            @pl.when(to == s)
            def _(half=half):
                pair_got[s % 2] = pair_low[half]

    def finish_pair():
        for half in range(2):
            to, copy = pair_copy(half)

            @pl.when(to != s)
            def _(copy=copy):
                copy.wait_send()

        for j in range(2):
            source = 2 * (s % 2) + j

            @pl.when(source != s)
            def _(j=j):
                pltpu.make_async_remote_copy(
                    src_ref=pair_low.at[0], dst_ref=pair_got.at[j],
                    send_sem=state_sends.at[20], recv_sem=state_recvs.at[20 + j],
                    device_id=(s ^ 1, d), device_id_type=MESH,
                ).wait_recv()

        own = pair_got.shape[2]
        for j in range(2):
            pair_out[:, j * own : (j + 1) * own] = pair_got[j].astype(F32)

    def turn(t, extra=None):
        count = len(units)
        if 0 <= t - 1 < count:
            home = homes[units[t - 1]]
            wait(home.cores())
            home.add_cores()
            start(home.first())
        if t < count:
            make(units[t])
        if extra is not None:
            extra()
        if t + 1 < count:
            start(fetch(units[t + 1]))
        if 0 <= t - 2 < count:
            home = homes[units[t - 2]]
            wait(home.first())
            home.add_first()
            start(home.second())
        if 0 <= t - 3 < count:
            home = homes[units[t - 3]]
            wait(home.second())
            home.add_second()
            start(home.along())
        if 0 <= t - 4 < count:
            finish(units[t - 4])

    start(fetch(units[0]))
    greet()
    start(dqs)
    start(finals)

    def opening(wq, wo, wp, do):
        start([pltpu.make_async_copy(*one) for one in
               ((wq_hbm, wq, local.at[0]), (wo_hbm, wo, local.at[1]), (wp_hbm, wp, local.at[2]))])
        turn(0)
        turn(1, lambda: rest_of_states(wq, wo, wp, do))

    pl.run_scoped(
        opening, *[pltpu.VMEM(w.shape, BF) for w in (wq_hbm, wo_hbm, wp_hbm)],
        pltpu.VMEM(da1.shape, BF),
    )
    small_step(0)

    def second(blocks, kv, total):
        turn(2, lambda: pair_gradient(blocks, kv, total))

    pl.run_scoped(
        second,
        pltpu.VMEM((2, images.shape[1], images.shape[2]), BF),
        pltpu.VMEM(dkv.shape, BF),
        pltpu.VMEM((dkv.shape[2], images.shape[2]), F32),
    )

    def pair_over_z():
        wait(homes["pair"].cores())
        homes["pair"].add_cores()
        start(homes["pair"].along())

    small_step(1)
    turn(3, pair_over_z)
    small_step(2)
    turn(4)
    small_step(3)
    turn(5, send_pair)
    small_step(4)
    turn(6)
    small_step(5)
    turn(7, finish_pair)
    turn(8)
    turn(9)
    turn(10)
    wait(finals)
    wait(dxs)


def tail(operands, sections, dp, width, hidden, query_count, head_size):
    n = dp // 2
    rows = operands[2].shape[0]
    r, own, wide_own = width // dp, width // sections, hidden // sections
    images, dkv = operands[19], operands[20]
    feat = images.shape[2]
    lanes = operands[0].shape[2]
    pair_r, pair_w = feat // dp, 2 * own

    def buffers(w):
        return [
            pltpu.VMEM((sections, n, r, w), BF),
            pltpu.VMEM((2, n, r // 2, w), BF), pltpu.VMEM((2, n, r // 2, w), BF),
            pltpu.VMEM((n, r // 2, w), BF), pltpu.VMEM((n, r // 2, w), BF),
            pltpu.VMEM((n - 1, r, w), BF),
        ]

    results = [
        shape((sections, rows, lanes), BF), shape((sections, rows, lanes), BF),
        shape((8, width), F32),
        shape((r, wide_own), F32), shape((hidden // dp, own), F32),
        shape((r, 3 * own), F32), shape((r, own), F32),
        shape((r, wide_own), F32), shape((hidden // dp, own), F32),
        shape((r, own), F32), shape((r, own), F32),
        shape((r, 3 * own), F32), shape((r, own), F32),
        shape((pair_r, pair_w), F32),
    ]
    scratch = []
    for w in (4 * own,) * 6 + (2 * own,):
        scratch += buffers(w)
    scratch += [
        pltpu.VMEM((1, n, 2, pair_r, pair_w), BF), pltpu.VMEM((1, n, pair_r, pair_w), BF),
        pltpu.VMEM((n - 1, pair_r, pair_w), BF),
        pltpu.VMEM((2, pair_r, own), BF), pltpu.VMEM((2, pair_r, own), BF),
        pltpu.VMEM((sections, n, 2, r, 4 * own), BF),
        pltpu.SemaphoreType.DMA((8, 10)), pltpu.SemaphoreType.DMA((8, 10)),
        pltpu.VMEM((rows, width), BF), pltpu.VMEM((rows, hidden), BF),
        pltpu.VMEM((rows, width), BF), pltpu.VMEM((rows, width), BF),
        pltpu.SemaphoreType.DMA((8, 4)),
        pltpu.VMEM((sections, rows, lanes), BF),
        pltpu.VMEM((rows, width), BF), pltpu.VMEM((rows, width), BF),
        pltpu.VMEM((rows, 3 * width), BF), pltpu.VMEM((sections, rows, lanes), BF),
        pltpu.VMEM((8, 8, width), F32),
        pltpu.SemaphoreType.DMA((24,)), pltpu.SemaphoreType.DMA((24,)),
        pltpu.SemaphoreType.DMA((6,)),
    ]
    return pl.pallas_call(
        functools.partial(tail_kernel, query_count, head_size),
        out_shape=results,
        in_specs=[whole(pl.ANY)] * 24 + [whole()] * 7,
        out_specs=[whole(pl.ANY)] * 2 + [whole()] * 12,
        scratch_shapes=scratch,
        compiler_params=pltpu.CompilerParams(
            vmem_limit_bytes=LIMIT, collective_id=0, has_side_effects=True
        ),
    )(*operands)


def body(
    starting_learned_vectors,
    frozen_picture_vectors,
    texts_per_picture,
    early_triple_matrix,
    early_mixing_exit_matrix,
    picture_asker_matrix,
    picture_pair_matrix,
    picture_exit_matrix,
    early_widen_matrix,
    early_narrow_matrix,
    later_triple_matrix,
    later_mixing_exit_matrix,
    later_widen_matrix,
    later_narrow_matrix,
    standardizer_factors,
    picture_divisors,
    closing_cotangent,
):
    sections = lax.axis_size("section")
    dp = lax.axis_size("dp")
    me = lax.axis_index("section")
    item_count, query_count, width = starting_learned_vectors.shape
    heads = picture_divisors.shape[0]
    images, patches, feat = frozen_picture_vectors.shape
    own_items = item_count // sections
    rows = own_items * query_count
    own_heads = heads // sections
    head_size = width // heads
    own_width = width // sections
    wide = -(-own_width // 128) * 128
    padded = -(-patches // 16) * 16
    hidden = early_widen_matrix.shape[1]
    gains = standardizer_factors

    ends = jnp.cumsum(texts_per_picture[0])
    positions = jnp.arange(item_count, dtype=jnp.int32)
    image_of = jnp.sum((ends[None, :] <= positions[:, None]).astype(jnp.int32), axis=1)[None, :]
    clamped = jnp.clip(picture_divisors, 0.5, 2.0)
    scale_all = 1.0 / math.sqrt(head_size) / clamped
    scale = lax.dynamic_slice_in_dim(scale_all, me * own_heads, own_heads, 0)[None, :]

    def own_rows(value):
        part = lax.dynamic_slice_in_dim(value, me * own_items, own_items, 0)
        return part.reshape(rows, width)

    def heads_to_sections(blocks):
        return exchange(blocks)

    x0 = own_rows(starting_learned_vectors)
    h1, low1, n1, r1, joined1, mixed_self1, q_blocks = call(
        functools.partial(front_kernel, query_count, head_size),
        (
            shape((rows, width), F32),
            shape((rows, width), BF),
            shape((rows, width), F32),
            shape((rows, 1), F32),
            shape((rows, 3 * width), BF),
            shape((rows, width), BF),
            shape((sections, rows, wide), BF),
        ),
        x0, early_triple_matrix, early_mixing_exit_matrix, picture_asker_matrix, gains,
    )
    q = exchange(q_blocks).reshape(sections * rows, wide)

    gap = jnp.zeros((feat, wide - own_width), BF)
    w_pair = jnp.concatenate(
        [
            lax.dynamic_slice_in_dim(picture_pair_matrix, me * own_width, own_width, 1),
            gap,
            lax.dynamic_slice_in_dim(picture_pair_matrix, width + me * own_width, own_width, 1),
            gap,
        ],
        axis=1,
    )
    keyval = pl.pallas_call(
        keyval_kernel,
        out_shape=shape((images, padded, 2 * wide), BF),
        grid=(images,),
        in_specs=[
            pl.BlockSpec((1, patches, feat), lambda j: (j, 0, 0)),
            pl.BlockSpec((feat, 2 * wide), lambda j: (0, 0)),
        ],
        out_specs=pl.BlockSpec((1, padded, 2 * wide), lambda j: (j, 0, 0)),
        compiler_params=pltpu.CompilerParams(vmem_limit_bytes=LIMIT),
    )(frozen_picture_vectors, w_pair)

    static = (patches, own_heads, head_size, query_count)
    o = call(
        functools.partial(attend_image_kernel, *static, 4),
        shape((sections * rows, wide), BF),
        image_of, scale, q, keyval,
        in_specs=[whole(SMEM), whole(SMEM), whole(), whole()],
    )
    mixed1 = exchange(o.reshape(sections, rows, wide))

    def act(*dims, dtype=BF):
        return shape((rows,) + dims, dtype)

    weights = (
        picture_exit_matrix, early_widen_matrix, early_narrow_matrix, later_triple_matrix,
        later_mixing_exit_matrix, later_widen_matrix, later_narrow_matrix,
    )
    (
        final_blocks, low2, m1, du1, da3, low3, mixed2, djoined2, da4,
        low4, m2, du2, da5, mixed1_rows, da2, do_blocks, dz2, dg_mid,
    ) = call(
        functools.partial(middle_kernel, query_count, head_size),
        (
            shape((sections, rows, wide), BF),
            act(width), act(hidden), act(hidden), act(width),
            act(width), act(width), act(3 * width), act(width),
            act(width), act(hidden), act(hidden), act(width),
            act(width), act(width), shape((sections, rows, wide), BF), act(width, dtype=F32),
            shape((4, width), F32),
        ),
        h1, mixed1, own_rows(closing_cotangent), gains, *weights,
        in_specs=[whole()] * 4 + [whole(pl.ANY)] * len(weights),
        scratch=[pltpu.VMEM(w.shape, BF) for w in weights]
        + [pltpu.SemaphoreType.DMA((len(weights),))]
        + [pltpu.VMEM((rows, hidden), F32)] * 2
        + [pltpu.VMEM((rows, 3 * width), BF), pltpu.VMEM((rows, width), BF)]
        + [pltpu.VMEM((rows, width), F32), pltpu.VMEM((rows, 1), F32)] * 4,
    )

    do = exchange(do_blocks).reshape(sections * rows, wide)
    dq, dkv, temper_rows = call(
        functools.partial(attend_image_back_kernel, *static, 2),
        (
            shape((sections * rows, wide), BF),
            shape((images, padded, 2 * wide), BF),
            shape((own_heads * query_count, 1), F32),
        ),
        image_of, scale, q, do, keyval,
        in_specs=[whole(SMEM), whole(SMEM), whole(), whole(), whole()],
        scratch=[pltpu.VMEM((images, padded, 2 * wide), F32)],
    )
    def home_states(got):
        got = got.reshape(item_count, query_count, wide)
        return got[:, :, :own_width].astype(F32)

    interior = ((picture_divisors > 0.5) & (picture_divisors < 2.0)).astype(F32)
    temper_factor = (-scale_all / clamped) * interior
    dq_sent = dq.reshape(sections, rows, wide)
    if width // dp % 32 == 0 and feat // dp % 16 == 0:
        (
            final_got, dx_got, small, expand2, reduce2, project2, out2, expand1, reduce1,
            asker, image_out, project1, out1, pair_part,
        ) = tail(
            (
                final_blocks, dq_sent, low4, du2, da5, m2, low3, djoined2, mixed2, da4,
                low2, du1, da3, m1, low1, mixed1_rows, da2, x0, mixed_self1,
                frozen_picture_vectors, dkv, picture_asker_matrix, early_mixing_exit_matrix,
                early_triple_matrix, dz2, n1, r1, gains, joined1, dg_mid, temper_rows,
            ),
            sections, dp, width, hidden, query_count, head_size,
        )
        gains_grad = small[:5]
        temper_grad = small[5, :heads] * temper_factor
    else:
        dq_blocks = exchange(dq_sent)
        d_pair = pl.pallas_call(
            keyval_grad_kernel,
            out_shape=shape((feat, 2 * own_width), BF),
            grid=(images,),
            in_specs=[
                pl.BlockSpec((1, patches, feat), lambda j: (j, 0, 0)),
                pl.BlockSpec((1, padded, 2 * wide), lambda j: (j, 0, 0)),
            ],
            out_specs=pl.BlockSpec((feat, 2 * own_width), lambda j: (0, 0)),
            scratch_shapes=[pltpu.VMEM((2 * wide, feat), F32)],
            compiler_params=pltpu.CompilerParams(vmem_limit_bytes=LIMIT),
        )(frozen_picture_vectors, dkv)

        dq_rows, da1, djoined1, dx_blocks, dg0 = call(
            functools.partial(last_kernel, query_count, head_size),
            (
                act(width), act(width), act(3 * width),
                shape((sections, rows, wide), BF), shape((1, width), F32),
            ),
            dz2, dq_blocks, picture_asker_matrix, n1, r1, gains, early_mixing_exit_matrix, joined1,
            early_triple_matrix,
            scratch=[pltpu.VMEM((rows, width), BF)],
        )

        def block_unit(grad):
            parts, k, own = grad.shape
            return grad.reshape(parts, dp, k // dp, own)

        def pair_grad(x, dy, y, dz):
            own = (dy.shape[1] + dz.shape[1]) // sections
            return block_unit(
                call(pair_weight_kernel, shape((sections, x.shape[1], own), BF), x, dy, y, dz)
            )

        expand2 = home(block_unit(expand_grad(low4, du2, sections)))
        reduce2 = home(reduce_grad(da5, m2, sections, dp)).T
        self2 = home(pair_grad(low3, djoined2, mixed2, da4))
        expand1 = home(block_unit(expand_grad(low2, du1, sections)))
        reduce1 = home(reduce_grad(da3, m1, sections, dp)).T
        pair_block = line_sum(
            core_sum(d_pair.reshape(1, dp, feat // dp, 2 * own_width))[0]
        )
        image_units = home(pair_grad(low1, dq_rows, mixed1_rows, da2))
        self1 = home(pair_grad(x0, djoined1, mixed_self1, da1))
        third = 3 * own_width
        project2, out2 = self2[:, :third], self2[:, third:]
        project1, out1 = self1[:, :third], self1[:, third:]
        asker, image_out = image_units[:, :own_width], image_units[:, own_width:]

        pair_rows = pair_block.shape[0]
        half = sections // 2
        pair_halves = pair_block.astype(BF).reshape(pair_rows, 2, own_width).transpose(1, 0, 2)
        key_home, val_home = me // 2, half + me // 2
        sent = jnp.zeros((sections, pair_rows, own_width), BF)
        sent = lax.dynamic_update_index_in_dim(sent, pair_halves[0], key_home, 0)
        sent = lax.dynamic_update_index_in_dim(sent, pair_halves[1], val_home, 0)
        got = exchange(sent)
        first = (me % half) * 2
        pair_part = lax.dynamic_slice_in_dim(got, first, 2, 0)
        pair_part = pair_part.transpose(1, 0, 2).reshape(pair_rows, 2 * own_width).astype(F32)

        final_got, dx_got = exchange(final_blocks), exchange(dx_blocks)
        d_temper = jnp.sum(temper_rows.reshape(own_heads, query_count), axis=1)
        spread = jnp.zeros((heads,), F32)
        spread = lax.dynamic_update_slice_in_dim(spread, d_temper, me * own_heads, 0)
        small = all_sum(jnp.concatenate([dg0.reshape(-1), dg_mid.reshape(-1), spread]))
        gains_grad = small[: 5 * width].reshape(5, width)
        temper_grad = small[5 * width :] * temper_factor

    final_part = home_states(final_got)
    grad_part = home_states(dx_got)

    def f(block):
        return block.astype(F32)

    return (
        final_part,
        grad_part,
        f(project1),
        f(out1),
        f(asker),
        pair_part,
        f(image_out),
        f(expand1),
        f(reduce1),
        f(project2),
        f(out2),
        f(expand2),
        f(reduce2),
        gains_grad,
        temper_grad,
    )


def solution(mesh):
    return jax.shard_map(
        body,
        mesh=mesh,
        in_specs=(P("dp", None, None), P("dp", None, None), P("dp", None))
        + (P(),) * 13
        + (P("dp", None, None),),
        out_specs=(P("dp", None, "section"),) * 2 + (P("dp", "section"),) * 11 + (P(), P()),
        check_vma=False,
    )
```

```python
import functools
import math

import jax
import jax.numpy as jnp
from jax import lax
from jax.experimental import pallas as pl
from jax.experimental.pallas import tpu as pltpu
from jax.sharding import PartitionSpec as P

EPSILON = 1e-06
BF = jnp.bfloat16
F32 = jnp.float32


def mm(left, right):
    return jnp.dot(left, right, preferred_element_type=F32)


def mm_tn(left, right):
    return lax.dot_general(left, right, (((0,), (0,)), ((), ())), preferred_element_type=F32)


def mm_nt(left, right):
    return lax.dot_general(left, right, (((1,), (1,)), ((), ())), preferred_element_type=F32)


def layer_norm(z, gain):
    centred = z - jnp.mean(z, axis=-1, keepdims=True)
    inverse = lax.rsqrt(jnp.mean(centred * centred, axis=-1, keepdims=True) + EPSILON)
    normed = centred * inverse
    return normed * gain, normed, inverse


def norm_back(dout, gain, normed, inverse):
    dn = dout * gain
    dgain = jnp.sum(dout * normed, axis=0)
    dz = inverse * (
        dn
        - jnp.mean(dn, axis=-1, keepdims=True)
        - normed * jnp.mean(dn * normed, axis=-1, keepdims=True)
    )
    return dz, dgain


def gelu_both(u):
    x = jnp.abs(u) * (0.5**0.5)
    e = jnp.exp(-0.5 * u * u)
    s = 1.0 / (1.0 + 0.3275911 * x)
    poly = s * (
        0.254829592
        + s * (-0.284496736 + s * (1.421413741 + s * (-1.453152027 + s * 1.061405429)))
    )
    tail = 0.5 * poly * e
    cdf = jnp.where(u < 0.0, tail, 1.0 - tail)
    return u * cdf, cdf + u * e * (1.0 / math.sqrt(2.0 * math.pi))


def swap(value, axis, bit):
    size = lax.axis_size(axis)
    return lax.ppermute(value, axis, [(i, i ^ bit) for i in range(size)])


def pick(value, index, axis):
    return lax.dynamic_index_in_dim(value, index, axis, keepdims=False)


def add_low(left, right):
    return (left.astype(F32) + right.astype(F32)).astype(BF)


def section_blocks(value):
    rows, width = value.shape
    parts = lax.axis_size("section")
    return value.reshape(rows, parts, width // parts).transpose(1, 0, 2)


def exchange(blocks):
    me = lax.axis_index("section")
    parts = lax.axis_size("section")
    out = blocks
    for bit in range(1, parts):
        got = swap(pick(blocks, me ^ bit, 0), "section", bit)
        out = lax.dynamic_update_index_in_dim(out, got, me ^ bit, 0)
    return out


def cols_to_section(value):
    return exchange(section_blocks(value))


def rows_from_section(blocks):
    got = exchange(blocks)
    parts, rows, width = got.shape
    return got.transpose(1, 0, 2).reshape(rows, parts * width)


def line_sum(blocks):
    n = blocks.shape[0]
    p = lax.axis_index("dp") // 2
    size = lax.axis_size("dp")
    kept = blocks
    for k in range(n - 1):
        up_at = jnp.clip(n - 1 - k + p, 0, n - 1)
        down_at = jnp.clip(p - (n - 1 - k), 0, n - 1)
        up_pairs = [(2 * q + c, 2 * q + 2 + c) for q in range(min(k, n - 2) + 1) for c in (0, 1)]
        down_pairs = [
            (2 * q + c, 2 * q - 2 + c) for q in range(max(n - 1 - k, 1), n) for c in (0, 1)
        ]
        up = lax.ppermute(pick(kept, up_at, 0), "dp", up_pairs)
        down = lax.ppermute(pick(kept, down_at, 0), "dp", down_pairs)
        up_to = jnp.clip(n - 2 - k + p, 0, n - 1)
        down_to = jnp.clip(p + 1 - (n - 1 - k), 0, n - 1)
        kept = lax.dynamic_update_index_in_dim(kept, add_low(pick(kept, up_to, 0), up), up_to, 0)
        kept = lax.dynamic_update_index_in_dim(
            kept, add_low(pick(kept, down_to, 0), down), down_to, 0
        )
    del size
    return pick(kept, p, 0)


def core_sum(unit):
    parts, dp, r, w = unit.shape
    c = lax.axis_index("dp") % 2
    pairs = unit.reshape(parts, dp // 2, 2, r, w)
    return add_low(pick(pairs, c, 2), swap(pick(pairs, 1 - c, 2), "dp", 1))


def plane_sum(unit):
    parts, n, r, w = unit.shape
    me = lax.axis_index("section")
    low, high = me % 2, me // 2
    square = unit.reshape(2, 2, n, r, w)
    a, b = square[:, :, :, : r // 2], square[:, :, :, r // 2 :]
    a = add_low(pick(a, low, 1), swap(pick(a, 1 - low, 1), "section", 1))
    b = add_low(pick(b, high, 0), swap(pick(b, 1 - high, 0), "section", 2))
    a = add_low(pick(a, high, 0), swap(pick(a, 1 - high, 0), "section", 2))
    b = add_low(pick(b, low, 0), swap(pick(b, 1 - low, 0), "section", 1))
    return jnp.concatenate([a, b], axis=1)


def home(unit):
    return line_sum(plane_sum(core_sum(unit)))


def unit_of(grad, dp, sections):
    rows, cols = grad.shape
    return (
        grad.astype(BF)
        .reshape(dp, rows // dp, sections, cols // sections)
        .transpose(2, 0, 1, 3)
    )


def all_sum(value):
    for axis in ("dp", "section"):
        bit = 1
        while bit < lax.axis_size(axis):
            value = value + swap(value, axis, bit)
            bit *= 2
    return value


VMEM = pltpu.MemorySpace.VMEM
SMEM = pltpu.MemorySpace.SMEM
LIMIT = 60 * 1024 * 1024
GROUP = 128


def whole(space=VMEM):
    return pl.BlockSpec(memory_space=space)


def head_lanes(shape, head, head_size):
    return lax.broadcasted_iota(jnp.int32, shape, len(shape) - 1) // head_size == head


def same_item(query_count):
    shape = (GROUP, GROUP)
    left = lax.broadcasted_iota(jnp.int32, shape, 0) // query_count
    right = lax.broadcasted_iota(jnp.int32, shape, 1) // query_count
    return left == right


def soft(t, mask, scale):
    t = jnp.where(mask, t * scale, -1e30)
    e = jnp.exp(t - jnp.max(t, axis=-1, keepdims=True))
    return e / jnp.sum(e, axis=-1, keepdims=True)


def masked(value, head, head_size):
    return jnp.where(head_lanes(value.shape, head, head_size), value, jnp.zeros_like(value))


def attend_self(joined_ref, mixed_ref, query_count, head_size):
    rows, width = mixed_ref.shape
    pair = 2 * head_size
    scale = 1.0 / math.sqrt(head_size)
    mask = same_item(query_count)

    def step(i, _):
        col = pl.multiple_of(i * pair, pair)
        for g in range(rows // GROUP):
            at = pl.ds(g * GROUP, GROUP)
            q = joined_ref[at, pl.ds(col, pair)]
            k = joined_ref[at, pl.ds(width + col, pair)]
            v = joined_ref[at, pl.ds(2 * width + col, pair)]
            o = jnp.zeros((GROUP, pair), F32)
            for h in range(2):
                p = soft(mm_nt(masked(q, h, head_size), k), mask, scale).astype(BF)
                o = o + mm(p, masked(v, h, head_size))
            mixed_ref[at, pl.ds(col, pair)] = o.astype(BF)
        return 0

    lax.fori_loop(0, width // pair, step, 0)


def attend_self_back(joined_ref, do_ref, djoined_ref, query_count, head_size):
    rows, width = do_ref.shape
    pair = 2 * head_size
    scale = 1.0 / math.sqrt(head_size)
    mask = same_item(query_count)

    def step(i, _):
        col = pl.multiple_of(i * pair, pair)
        for g in range(rows // GROUP):
            at = pl.ds(g * GROUP, GROUP)
            q = joined_ref[at, pl.ds(col, pair)]
            k = joined_ref[at, pl.ds(width + col, pair)]
            v = joined_ref[at, pl.ds(2 * width + col, pair)]
            do = do_ref[at, pl.ds(col, pair)]
            dq = jnp.zeros((GROUP, pair), F32)
            dk = jnp.zeros((GROUP, pair), F32)
            dv = jnp.zeros((GROUP, pair), F32)
            for h in range(2):
                qh, kh = masked(q, h, head_size), masked(k, h, head_size)
                doh = masked(do, h, head_size)
                p = soft(mm_nt(qh, k), mask, scale)
                dp = mm_nt(doh, v)
                ds = p * (dp - jnp.sum(p * dp, axis=-1, keepdims=True))
                dt = (ds * scale).astype(BF)
                dv = dv + mm_tn(p.astype(BF), doh)
                dq = dq + mm(dt, kh)
                dk = dk + mm_tn(dt, qh)
            djoined_ref[at, pl.ds(col, pair)] = dq.astype(BF)
            djoined_ref[at, pl.ds(width + col, pair)] = dk.astype(BF)
            djoined_ref[at, pl.ds(2 * width + col, pair)] = dv.astype(BF)
        return 0

    lax.fori_loop(0, width // pair, step, 0)


def project_into(out_ref, low, w_ref, block=768):
    for at in range(0, w_ref.shape[1], block):
        out_ref[:, at : at + block] = mm(low, w_ref[:, at : at + block]).astype(BF)


def back_through(dy_ref, w_ref, block=768):
    total = None
    for at in range(0, w_ref.shape[1], block):
        term = mm_nt(dy_ref[:, at : at + block], w_ref[:, at : at + block])
        total = term if total is None else total + term
    return total


def hidden_forward(low, w_expand_ref, w_reduce_ref, m_ref, slope_ref, block=512):
    total = None
    for at in range(0, w_expand_ref.shape[1], block):
        u = mm(low, w_expand_ref[:, at : at + block]).astype(BF).astype(F32)
        m, slope = gelu_both(u)
        m = m.astype(BF)
        m_ref[:, at : at + block] = m
        slope_ref[:, at : at + block] = slope
        term = mm(m, w_reduce_ref[at : at + block, :])
        total = term if total is None else total + term
    return total


def hidden_backward(da, w_expand_ref, w_reduce_ref, slope_ref, du_ref, block=512):
    total = None
    for at in range(0, w_expand_ref.shape[1], block):
        dm = mm_nt(da, w_reduce_ref[at : at + block, :])
        du = (dm * slope_ref[:, at : at + block]).astype(BF)
        du_ref[:, at : at + block] = du
        term = mm_nt(du, w_expand_ref[:, at : at + block])
        total = term if total is None else total + term
    return total


def norm_into(z, gain, n_ref, r_ref):
    out, n, r = layer_norm(z, gain)
    n_ref[...] = n
    r_ref[...] = r
    return out


def window(t, own):
    low = t * own // 128 * 128
    return low, t * own - low


def put_blocks(out_ref, value):
    parts, _, wide = out_ref.shape
    own = value.shape[1] // parts
    for t in range(parts):
        low, _ = window(t, own)
        out_ref[t] = value[:, low : low + wide]


def take_blocks(in_ref, own):
    parts, _, wide = in_ref.shape
    pieces = []
    for low in range(0, parts * own, 128):
        piece = None
        for t in range(parts):
            first, _ = window(t, own)
            if first <= low < first + wide:
                part = in_ref[t, :, low - first : low - first + 128]
                piece = part if piece is None else piece + part
        pieces.append(piece)
    return jnp.concatenate(pieces, axis=1)


MESH = pl.DeviceIdType.MESH


def start(copies):
    for copy in copies:
        copy.start()


def wait(copies):
    for copy in copies:
        copy.wait()


def exchange_copies(source, target, sends, recvs):
    s, d = lax.axis_index("section"), lax.axis_index("dp")
    out = []
    for bit in range(1, lax.axis_size("section")):
        to = s ^ bit
        out.append(pltpu.make_async_remote_copy(
            src_ref=source.at[to], dst_ref=target.at[s], send_sem=sends.at[bit],
            recv_sem=recvs.at[bit], device_id=(to, d), device_id_type=MESH,
        ))
    out.append(pltpu.make_async_copy(source.at[s], target.at[s], sends.at[0]))
    return out


def greet_sections():
    s, d = lax.axis_index("section"), lax.axis_index("dp")
    barrier = pltpu.get_barrier_semaphore()
    parts = lax.axis_size("section")
    for bit in range(1, parts):
        pl.semaphore_signal(barrier, inc=1, device_id=(s ^ bit, d), device_id_type=MESH)
    pl.semaphore_wait(barrier, parts - 1)


def owner_copies(source, target, kind, which, sends, recvs):
    s, d = lax.axis_index("section"), lax.axis_index("dp")
    out = []
    for i in range(2):
        to = 2 * which + i
        out.append((to != s, pltpu.make_async_remote_copy(
            src_ref=source, dst_ref=target.at[s], send_sem=sends.at[kind, which, i],
            recv_sem=recvs.at[kind, s], device_id=(to, d), device_id_type=MESH,
        )))
        out.append((to == s, pltpu.make_async_copy(source, target.at[s], sends.at[kind, which, i])))
    return out


def start_if(pairs):
    for condition, copy in pairs:
        pl.when(condition)(copy.start)


def sent_if(pairs):
    for remote, local in zip(pairs[::2], pairs[1::2]):
        pl.when(remote[0])(remote[1].wait_send)
        pl.when(local[0])(local[1].wait)


def received(target, kind, sends, recvs):
    s, d = lax.axis_index("section"), lax.axis_index("dp")
    for t in range(lax.axis_size("section")):
        copy = pltpu.make_async_remote_copy(
            src_ref=target.at[t], dst_ref=target.at[t], send_sem=sends.at[kind, 0, 0],
            recv_sem=recvs.at[kind, t], device_id=(s ^ 1, d), device_id_type=MESH,
        )
        pl.when(t != s)(copy.wait_recv)


def front_kernel(
    query_count, head_size, own_heads,
    texts_ref, divisor_ref, g_ref, x_hbm, images_hbm, wp_hbm, wo_hbm, wq_hbm, pair_hbm,
    x_ref, h_ref, low_ref, n_ref, r_ref, joined_ref, mixed_ref, q_got, kv_ref, mixed1_ref,
    x_in, wp, wo, wq, w_pair, blocks, q_blocks, o_blocks, o_got,
    loads, image_sems, q_sends, q_recvs, o_sends, o_recvs,
):
    s, d = lax.axis_index("section"), lax.axis_index("dp")
    parts, rows, wide = q_got.shape
    images, patches, feat = images_hbm.shape
    width = x_ref.shape[1]
    own = width // parts
    items = x_in.shape[0]
    low_at = pl.multiple_of(s * own // 128 * 128, 128)
    copies = [
        pltpu.make_async_copy(source, target, loads.at[i])
        for i, (source, target) in enumerate((
            (x_hbm.at[pl.ds(s * items, items)], x_in),
            (wp_hbm, wp), (wo_hbm, wo), (wq_hbm, wq),
            (pair_hbm.at[:, pl.ds(low_at, wide)], w_pair.at[:, :wide]),
            (pair_hbm.at[:, pl.ds(pl.multiple_of(width + low_at, 128), wide)], w_pair.at[:, wide:]),
        ))
    ]
    start(copies)

    def image(j):
        return pltpu.make_async_copy(images_hbm.at[j], blocks.at[j % 2], image_sems.at[j % 2])

    image(0).start()
    greet_sections()
    copies[0].wait()
    x_ref[...] = x_in[...].reshape(rows, width)
    copies[1].wait()
    project_into(joined_ref, x_ref[...], wp)
    attend_self(joined_ref, mixed_ref, query_count, head_size)
    copies[2].wait()
    z = x_ref[...].astype(F32) + mm(mixed_ref[...], wo[...])
    h = norm_into(z, g_ref[0:1, :], n_ref, r_ref)
    h_ref[...] = h
    low_ref[...] = h.astype(BF)
    copies[3].wait()
    put_blocks(q_blocks, mm(low_ref[...], wq[...]).astype(BF))
    q_copies = exchange_copies(q_blocks, q_got, q_sends, q_recvs)
    start(q_copies)

    copies[4].wait()
    copies[5].wait()
    padded = kv_ref.shape[1]
    full = patches // 16 * 16
    for j in range(images):
        image(j).wait()
        if j + 1 < images:
            image(j + 1).start()
        kv_ref[j, full:, :] = jnp.zeros((padded - full, kv_ref.shape[2]), BF)
        kv_ref[j, :patches, :] = mm(blocks[j % 2], w_pair[...]).astype(BF)

    scales = row_scales(divisor_ref, own_heads, head_size, query_count)
    shift = s * own % 128 // head_size
    ends = caption_ends(texts_ref)
    together = 4

    for copy in q_copies[:-1]:
        copy.wait()
    q_copies[-1].wait()
    o_copies = []
    for bit in (1, 2, 3, 0):
        t = s ^ bit

        def step(i, _, t=t):
            for b in range(together):
                item = i * together + b
                at = pl.ds(pl.multiple_of(item * query_count, query_count), query_count)
                j = image_at(ends, t * items + item)
                o_blocks[t, at, :] = attend_image(
                    q_got[t, at, :], kv_ref, j, patches, scales, own_heads, head_size, shift
                )
            return 0

        lax.fori_loop(0, items // together, step, 0)
        if bit:
            copy = pltpu.make_async_remote_copy(
                src_ref=o_blocks.at[t], dst_ref=o_got.at[s], send_sem=o_sends.at[bit],
                recv_sem=o_recvs.at[bit], device_id=(t, d), device_id_type=MESH,
            )
        else:
            copy = pltpu.make_async_copy(o_blocks.at[t], o_got.at[t], o_sends.at[0])
        copy.start()
        o_copies.append(copy)
    wait(o_copies)
    mixed1_ref[...] = take_blocks(o_got, own)


def stacked(value, own_heads, head_size, shift):
    return jnp.concatenate(
        [masked(value, h + shift, head_size) for h in range(own_heads)], axis=0
    )


def unstacked(value, own_heads, head_size, shift):
    rows = value.shape[0] // own_heads
    total = None
    for h in range(own_heads):
        part = masked(value[h * rows : (h + 1) * rows], h + shift, head_size)
        total = part if total is None else total + part
    return total


def row_scales(divisor_ref, own_heads, head_size, query_count):
    first = lax.axis_index("section") * own_heads
    divisors = jnp.concatenate(
        [jnp.full((query_count, 1), divisor_ref[first + h], F32) for h in range(own_heads)], axis=0
    )
    return 1.0 / math.sqrt(head_size) / jnp.clip(divisors, 0.5, 2.0)


def caption_ends(texts_ref):
    ends, total = [], 0
    for j in range(texts_ref.shape[1]):
        total = total + texts_ref[0, j]
        ends.append(total)
    return ends


def image_at(ends, item):
    j = 0
    for end in ends:
        j = j + jnp.where(end <= item, 1, 0)
    return jnp.minimum(j, len(ends) - 1)


def image_soft(q, k, k_last, scales):
    t = mm_nt(q, k)
    t_last = jnp.sum(q.astype(F32) * k_last.astype(F32), axis=-1, keepdims=True)
    s, s_last = t * scales, t_last * scales
    top = jnp.maximum(jnp.max(s, axis=-1, keepdims=True), s_last)
    e, e_last = jnp.exp(s - top), jnp.exp(s_last - top)
    total = jnp.sum(e, axis=-1, keepdims=True) + e_last
    return t, t_last, e / total, e_last / total


def attend_image(q, kv_ref, j, patches, scales, own_heads, head_size, shift):
    wide = q.shape[1]
    last = patches - 1
    q = stacked(q, own_heads, head_size, shift)
    _, _, p, p_last = image_soft(
        q, kv_ref[j, :last, :wide], kv_ref[j, last : last + 1, :wide], scales
    )
    v_last = kv_ref[j, last : last + 1, wide:].astype(F32)
    o = mm(p.astype(BF), kv_ref[j, :last, wide:]) + p_last.astype(BF).astype(F32) * v_last
    return unstacked(o, own_heads, head_size, shift).astype(BF)


def attend_image_back_kernel(
    patches, own_heads, head_size, query_count, together,
    texts_ref, divisor_ref, q_ref, do_ref, kv_ref, dq_ref, dkv_ref, temper_ref, total_ref,
):
    wide = q_ref.shape[1]
    items = q_ref.shape[0] // query_count
    last = patches - 1
    scales = row_scales(divisor_ref, own_heads, head_size, query_count)
    shift = lax.axis_index("section") * own_heads * head_size % 128 // head_size
    ends = caption_ends(texts_ref)
    total_ref[...] = jnp.zeros_like(total_ref)
    temper_ref[...] = jnp.zeros_like(temper_ref)

    def step(i, _):
        temper = None
        for b in range(together):
            item = i * together + b
            at = pl.ds(pl.multiple_of(item * query_count, query_count), query_count)
            j = image_at(ends, item)
            q = stacked(q_ref[at, :], own_heads, head_size, shift)
            do = stacked(do_ref[at, :], own_heads, head_size, shift)
            k, v = kv_ref[j, :last, :wide], kv_ref[j, :last, wide:]
            k_last = kv_ref[j, last : last + 1, :wide].astype(F32)
            v_last = kv_ref[j, last : last + 1, wide:].astype(F32)
            t, t_last, p, p_last = image_soft(q, k, k_last, scales)
            dp = mm_nt(do, v)
            dp_last = jnp.sum(do.astype(F32) * v_last, axis=-1, keepdims=True)
            mean = jnp.sum(p * dp, axis=-1, keepdims=True) + p_last * dp_last
            ds, ds_last = p * (dp - mean), p_last * (dp_last - mean)
            term = jnp.sum(ds * t, axis=-1, keepdims=True) + ds_last * t_last
            temper = term if temper is None else temper + term
            dt = (ds * scales).astype(BF)
            dt_last = (ds_last * scales).astype(BF).astype(F32)
            dq = mm(dt, k) + dt_last * k_last
            dq_ref[at, :] = unstacked(dq, own_heads, head_size, shift).astype(BF)
            total_ref[j, :last, :wide] += mm_tn(dt, q)
            total_ref[j, :last, wide:] += mm_tn(p.astype(BF), do)
            total_ref[j, last : last + 1, :wide] += jnp.sum(
                dt_last * q.astype(F32), axis=0, keepdims=True
            )
            total_ref[j, last : last + 1, wide:] += jnp.sum(
                p_last.astype(BF).astype(F32) * do.astype(F32), axis=0, keepdims=True
            )
        temper_ref[...] += temper
        return 0

    lax.fori_loop(0, items // together, step, 0)
    dkv_ref[...] = total_ref[...].astype(BF)


def pair_columns(total_ref, own):
    s = lax.axis_index("section")
    shift = s * own % 128
    halves = []
    for half in range(2):
        base = half * (total_ref.shape[0] // 2)
        out = total_ref[base : base + own, :]
        for offset in sorted({window(t, own)[1] for t in range(4)} - {0}):
            out = jnp.where(
                shift == offset, total_ref[base + offset : base + offset + own, :], out
            )
        halves.append(out.T.astype(BF))
    return jnp.concatenate(halves, axis=1)


def keyval_grad_kernel(x_ref, dkv_ref, out_ref, total_ref):
    @pl.when(pl.program_id(0) == 0)
    def _():
        total_ref[...] = jnp.zeros_like(total_ref)

    patches = x_ref.shape[1]
    total_ref[...] += mm_tn(dkv_ref[0, :patches, :], x_ref[0])

    @pl.when(pl.program_id(0) == pl.num_programs(0) - 1)
    def _():
        out_ref[...] = pair_columns(total_ref, out_ref.shape[1] // 2)


def middle_kernel(query_count, head_size, owners, *refs):
    refs = list(refs)

    def take(count):
        out = refs[:count]
        del refs[:count]
        return out

    h1_ref, mixed1_ref, g_ref, dout_hbm = take(4)
    hbm_weights = take(7)
    final_got, do_got, low3_ref, mixed2_ref, djoined_ref, da4_ref, da2_ref, dz2_ref, dg_ref = take(9)
    if owners:
        x_got, da_got = take(2)
    low2_ref, m1_ref, du1_ref, da3_ref, low4_ref, m2_ref, du2_ref, da5_ref = take(8)
    weights = take(7)
    wx, we1, wr1, wp, wo, we2, wr2 = weights
    dout, final_blocks, do_blocks, sems, sends, recvs, owner_sends, owner_recvs = take(8)
    slope1, slope2, joined, do2, n2, r2, n3, r3, n4, r4, n5, r5 = refs
    given = []

    def give(source, kind, which):
        if owners:
            target = (x_got, da_got)[kind]
            pairs = owner_copies(source, target, kind, which, owner_sends, owner_recvs)
            start_if(pairs)
            given.append(pairs)

    copies = [
        pltpu.make_async_copy(src, dst, sems.at[i])
        for i, (src, dst) in enumerate(zip(hbm_weights, weights))
    ]
    for copy in copies:
        copy.start()
    items = dout.shape[0]
    dout_copy = pltpu.make_async_copy(
        dout_hbm.at[pl.ds(lax.axis_index("section") * items, items)], dout, sems.at[len(copies)]
    )
    dout_copy.start()
    finals = exchange_copies(
        final_blocks, final_got, sends.at[pl.ds(0, 4)], recvs.at[pl.ds(0, 4)]
    )
    dos = exchange_copies(do_blocks, do_got, sends.at[pl.ds(4, 4)], recvs.at[pl.ds(4, 4)])
    greet_sections()
    copies[0].wait()
    h2 = norm_into(h1_ref[...] + mm(mixed1_ref[...], wx[...]), g_ref[1:2, :], n2, r2)
    low2_ref[...] = h2.astype(BF)
    give(low2_ref, 0, 0)
    copies[1].wait()
    copies[2].wait()
    a = hidden_forward(low2_ref[...], we1, wr1, m1_ref, slope1)
    h3 = norm_into(n2[...] * g_ref[1:2, :] + a, g_ref[2:3, :], n3, r3)
    low3_ref[...] = h3.astype(BF)
    copies[3].wait()
    project_into(joined, low3_ref[...], wp)
    attend_self(joined, mixed2_ref, query_count, head_size)
    copies[4].wait()
    a = mm(mixed2_ref[...], wo[...])
    h4 = norm_into(n3[...] * g_ref[2:3, :] + a, g_ref[3:4, :], n4, r4)
    low4_ref[...] = h4.astype(BF)
    give(low4_ref, 0, 1)
    copies[5].wait()
    copies[6].wait()
    a = hidden_forward(low4_ref[...], we2, wr2, m2_ref, slope2)
    h5 = norm_into(n4[...] * g_ref[3:4, :] + a, g_ref[4:5, :], n5, r5)
    put_blocks(final_blocks, h5.astype(BF))
    start(finals)
    dout_copy.wait()

    dz, dg4 = norm_back(
        dout[...].reshape(n5.shape).astype(F32), g_ref[4:5, :], n5[...], r5[...]
    )
    da5_ref[...] = dz.astype(BF)
    give(da5_ref, 1, 1)
    d4 = dz + hidden_backward(da5_ref[...], we2, wr2, slope2, du2_ref)

    dz, dg3 = norm_back(d4, g_ref[3:4, :], n4[...], r4[...])
    da4_ref[...] = dz.astype(BF)
    do2[...] = mm_nt(da4_ref[...], wo[...]).astype(BF)
    attend_self_back(joined, do2, djoined_ref, query_count, head_size)
    d3 = dz + back_through(djoined_ref, wp)

    dz, dg2 = norm_back(d3, g_ref[2:3, :], n3[...], r3[...])
    da3_ref[...] = dz.astype(BF)
    give(da3_ref, 1, 0)
    d2 = dz + hidden_backward(da3_ref[...], we1, wr1, slope1, du1_ref)

    dz, dg1 = norm_back(d2, g_ref[1:2, :], n2[...], r2[...])
    dz2_ref[...] = dz
    da2_ref[...] = dz.astype(BF)
    put_blocks(do_blocks, mm_nt(da2_ref[...], wx[...]).astype(BF))
    start(dos)
    dg_ref[...] = jnp.concatenate([d[None, :] for d in (dg1, dg2, dg3, dg4)], axis=0)
    for pairs in given:
        sent_if(pairs)
    if owners:
        received(x_got, 0, owner_sends, owner_recvs)
        received(da_got, 1, owner_sends, owner_recvs)
    wait(finals)
    wait(dos)


def last_kernel(
    query_count, head_size, dz2_ref, dq_ref, wq_ref, n_ref, r_ref, g_ref, wo_ref, joined_ref, wp_ref,
    dqr_ref, da_ref, djoined_ref, dx_ref, dg_ref, do,
):
    own = wq_ref.shape[1] // dq_ref.shape[0]
    dqr_ref[...] = take_blocks(dq_ref, own)
    d1 = dz2_ref[...] + mm_nt(dqr_ref[...], wq_ref[...])
    dz, dg = norm_back(d1, g_ref[0:1, :], n_ref[...], r_ref[...])
    dg_ref[...] = dg[None, :]
    da_ref[...] = dz.astype(BF)
    do[...] = mm_nt(da_ref[...], wo_ref[...]).astype(BF)
    attend_self_back(joined_ref, do, djoined_ref, query_count, head_size)
    put_blocks(dx_ref, (dz + back_through(djoined_ref, wp_ref)).astype(BF))


def weight_kernel(x_ref, dy_ref, out_ref):
    out_ref[0] = mm_tn(x_ref[...], dy_ref[...]).astype(BF)


def pair_weight_kernel(x_ref, dy_ref, y_ref, dz_ref, out_ref):
    parts = out_ref.shape[0]
    own_a, own_b = dy_ref.shape[1] // parts, dz_ref.shape[1] // parts
    for t in range(parts):
        a = mm_tn(x_ref[...], dy_ref[:, t * own_a : (t + 1) * own_a]).astype(BF)
        b = mm_tn(y_ref[...], dz_ref[:, t * own_b : (t + 1) * own_b]).astype(BF)
        out_ref[t] = jnp.concatenate([a, b], axis=1)


def turned_weight_kernel(dy_ref, x_ref, out_ref):
    _, dp, own, wide = out_ref.shape
    r = mm_tn(dy_ref[...], x_ref[...]).astype(BF)
    for d in range(dp):
        out_ref[0, d] = r[:, d * wide : (d + 1) * wide]


def shape(dims, dtype):
    return jax.ShapeDtypeStruct(tuple(dims), dtype)


def call(kernel, outs, *args, in_specs=None, scratch=(), flops=0):
    return pl.pallas_call(
        kernel,
        out_shape=outs,
        in_specs=in_specs or [whole()] * len(args),
        out_specs=jax.tree.map(lambda _: whole(), outs),
        scratch_shapes=list(scratch),
        compiler_params=pltpu.CompilerParams(vmem_limit_bytes=LIMIT),
        cost_estimate=pl.CostEstimate(
            flops=flops, bytes_accessed=int(flops) // 400, transcendentals=0
        ),
    )(*args)


def expand_grad(low, du, parts):
    rows, width = low.shape
    own = du.shape[1] // parts
    return pl.pallas_call(
        weight_kernel,
        out_shape=shape((parts, width, own), BF),
        grid=(parts,),
        in_specs=[
            pl.BlockSpec((rows, width), lambda t: (0, 0)),
            pl.BlockSpec((rows, own), lambda t: (0, t)),
        ],
        out_specs=pl.BlockSpec((1, width, own), lambda t: (t, 0, 0)),
        compiler_params=pltpu.CompilerParams(vmem_limit_bytes=LIMIT),
    )(low, du)


def reduce_grad(da, m, parts, dp):
    rows, width = da.shape
    wide = m.shape[1] // dp
    own = width // parts
    per = 4 if dp % 4 == 0 and (dp // 4 * wide) % 128 == 0 else 1
    blocks = dp // per
    return pl.pallas_call(
        functools.partial(turned_weight_all_kernel, parts),
        out_shape=shape((parts, dp, own, wide), BF),
        grid=(per,),
        in_specs=[
            pl.BlockSpec((rows, width), lambda b: (0, 0)),
            pl.BlockSpec((rows, blocks * wide), lambda b: (0, b)),
        ],
        out_specs=pl.BlockSpec((parts, blocks, own, wide), lambda b: (0, b, 0, 0)),
        compiler_params=pltpu.CompilerParams(vmem_limit_bytes=LIMIT),
    )(da, m)


def turned_weight_all_kernel(parts, dy_ref, x_ref, out_ref):
    _, blocks, own, wide = out_ref.shape
    r = mm_tn(dy_ref[...], x_ref[...]).astype(BF)
    for t in range(parts):
        for d in range(blocks):
            out_ref[t, d] = r[t * own : (t + 1) * own, d * wide : (d + 1) * wide]


def device_of(section, z, core):
    return (section, z * 2 + core)


class Home:
    def __init__(self, unit, kept, from_x, from_y, then_x, then_y, from_z, sends, recvs):
        self.unit, self.kept = unit, kept
        self.from_x, self.from_y = from_x, from_y
        self.then_x, self.then_y = then_x, then_y
        self.from_z = from_z
        self.sends, self.recvs = sends, recvs
        self.s, d = lax.axis_index("section"), lax.axis_index("dp")
        self.sx, self.sy = self.s % 2, self.s // 2
        self.z, self.c = d // 2, d % 2
        self.half = kept.shape[2] // 2

    def copy(self, i, src, dst, device):
        return pltpu.make_async_remote_copy(
            src_ref=src, dst_ref=dst, send_sem=self.sends.at[i], recv_sem=self.recvs.at[i],
            device_id=device, device_id_type=MESH,
        )

    def mine(self):
        return self.s if self.kept.shape[0] > 1 else 0

    def cores(self):
        return [
            self.copy(
                0, self.unit.at[:, :, 1 - self.c], self.kept, device_of(self.s, self.z, 1 - self.c)
            )
        ]

    def first(self):
        s, sx, sy, z, c, half = self.s, self.sx, self.sy, self.z, self.c, self.half
        out = []
        for i in range(2):
            out.append(self.copy(
                1 + i, self.kept.at[2 * i + 1 - sx, :, :half], self.from_x.at[i],
                device_of(s + 1 - 2 * sx, z, c),
            ))
            out.append(self.copy(
                3 + i, self.kept.at[2 * (1 - sy) + i, :, half:], self.from_y.at[i],
                device_of(s + 2 - 4 * sy, z, c),
            ))
        return out

    def second(self):
        s, sx, sy, z, c, half = self.s, self.sx, self.sy, self.z, self.c, self.half
        return [
            self.copy(
                5, self.kept.at[2 * (1 - sy) + sx, :, :half], self.then_y,
                device_of(s + 2 - 4 * sy, z, c),
            ),
            self.copy(
                6, self.kept.at[2 * sy + 1 - sx, :, half:], self.then_x,
                device_of(s + 1 - 2 * sx, z, c),
            ),
        ]

    def along(self):
        n = self.kept.shape[1]
        out = []
        for k in range(1, n):
            to = (self.z + k) % n
            out.append(self.copy(
                6 + k, self.kept.at[self.mine(), to], self.from_z.at[k - 1],
                device_of(self.s, to, self.c),
            ))
        return out

    def add_cores(self):
        n = self.kept.shape[1]

        def step(i, _):
            t, z = i // n, i % n
            self.kept[t, z] = self.kept[t, z] + self.unit[t, z, self.c]
            return 0

        lax.fori_loop(0, self.kept.shape[0] * n, step, 0)

    def add_first(self):
        n, half = self.kept.shape[1], self.half

        def step(i, _):
            t, z = i // n, i % n
            x, y = 2 * t + self.sx, 2 * self.sy + t
            self.kept[x, z, :half] = self.kept[x, z, :half] + self.from_x[t, z]
            self.kept[y, z, half:] = self.kept[y, z, half:] + self.from_y[t, z]
            return 0

        lax.fori_loop(0, 2 * n, step, 0)

    def add_second(self):
        n, half = self.kept.shape[1], self.half

        def step(z, _):
            self.kept[self.s, z, :half] = self.kept[self.s, z, :half] + self.then_y[z]
            self.kept[self.s, z, half:] = self.kept[self.s, z, half:] + self.then_x[z]
            return 0

        lax.fori_loop(0, n, step, 0)

    def total(self):
        total = self.kept[self.mine(), self.z].astype(F32)
        for k in range(self.from_z.shape[0]):
            total = total + self.from_z[k].astype(F32)
        return total


def greet():
    s, d = lax.axis_index("section"), lax.axis_index("dp")
    sections, dp = lax.axis_size("section"), lax.axis_size("dp")
    n = dp // 2
    z, c = d // 2, d % 2
    barrier = pltpu.get_barrier_semaphore()
    near = [device_of(s, z, 1 - c)]
    for bit in range(1, sections):
        near.append(device_of(s ^ bit, z, c))
    for k in range(1, n):
        near.append(device_of(s, (z + k) % n, c))
    for device in near:
        pl.semaphore_signal(barrier, inc=1, device_id=device, device_id_type=MESH)
    pl.semaphore_wait(barrier, len(near))


def fill_pair(unit, x, dy, y, dz):
    parts, n, two, r, w = unit.shape
    own_a, own_b = dy.shape[1] // parts, dz.shape[1] // parts
    for t in range(parts):
        a = mm_tn(x[...], dy[:, t * own_a : (t + 1) * own_a]).astype(BF)
        b = mm_tn(y[...], dz[:, t * own_b : (t + 1) * own_b]).astype(BF)
        g = jnp.concatenate([a, b], axis=1)
        for d in range(2 * n):
            unit[t, d // 2, d % 2] = g[d * r : (d + 1) * r]


class Owned:
    def __init__(self, refs, expand1, reduce1, expand2, reduce2):
        (self.e_unit, self.r_unit, self.e_kept, self.r_kept, self.e_from, self.r_from,
         self.e_low, self.r_low, self.e_got, self.r_got,
         self.loads, self.cores, self.e_z, self.r_z, self.homes) = refs
        self.out = (expand1, reduce1, expand2, reduce2)
        self.s, d = lax.axis_index("section"), lax.axis_index("dp")
        self.d, self.z, self.c = d, d // 2, d % 2
        self.h = self.s % 2
        self.has_rows = self.c == self.h
        self.n = self.e_unit.shape[1]

    def load(self, x_got, da_got, we1, wr1, we2, wr2, held):
        self.x, self.da, self.xt, self.we, self.wr, self.m, self.du = held
        wide = self.we.shape[2]
        self.copies = [
            pltpu.make_async_copy(x_got, self.x, self.loads.at[0]),
            pltpu.make_async_copy(da_got, self.da, self.loads.at[1]),
        ]
        start(self.copies)
        for which, (we, wr) in enumerate(((we1, wr1), (we2, wr2))):
            copies = []
            for i in range(self.n):
                at = pl.multiple_of((2 * i + self.h) * wide, 128)
                copies.append(
                    pltpu.make_async_copy(
                        we.at[:, pl.ds(at, wide)], self.we.at[i], self.loads.at[2 + 2 * i]
                    )
                )
                copies.append(
                    pltpu.make_async_copy(
                        wr.at[pl.ds(at, wide), :], self.wr.at[i], self.loads.at[3 + 2 * i]
                    )
                )

            @pl.when(self.s // 2 == which)
            def _(copies=copies):
                start(copies)

        self.copies += copies

    def loaded(self):
        wait(self.copies)
        for t in range(self.x.shape[0]):
            rows = self.x.shape[1]
            self.xt[:, t * rows : (t + 1) * rows] = self.x[t].T

    def core_e(self, i):
        return pltpu.make_async_remote_copy(
            src_ref=self.e_unit.at[i, :, 1 - self.c], dst_ref=self.e_kept.at[i],
            send_sem=self.cores.at[0, i], recv_sem=self.cores.at[1, i],
            device_id=(self.s, self.z * 2 + 1 - self.c), device_id_type=MESH,
        )

    def core_r(self, i):
        return pltpu.make_async_remote_copy(
            src_ref=self.r_unit.at[i], dst_ref=self.r_kept.at[i],
            send_sem=self.cores.at[2, i], recv_sem=self.cores.at[3, i],
            device_id=(self.s, self.z * 2 + 1 - self.c), device_id_type=MESH,
        )

    def along_e(self, i):
        out = []
        for k in range(1, self.n):
            to = (self.z + k) % self.n
            out.append(pltpu.make_async_remote_copy(
                src_ref=self.e_kept.at[i, to], dst_ref=self.e_from.at[k - 1, i],
                send_sem=self.e_z.at[0, i, k], recv_sem=self.e_z.at[1, i, k],
                device_id=(self.s, to * 2 + self.c), device_id_type=MESH,
            ))
        return out

    def along_r(self, i):
        k = (self.z - i + self.n) % self.n
        slot = jnp.maximum(k - 1, 0)
        return pltpu.make_async_remote_copy(
            src_ref=self.r_kept.at[i], dst_ref=self.r_from.at[slot],
            send_sem=self.r_z.at[0, i], recv_sem=self.r_z.at[1, slot],
            device_id=(self.s, i * 2 + self.c), device_id_type=MESH,
        )

    def make(self, i):
        parts, rows, width = self.x.shape
        wide = self.we.shape[2]

        def rows_of(t, _):
            u = mm(self.x[t], self.we[i]).astype(BF).astype(F32)
            m, slope = gelu_both(u)
            at = pl.ds(pl.multiple_of(t * rows, rows), rows)
            self.m[at, :] = m.astype(BF)
            self.du[at, :] = (mm_nt(self.da[t], self.wr[i]) * slope).astype(BF)
            return 0

        lax.fori_loop(0, parts, rows_of, 0)
        r = self.e_unit.shape[3]

        def columns_of(z, _):
            at = pl.ds(pl.multiple_of(z * 2 * r, 2 * r), 2 * r)
            g = mm(self.xt[at, :], self.du[...]).astype(BF)
            for c in range(2):
                self.e_unit[i, z, c] = g[c * r : (c + 1) * r]
            return 0

        lax.fori_loop(0, self.n, columns_of, 0)
        self.core_e(i).start()
        for at in range(0, width, 256):
            self.r_unit[i, :, at : at + 256] = mm_tn(
                self.m[...], self.da[:, :, at : at + 256].reshape(parts * rows, 256)
            ).astype(BF)
        pl.when(jnp.logical_not(self.has_rows))(self.core_r(i).start)

    def over_cores(self, i):
        self.core_e(i).wait()

        def step(z, _):
            self.e_kept[i, z] = self.e_kept[i, z] + self.e_unit[i, z, self.c]
            return 0

        lax.fori_loop(0, self.n, step, 0)
        start(self.along_e(i))
        pl.when(jnp.logical_not(self.has_rows))(self.core_r(i).wait_send)

        @pl.when(self.has_rows)
        def _():
            self.core_r(i).wait_recv()
            self.r_kept[i] = self.r_kept[i] + self.r_unit[i]

        pl.when(self.has_rows & (self.z != i))(self.along_r(i).start)

    def home_e(self, t):
        return pltpu.make_async_remote_copy(
            src_ref=self.e_low.at[t], dst_ref=self.e_got.at[self.s],
            send_sem=self.homes.at[0, t], recv_sem=self.homes.at[1, self.s],
            device_id=(t, self.d), device_id_type=MESH,
        )

    def home_r(self, t):
        return pltpu.make_async_remote_copy(
            src_ref=self.r_low.at[t], dst_ref=self.r_got.at[self.s // 2],
            send_sem=self.homes.at[2, t], recv_sem=self.homes.at[3, self.s // 2],
            device_id=(t, self.d), device_id_type=MESH,
        )

    def over_z_e(self):
        for i in range(self.n):
            wait(self.along_e(i))
            total = self.e_kept[i, self.z].astype(F32)
            for k in range(self.n - 1):
                total = total + self.e_from[k, i].astype(F32)
            self.e_low[i] = total.astype(BF)

            @pl.when(self.s == i)
            def _(i=i):
                self.e_got[i] = self.e_low[i]

            pl.when(self.s != i)(self.home_e(i).start)

    def over_z_r(self):
        parts, rows, wide = self.r_low.shape
        own = self.r_kept.shape[2] // parts
        for i in range(self.n):
            pl.when(self.has_rows & (self.z != i))(self.along_r(i).wait_send)

        @pl.when(self.has_rows)
        def _():
            for k in range(1, self.n):
                pltpu.make_async_remote_copy(
                    src_ref=self.r_kept.at[0], dst_ref=self.r_from.at[k - 1],
                    send_sem=self.r_z.at[0, 0], recv_sem=self.r_z.at[1, k - 1],
                    device_id=(self.s, (self.z + k) % self.n * 2 + self.c), device_id_type=MESH,
                ).wait_recv()
            step = rows // 4
            for at in range(0, rows, step):
                total = self.r_kept[self.z, at : at + step].astype(F32)
                for k in range(self.n - 1):
                    total = total + self.r_from[k, at : at + step].astype(F32)
                total = total.astype(BF)
                for t in range(parts):
                    low, _ = window(t, own)
                    self.r_low[t, at : at + step] = total[:, low : low + wide]
            for t in range(parts):
                pl.when(self.s != t)(self.home_r(t).start)

                @pl.when(self.s == t)
                def _(t=t):
                    self.r_got[self.s // 2] = self.r_low[t]

    def finish(self):
        parts = self.e_low.shape[0]
        for t in range(parts):
            pl.when(self.s != t)(self.home_e(t).wait_send)
            pl.when(self.has_rows & (self.s != t))(self.home_r(t).wait_send)
        for t in range(parts):
            copy = pltpu.make_async_remote_copy(
                src_ref=self.e_low.at[0], dst_ref=self.e_got.at[t],
                send_sem=self.homes.at[0, 0], recv_sem=self.homes.at[1, t],
                device_id=(self.s ^ 1, self.d), device_id_type=MESH,
            )
            pl.when(self.s != t)(copy.wait_recv)
        for which in range(2):
            copy = pltpu.make_async_remote_copy(
                src_ref=self.r_low.at[0], dst_ref=self.r_got.at[which],
                send_sem=self.homes.at[2, 0], recv_sem=self.homes.at[3, which],
                device_id=(self.s ^ 1, self.d), device_id_type=MESH,
            )
            pl.when(self.s != 2 * which + self.c)(copy.wait_recv)
        wide = self.e_got.shape[2]
        own = self.out[1].shape[1]
        shift = self.s * own % 128
        for which in range(2):
            expand, reduce = self.out[2 * which : 2 * which + 2]
            for h in range(2):
                expand[:, h * wide : (h + 1) * wide] = self.e_got[2 * which + h].astype(F32)
            block = self.r_got[which].astype(F32)
            out = block[:, :own]
            for offset in sorted({window(t, own)[1] for t in range(parts)} - {0}):
                out = jnp.where(shift == offset, block[:, offset : offset + own], out)
            reduce[...] = out


def tail_kernel(query_count, head_size, *refs):
    refs = list(refs)

    def take(count):
        out = refs[:count]
        del refs[:count]
        return out

    dq_blocks = take(1)[0]
    x_got, da_got, we1, wr1, we2, wr2 = take(6)
    low3, djoined2, mixed2, da4 = take(4)
    low1, mixed1, da2, x0, mixed_self1 = take(5)
    images, dkv, wq_hbm, wo_hbm, wp_hbm = take(5)
    dz2, n1, r1, gains, joined1, dg_mid, temper_rows = take(7)
    dx_got, small = take(2)
    expand2, reduce2, project2, out2, expand1, reduce1, asker, image_out, project1, out1 = take(10)
    pair_out = take(1)[0]
    units = ("self2", "self1", "image")
    buffers = {name: take(6) for name in units}
    pair_unit, pair_kept, pair_from_z, pair_low, pair_got = take(5)
    wide, sends, recvs, slots_a, slots_b, slots_c, slots_d, loads = take(8)
    slots = (slots_a, slots_b, slots_c, slots_d)
    dq_got, dqr, da1, djoined1, dx_blocks, sums, state_sends, state_recvs, local = take(9)
    owned = Owned(refs, expand1, reduce1, expand2, reduce2)
    own_heads = temper_rows.shape[0] // query_count

    s, d = lax.axis_index("section"), lax.axis_index("dp")
    z, c = d // 2, d % 2

    homes = {}
    for i, name in enumerate(units):
        unit = wide.at[:, :, :, :, : buffers[name][0].shape[3]]
        homes[name] = Home(unit, *buffers[name], sends.at[i], recvs.at[i])
    homes["pair"] = Home(
        pair_unit, pair_kept, None, None, None, None, pair_from_z,
        sends.at[len(units)], recvs.at[len(units)],
    )
    factors = {
        "self2": (low3, djoined2, mixed2, da4), "self1": (x0, djoined1, mixed_self1, da1),
        "image": (low1, dqr, mixed1, da2),
    }
    results = {
        "self2": (project2, out2), "self1": (project1, out1), "image": (asker, image_out),
    }

    def held(name):
        return [
            slots[j].at[:, : source.shape[1]] for j, source in enumerate(factors[name])
        ]

    def fetch(name):
        return [
            pltpu.make_async_copy(source, target, loads.at[units.index(name), j])
            for j, (source, target) in enumerate(zip(factors[name], held(name)))
        ]

    def make(name):
        wait(fetch(name))
        fill_pair(homes[name].unit, *held(name))
        start(homes[name].cores())

    def finish(name):
        wait(homes[name].along())
        total = homes[name].total()
        out = results[name]
        own = out[0].shape[1]
        out[0][...] = total[:, :own]
        out[1][...] = total[:, own:]

    steps = [("dp", 1), ("section", 1), ("section", 2)]
    bit = 2
    while bit < lax.axis_size("dp"):
        steps.append(("dp", bit))
        bit *= 2

    def small_copy(k):
        axis, bit = steps[k]
        to = (s ^ bit, d) if axis == "section" else (s, d ^ bit)
        return [pltpu.make_async_remote_copy(
            src_ref=small, dst_ref=sums.at[k], send_sem=state_sends.at[8 + k],
            recv_sem=state_recvs.at[8 + k], device_id=to, device_id_type=MESH,
        )]

    def small_step(k):
        if k > 0:
            wait(small_copy(k - 1))
            small[...] = small[...] + sums[k - 1]
        if k < len(steps):
            start(small_copy(k))

    dqs = exchange_copies(dq_blocks, dq_got, state_sends.at[pl.ds(4, 4)], state_recvs.at[pl.ds(4, 4)])
    dxs = exchange_copies(dx_blocks, dx_got, state_sends.at[pl.ds(16, 4)], state_recvs.at[pl.ds(16, 4)])

    def rest_of_states(wq, wo, wp, do):
        own = wq.shape[1] // dq_got.shape[0]
        wait(dqs)
        wait([pltpu.make_async_copy(*one) for one in
              ((wq_hbm, wq, local.at[0]), (wo_hbm, wo, local.at[1]), (wp_hbm, wp, local.at[2]))])
        dqr[...] = take_blocks(dq_got, own)
        d1 = dz2[...] + mm_nt(dqr[...], wq[...])
        dz, dg = norm_back(d1, gains[0:1, :], n1[...], r1[...])
        da1[...] = dz.astype(BF)
        do[...] = mm_nt(da1[...], wo[...]).astype(BF)
        attend_self_back(joined1, do, djoined1, query_count, head_size)
        put_blocks(dx_blocks, (dz + back_through(djoined1, wp)).astype(BF))
        start(dxs)
        width = small.shape[1]
        lane = lax.broadcasted_iota(jnp.int32, (1, width), 1)
        row = jnp.zeros((1, width), F32)
        for h in range(own_heads):
            one = jnp.sum(temper_rows[h * query_count : (h + 1) * query_count, :], keepdims=True)
            row = row + jnp.where(lane == s * own_heads + h, one, 0.0)
        small[...] = jnp.concatenate(
            [dg[None, :], dg_mid[...], row, jnp.zeros((2, width), F32)], axis=0
        )

    def image_block(j, slot, blocks):
        return pltpu.make_async_copy(
            images.at[j], blocks.at[slot], local.at[4 + slot]
        )

    def pair_gradient(blocks, kv, total):
        patches = images.shape[1]
        copy = pltpu.make_async_copy(dkv, kv, local.at[3])
        copy.start()
        image_block(0, 0, blocks).start()
        total[...] = jnp.zeros_like(total)
        copy.wait()

        def one_image(j, _):
            image_block(j, j % 2, blocks).wait()

            @pl.when(j + 1 < images.shape[0])
            def _():
                image_block(j + 1, (j + 1) % 2, blocks).start()

            total[...] += mm_tn(kv[j, :patches, :], blocks[j % 2])
            return 0

        lax.fori_loop(0, images.shape[0], one_image, 0)
        turned = pair_columns(total, pair_unit.shape[4] // 2)
        r = pair_unit.shape[3]
        for i in range(2 * pair_unit.shape[1]):
            pair_unit[0, i // 2, i % 2] = turned[i * r : (i + 1) * r]
        start(homes["pair"].cores())

    def pair_copy(half):
        to = 2 * half + s // 2
        return to, pltpu.make_async_remote_copy(
            src_ref=pair_low.at[half], dst_ref=pair_got.at[s % 2],
            send_sem=state_sends.at[20 + half], recv_sem=state_recvs.at[20 + s % 2],
            device_id=(to, d), device_id_type=MESH,
        )

    def send_pair():
        wait(homes["pair"].along())
        total = homes["pair"].total().astype(BF)
        own = total.shape[1] // 2
        for half in range(2):
            pair_low[half] = total[:, half * own : (half + 1) * own]
            to, copy = pair_copy(half)

            @pl.when(to != s)
            def _(copy=copy):
                copy.start()

            @pl.when(to == s)
            def _(half=half):
                pair_got[s % 2] = pair_low[half]

    def finish_pair():
        for half in range(2):
            to, copy = pair_copy(half)

            @pl.when(to != s)
            def _(copy=copy):
                copy.wait_send()

        for j in range(2):
            source = 2 * (s % 2) + j

            @pl.when(source != s)
            def _(j=j):
                pltpu.make_async_remote_copy(
                    src_ref=pair_low.at[0], dst_ref=pair_got.at[j],
                    send_sem=state_sends.at[20], recv_sem=state_recvs.at[20 + j],
                    device_id=(s ^ 1, d), device_id_type=MESH,
                ).wait_recv()

        own = pair_got.shape[2]
        for j in range(2):
            pair_out[:, j * own : (j + 1) * own] = pair_got[j].astype(F32)

    def over_cores(name):
        wait(homes[name].cores())
        homes[name].add_cores()
        start(homes[name].first())

    def over_first(name):
        wait(homes[name].first())
        homes[name].add_first()
        start(homes[name].second())

    def over_second(name):
        wait(homes[name].second())
        homes[name].add_second()
        start(homes[name].along())

    def owned_blocks(first, last):
        def step(i, _):
            owned.make(i)
            pl.when(i > 0)(lambda: owned.over_cores(i - 1))
            return 0

        lax.fori_loop(first, last, step, 0)

    start(fetch("self2"))

    def owner(*held):
        owned.load(x_got, da_got, we1, wr1, we2, wr2, held)
        greet()
        start(dqs)
        make("self2")
        owned.loaded()
        over_cores("self2")
        half = owned.n // 2
        owned_blocks(0, half)
        over_first("self2")
        owned_blocks(half, owned.n)

    parts, rows, width = x_got.shape
    block = we1.shape[1] // lax.axis_size("dp")
    n = owned.n
    pl.run_scoped(
        owner,
        *[
            pltpu.VMEM(dims, BF)
            for dims in (
                (parts, rows, width), (parts, rows, width), (width, parts * rows),
                (n, width, block), (n, block, width),
                (parts * rows, block), (parts * rows, block),
            )
        ],
    )

    def rest(wq, wo, wp, do):
        start([pltpu.make_async_copy(*one) for one in
               ((wq_hbm, wq, local.at[0]), (wo_hbm, wo, local.at[1]), (wp_hbm, wp, local.at[2]))])
        over_second("self2")
        rest_of_states(wq, wo, wp, do)

    pl.run_scoped(
        rest, *[pltpu.VMEM(w.shape, BF) for w in (wq_hbm, wo_hbm, wp_hbm)],
        pltpu.VMEM(da1.shape, BF),
    )
    owned.over_cores(owned.n - 1)
    start(fetch("self1"))
    small_step(0)
    make("self1")
    start(fetch("image"))
    small_step(1)
    over_cores("self1")
    make("image")

    def second(blocks, kv, total):
        pair_gradient(blocks, kv, total)

    pl.run_scoped(
        second,
        pltpu.VMEM((2, images.shape[1], images.shape[2]), BF),
        pltpu.VMEM(dkv.shape, BF),
        pltpu.VMEM((dkv.shape[2], images.shape[2]), F32),
    )
    over_first("self1")
    over_cores("image")
    small_step(2)
    wait(homes["pair"].cores())
    homes["pair"].add_cores()
    start(homes["pair"].along())
    owned.over_z_e()
    over_second("self1")
    over_first("image")
    small_step(3)
    owned.over_z_r()
    finish("self2")
    over_second("image")
    small_step(4)
    send_pair()
    owned.finish()
    small_step(5)
    finish("self1")
    finish_pair()
    finish("image")
    wait(dxs)


def tail(operands, sections, dp, width, hidden, query_count, head_size):
    n = dp // 2
    rows, most = operands[7].shape[0], operands[8].shape[1]
    r, own, wide_own = width // dp, width // sections, hidden // sections
    images, dkv = operands[16], operands[17]
    feat = images.shape[2]
    lanes = operands[0].shape[2]
    pair_r, pair_w = feat // dp, 2 * own

    def buffers(w):
        return [
            pltpu.VMEM((sections, n, r, w), BF),
            pltpu.VMEM((2, n, r // 2, w), BF), pltpu.VMEM((2, n, r // 2, w), BF),
            pltpu.VMEM((n, r // 2, w), BF), pltpu.VMEM((n, r // 2, w), BF),
            pltpu.VMEM((n - 1, r, w), BF),
        ]

    results = [
        shape((sections, rows, lanes), BF),
        shape((8, width), F32),
        shape((r, wide_own), F32), shape((hidden // dp, own), F32),
        shape((r, 3 * own), F32), shape((r, own), F32),
        shape((r, wide_own), F32), shape((hidden // dp, own), F32),
        shape((r, own), F32), shape((r, own), F32),
        shape((r, 3 * own), F32), shape((r, own), F32),
        shape((pair_r, pair_w), F32),
    ]
    scratch = []
    for w in (4 * own,) * 2 + (2 * own,):
        scratch += buffers(w)
    scratch += [
        pltpu.VMEM((1, n, 2, pair_r, pair_w), BF), pltpu.VMEM((1, n, pair_r, pair_w), BF),
        pltpu.VMEM((n - 1, pair_r, pair_w), BF),
        pltpu.VMEM((2, pair_r, own), BF), pltpu.VMEM((2, pair_r, own), BF),
        pltpu.VMEM((sections, n, 2, r, 4 * own), BF),
        pltpu.SemaphoreType.DMA((8, 10)), pltpu.SemaphoreType.DMA((8, 10)),
        pltpu.VMEM((rows, width), BF), pltpu.VMEM((rows, most), BF),
        pltpu.VMEM((rows, width), BF), pltpu.VMEM((rows, width), BF),
        pltpu.SemaphoreType.DMA((8, 4)),
        pltpu.VMEM((sections, rows, lanes), BF),
        pltpu.VMEM((rows, width), BF), pltpu.VMEM((rows, width), BF),
        pltpu.VMEM((rows, 3 * width), BF), pltpu.VMEM((sections, rows, lanes), BF),
        pltpu.VMEM((8, 8, width), F32),
        pltpu.SemaphoreType.DMA((24,)), pltpu.SemaphoreType.DMA((24,)),
        pltpu.SemaphoreType.DMA((6,)),
    ]
    block = hidden // dp
    scratch += [
        pltpu.VMEM((n, n, 2, r, block), BF), pltpu.VMEM((n, block, width), BF),
        pltpu.VMEM((n, n, r, block), BF), pltpu.VMEM((n, block, width), BF),
        pltpu.VMEM((n - 1, n, r, block), BF), pltpu.VMEM((n - 1, block, width), BF),
        pltpu.VMEM((n, r, block), BF), pltpu.VMEM((sections, block, lanes), BF),
        pltpu.VMEM((sections, r, block), BF), pltpu.VMEM((2, block, lanes), BF),
        pltpu.SemaphoreType.DMA((2 + 2 * n,)), pltpu.SemaphoreType.DMA((4, n)),
        pltpu.SemaphoreType.DMA((2, n, n)), pltpu.SemaphoreType.DMA((2, n)),
        pltpu.SemaphoreType.DMA((4, sections)),
    ]
    return pl.pallas_call(
        functools.partial(tail_kernel, query_count, head_size),
        out_shape=results,
        in_specs=[whole(pl.ANY)] * 21 + [whole()] * 7,
        out_specs=[whole(pl.ANY)] + [whole()] * 12,
        scratch_shapes=scratch,
        compiler_params=pltpu.CompilerParams(
            vmem_limit_bytes=LIMIT, collective_id=2, has_side_effects=True
        ),
    )(*operands)


def body(
    starting_learned_vectors,
    frozen_picture_vectors,
    texts_per_picture,
    early_triple_matrix,
    early_mixing_exit_matrix,
    picture_asker_matrix,
    picture_pair_matrix,
    picture_exit_matrix,
    early_widen_matrix,
    early_narrow_matrix,
    later_triple_matrix,
    later_mixing_exit_matrix,
    later_widen_matrix,
    later_narrow_matrix,
    standardizer_factors,
    picture_divisors,
    closing_cotangent,
):
    sections = lax.axis_size("section")
    dp = lax.axis_size("dp")
    me = lax.axis_index("section")
    item_count, query_count, width = starting_learned_vectors.shape
    heads = picture_divisors.shape[0]
    images, patches, feat = frozen_picture_vectors.shape
    own_items = item_count // sections
    rows = own_items * query_count
    own_heads = heads // sections
    head_size = width // heads
    own_width = width // sections
    wide = -(-own_width // 128) * 128
    padded = -(-patches // 16) * 16
    hidden = early_widen_matrix.shape[1]
    gains = standardizer_factors

    clamped = jnp.clip(picture_divisors, 0.5, 2.0)
    scale_all = 1.0 / math.sqrt(head_size) / clamped

    def act(*dims, dtype=BF):
        return shape((rows,) + dims, dtype)

    def blocks():
        return (sections, rows, wide)

    def comm(kernel, outs, args, specs, out_specs, scratch, identity):
        return pl.pallas_call(
            kernel, out_shape=outs, in_specs=specs, out_specs=out_specs, scratch_shapes=scratch,
            compiler_params=pltpu.CompilerParams(
                vmem_limit_bytes=LIMIT, collective_id=identity, has_side_effects=True
            ),
        )(*args)

    sems = pltpu.SemaphoreType.DMA
    x0, h1, low1, n1, r1, joined1, mixed_self1, q_got, keyval, mixed1_rows = comm(
        functools.partial(front_kernel, query_count, head_size, own_heads),
        (
            act(width), act(width, dtype=F32), act(width), act(width, dtype=F32), act(1, dtype=F32),
            act(3 * width), act(width), shape(blocks(), BF),
            shape((images, padded, 2 * wide), BF), act(width),
        ),
        (
            texts_per_picture, picture_divisors, gains, starting_learned_vectors,
            frozen_picture_vectors, early_triple_matrix, early_mixing_exit_matrix,
            picture_asker_matrix, picture_pair_matrix,
        ),
        [whole(SMEM), whole(SMEM), whole()] + [whole(pl.ANY)] * 6,
        [whole()] * 10,
        [
            pltpu.VMEM((own_items, query_count, width), BF),
            pltpu.VMEM(early_triple_matrix.shape, BF), pltpu.VMEM((width, width), BF),
            pltpu.VMEM((width, width), BF), pltpu.VMEM((feat, 2 * wide), BF),
            pltpu.VMEM((2, patches, feat), BF),
            pltpu.VMEM(blocks(), BF), pltpu.VMEM(blocks(), BF), pltpu.VMEM(blocks(), BF),
            sems((6,)), sems((2,)), sems((4,)), sems((4,)), sems((4,)), sems((4,)),
        ],
        0,
    )

    weights = (
        picture_exit_matrix, early_widen_matrix, early_narrow_matrix, later_triple_matrix,
        later_mixing_exit_matrix, later_widen_matrix, later_narrow_matrix,
    )
    owners = width // dp % 32 == 0 and feat // dp % 16 == 0 and hidden // dp % 128 == 0
    factors = (
        act(width), act(hidden), act(hidden), act(width),
        act(width), act(hidden), act(hidden), act(width),
    )
    everywhere = shape((sections, rows, width), BF)
    final_got, do_got, low3, mixed2, djoined2, da4, da2, dz2, dg_mid, *given = comm(
        functools.partial(middle_kernel, query_count, head_size, owners),
        (
            shape(blocks(), BF), shape(blocks(), BF),
            act(width), act(width), act(3 * width), act(width),
            act(width), act(width, dtype=F32), shape((4, width), F32),
        ) + ((everywhere, everywhere) if owners else factors),
        (h1, mixed1_rows, gains, closing_cotangent) + weights,
        [whole()] * 3 + [whole(pl.ANY)] * (1 + len(weights)),
        [whole(pl.ANY)] * 2 + [whole()] * 7
        + ([whole(pl.ANY)] * 2 if owners else [whole()] * len(factors)),
        ([pltpu.VMEM(f.shape, BF) for f in factors] if owners else [])
        + [pltpu.VMEM(w.shape, BF) for w in weights]
        + [pltpu.VMEM((own_items, query_count, width), BF)]
        + [pltpu.VMEM(blocks(), BF)] * 2
        + [sems((len(weights) + 1,)), sems((8,)), sems((8,)), sems((2, 2, 2)), sems((2, sections))]
        + [pltpu.VMEM((rows, hidden), F32)] * 2
        + [pltpu.VMEM((rows, 3 * width), BF), pltpu.VMEM((rows, width), BF)]
        + [pltpu.VMEM((rows, width), F32), pltpu.VMEM((rows, 1), F32)] * 4,
        1,
    )

    dq, dkv, temper_rows = call(
        functools.partial(
            attend_image_back_kernel, patches, own_heads, head_size, query_count, 2
        ),
        (
            shape((sections * rows, wide), BF),
            shape((images, padded, 2 * wide), BF),
            shape((own_heads * query_count, 1), F32),
        ),
        texts_per_picture, picture_divisors, q_got.reshape(sections * rows, wide),
        do_got.reshape(sections * rows, wide), keyval,
        in_specs=[whole(SMEM), whole(SMEM), whole(), whole(), whole()],
        scratch=[pltpu.VMEM((images, padded, 2 * wide), F32)],
    )

    def home_states(got):
        got = got.reshape(item_count, query_count, wide)
        at = me * own_width % 128
        return lax.dynamic_slice_in_dim(got, at, own_width, 2).astype(F32)

    interior = ((picture_divisors > 0.5) & (picture_divisors < 2.0)).astype(F32)
    temper_factor = (-scale_all / clamped) * interior
    dq_sent = dq.reshape(sections, rows, wide)
    if owners:
        (
            dx_got, small, expand2, reduce2, project2, out2, expand1, reduce1,
            asker, image_out, project1, out1, pair_part,
        ) = tail(
            (
                dq_sent, *given, early_widen_matrix, early_narrow_matrix,
                later_widen_matrix, later_narrow_matrix, low3, djoined2, mixed2, da4,
                low1, mixed1_rows, da2, x0, mixed_self1,
                frozen_picture_vectors, dkv, picture_asker_matrix, early_mixing_exit_matrix,
                early_triple_matrix, dz2, n1, r1, gains, joined1, dg_mid, temper_rows,
            ),
            sections, dp, width, hidden, query_count, head_size,
        )
        gains_grad = small[:5]
        temper_grad = small[5, :heads] * temper_factor
    else:
        low2, m1, du1, da3, low4, m2, du2, da5 = given
        dq_blocks = exchange(dq_sent)
        d_pair = pl.pallas_call(
            keyval_grad_kernel,
            out_shape=shape((feat, 2 * own_width), BF),
            grid=(images,),
            in_specs=[
                pl.BlockSpec((1, patches, feat), lambda j: (j, 0, 0)),
                pl.BlockSpec((1, padded, 2 * wide), lambda j: (j, 0, 0)),
            ],
            out_specs=pl.BlockSpec((feat, 2 * own_width), lambda j: (0, 0)),
            scratch_shapes=[pltpu.VMEM((2 * wide, feat), F32)],
            compiler_params=pltpu.CompilerParams(vmem_limit_bytes=LIMIT),
        )(frozen_picture_vectors, dkv)

        dq_rows, da1, djoined1, dx_blocks, dg0 = call(
            functools.partial(last_kernel, query_count, head_size),
            (
                act(width), act(width), act(3 * width),
                shape((sections, rows, wide), BF), shape((1, width), F32),
            ),
            dz2, dq_blocks, picture_asker_matrix, n1, r1, gains, early_mixing_exit_matrix, joined1,
            early_triple_matrix,
            scratch=[pltpu.VMEM((rows, width), BF)],
        )

        def block_unit(grad):
            parts, k, own = grad.shape
            return grad.reshape(parts, dp, k // dp, own)

        def pair_grad(x, dy, y, dz):
            own = (dy.shape[1] + dz.shape[1]) // sections
            return block_unit(
                call(pair_weight_kernel, shape((sections, x.shape[1], own), BF), x, dy, y, dz)
            )

        expand2 = home(block_unit(expand_grad(low4, du2, sections)))
        reduce2 = home(reduce_grad(da5, m2, sections, dp)).T
        self2 = home(pair_grad(low3, djoined2, mixed2, da4))
        expand1 = home(block_unit(expand_grad(low2, du1, sections)))
        reduce1 = home(reduce_grad(da3, m1, sections, dp)).T
        pair_block = line_sum(
            core_sum(d_pair.reshape(1, dp, feat // dp, 2 * own_width))[0]
        )
        image_units = home(pair_grad(low1, dq_rows, mixed1_rows, da2))
        self1 = home(pair_grad(x0, djoined1, mixed_self1, da1))
        third = 3 * own_width
        project2, out2 = self2[:, :third], self2[:, third:]
        project1, out1 = self1[:, :third], self1[:, third:]
        asker, image_out = image_units[:, :own_width], image_units[:, own_width:]

        pair_rows = pair_block.shape[0]
        half = sections // 2
        pair_halves = pair_block.astype(BF).reshape(pair_rows, 2, own_width).transpose(1, 0, 2)
        key_home, val_home = me // 2, half + me // 2
        sent = jnp.zeros((sections, pair_rows, own_width), BF)
        sent = lax.dynamic_update_index_in_dim(sent, pair_halves[0], key_home, 0)
        sent = lax.dynamic_update_index_in_dim(sent, pair_halves[1], val_home, 0)
        got = exchange(sent)
        first = (me % half) * 2
        pair_part = lax.dynamic_slice_in_dim(got, first, 2, 0)
        pair_part = pair_part.transpose(1, 0, 2).reshape(pair_rows, 2 * own_width).astype(F32)

        dx_got = exchange(dx_blocks)
        d_temper = jnp.sum(temper_rows.reshape(own_heads, query_count), axis=1)
        spread = jnp.zeros((heads,), F32)
        spread = lax.dynamic_update_slice_in_dim(spread, d_temper, me * own_heads, 0)
        small = all_sum(jnp.concatenate([dg0.reshape(-1), dg_mid.reshape(-1), spread]))
        gains_grad = small[: 5 * width].reshape(5, width)
        temper_grad = small[5 * width :] * temper_factor

    final_part = home_states(final_got)
    grad_part = home_states(dx_got)

    def f(block):
        return block.astype(F32)

    return (
        final_part,
        grad_part,
        f(project1),
        f(out1),
        f(asker),
        pair_part,
        f(image_out),
        f(expand1),
        f(reduce1),
        f(project2),
        f(out2),
        f(expand2),
        f(reduce2),
        gains_grad,
        temper_grad,
    )


def solution(mesh):
    return jax.shard_map(
        body,
        mesh=mesh,
        in_specs=(P("dp", None, None), P("dp", None, None), P("dp", None))
        + (P(),) * 13
        + (P("dp", None, None),),
        out_specs=(P("dp", None, "section"),) * 2 + (P("dp", "section"),) * 11 + (P(), P()),
        check_vma=False,
    )
```

```python
import functools
import math

import jax
import jax.numpy as jnp
from jax import lax
from jax.experimental import pallas as pl
from jax.experimental.pallas import tpu as pltpu
from jax.sharding import PartitionSpec as P

EPSILON = 1e-06
BF = jnp.bfloat16
F32 = jnp.float32


def mm(left, right):
    return jnp.dot(left, right, preferred_element_type=F32)


def mm_tn(left, right):
    return lax.dot_general(left, right, (((0,), (0,)), ((), ())), preferred_element_type=F32)


def mm_nt(left, right):
    return lax.dot_general(left, right, (((1,), (1,)), ((), ())), preferred_element_type=F32)


def layer_norm(z, gain):
    centred = z - jnp.mean(z, axis=-1, keepdims=True)
    inverse = lax.rsqrt(jnp.mean(centred * centred, axis=-1, keepdims=True) + EPSILON)
    normed = centred * inverse
    return normed * gain, normed, inverse


def norm_back(dout, gain, normed, inverse):
    dn = dout * gain
    dgain = jnp.sum(dout * normed, axis=0)
    dz = inverse * (
        dn
        - jnp.mean(dn, axis=-1, keepdims=True)
        - normed * jnp.mean(dn * normed, axis=-1, keepdims=True)
    )
    return dz, dgain


def gelu_both(u):
    cdf = 0.5 * (1.0 + lax.erf(u * (0.5**0.5)))
    return u * cdf, cdf + u * jnp.exp(-0.5 * u * u) * (1.0 / math.sqrt(2.0 * math.pi))


def swap(value, axis, bit):
    size = lax.axis_size(axis)
    return lax.ppermute(value, axis, [(i, i ^ bit) for i in range(size)])


def pick(value, index, axis):
    return lax.dynamic_index_in_dim(value, index, axis, keepdims=False)


def add_low(left, right):
    return (left.astype(F32) + right.astype(F32)).astype(BF)


def section_blocks(value):
    rows, width = value.shape
    parts = lax.axis_size("section")
    return value.reshape(rows, parts, width // parts).transpose(1, 0, 2)


def exchange(blocks):
    me = lax.axis_index("section")
    parts = lax.axis_size("section")
    out = blocks
    for bit in range(1, parts):
        got = swap(pick(blocks, me ^ bit, 0), "section", bit)
        out = lax.dynamic_update_index_in_dim(out, got, me ^ bit, 0)
    return out


def cols_to_section(value):
    return exchange(section_blocks(value))


def rows_from_section(blocks):
    got = exchange(blocks)
    parts, rows, width = got.shape
    return got.transpose(1, 0, 2).reshape(rows, parts * width)


def line_sum(blocks):
    n = blocks.shape[0]
    p = lax.axis_index("dp") // 2
    size = lax.axis_size("dp")
    kept = blocks
    for k in range(n - 1):
        up_at = jnp.clip(n - 1 - k + p, 0, n - 1)
        down_at = jnp.clip(p - (n - 1 - k), 0, n - 1)
        up_pairs = [(2 * q + c, 2 * q + 2 + c) for q in range(min(k, n - 2) + 1) for c in (0, 1)]
        down_pairs = [
            (2 * q + c, 2 * q - 2 + c) for q in range(max(n - 1 - k, 1), n) for c in (0, 1)
        ]
        up = lax.ppermute(pick(kept, up_at, 0), "dp", up_pairs)
        down = lax.ppermute(pick(kept, down_at, 0), "dp", down_pairs)
        up_to = jnp.clip(n - 2 - k + p, 0, n - 1)
        down_to = jnp.clip(p + 1 - (n - 1 - k), 0, n - 1)
        kept = lax.dynamic_update_index_in_dim(kept, add_low(pick(kept, up_to, 0), up), up_to, 0)
        kept = lax.dynamic_update_index_in_dim(
            kept, add_low(pick(kept, down_to, 0), down), down_to, 0
        )
    del size
    return pick(kept, p, 0)


def core_sum(unit):
    parts, dp, r, w = unit.shape
    c = lax.axis_index("dp") % 2
    pairs = unit.reshape(parts, dp // 2, 2, r, w)
    return add_low(pick(pairs, c, 2), swap(pick(pairs, 1 - c, 2), "dp", 1))


def plane_sum(unit):
    parts, n, r, w = unit.shape
    me = lax.axis_index("section")
    low, high = me % 2, me // 2
    square = unit.reshape(2, 2, n, r, w)
    a, b = square[:, :, :, : r // 2], square[:, :, :, r // 2 :]
    a = add_low(pick(a, low, 1), swap(pick(a, 1 - low, 1), "section", 1))
    b = add_low(pick(b, high, 0), swap(pick(b, 1 - high, 0), "section", 2))
    a = add_low(pick(a, high, 0), swap(pick(a, 1 - high, 0), "section", 2))
    b = add_low(pick(b, low, 0), swap(pick(b, 1 - low, 0), "section", 1))
    return jnp.concatenate([a, b], axis=1)


def home(unit):
    return line_sum(plane_sum(core_sum(unit)))


def unit_of(grad, dp, sections):
    rows, cols = grad.shape
    return (
        grad.astype(BF)
        .reshape(dp, rows // dp, sections, cols // sections)
        .transpose(2, 0, 1, 3)
    )


def all_sum(value):
    for axis in ("dp", "section"):
        bit = 1
        while bit < lax.axis_size(axis):
            value = value + swap(value, axis, bit)
            bit *= 2
    return value


VMEM = pltpu.MemorySpace.VMEM
SMEM = pltpu.MemorySpace.SMEM
LIMIT = 60 * 1024 * 1024
GROUP = 128


def whole(space=VMEM):
    return pl.BlockSpec(memory_space=space)


def head_lanes(shape, head, head_size):
    return lax.broadcasted_iota(jnp.int32, shape, len(shape) - 1) // head_size == head


def same_item(query_count):
    shape = (GROUP, GROUP)
    left = lax.broadcasted_iota(jnp.int32, shape, 0) // query_count
    right = lax.broadcasted_iota(jnp.int32, shape, 1) // query_count
    return left == right


def soft(t, mask, scale):
    t = jnp.where(mask, t * scale, -1e30)
    e = jnp.exp(t - jnp.max(t, axis=0, keepdims=True))
    return e * (1.0 / jnp.sum(e, axis=0, keepdims=True))


def masked(value, head, head_size):
    return jnp.where(head_lanes(value.shape, head, head_size), value, jnp.zeros_like(value))


def pairs_at_once(pairs):
    return 3 if pairs % 3 == 0 else 1


def attend_self(joined_ref, mixed_ref, query_count, head_size):
    rows, width = mixed_ref.shape
    pair = 2 * head_size
    scale = 1.0 / math.sqrt(head_size)
    mask = same_item(query_count)
    many = pairs_at_once(width // pair)

    def step(i, _):
        places = [
            (pl.ds(g * GROUP, GROUP), pl.multiple_of((i * many + j) * pair, pair))
            for j in range(many)
            for g in range(rows // GROUP)
        ]
        heads = [(at, col, h) for at, col in places for h in range(2)]
        t = [
            mm_nt(
                masked(joined_ref[at, pl.ds(width + col, pair)], h, head_size),
                joined_ref[at, pl.ds(col, pair)],
            )
            for at, col, h in heads
        ]
        turned = [joined_ref[at, pl.ds(2 * width + col, pair)].T for at, col in places]
        p = [soft(one, mask, scale).astype(BF) for one in t]
        o = [
            mm(turned[n // 2][h * head_size : (h + 1) * head_size], p[n])
            for n, (_, _, h) in enumerate(heads)
        ]
        for n, (at, col) in enumerate(places):
            both = jnp.concatenate([o[2 * n], o[2 * n + 1]], axis=0)
            mixed_ref[at, pl.ds(col, pair)] = both.astype(BF).T
        return 0

    lax.fori_loop(0, width // pair // many, step, 0)


def attend_self_back(joined_ref, do_ref, djoined_ref, query_count, head_size, many=None):
    rows, width = do_ref.shape
    pair = 2 * head_size
    scale = 1.0 / math.sqrt(head_size)
    mask = same_item(query_count)
    many = many or pairs_at_once(width // pair)

    def step(i, _):
        places = [
            (pl.ds(g * GROUP, GROUP), pl.multiple_of((i * many + j) * pair, pair))
            for j in range(many)
            for g in range(rows // GROUP)
        ]
        heads = [(at, col, h) for at, col in places for h in range(2)]

        def part(at, col, which):
            return joined_ref[at, pl.ds(which * width + col, pair)]

        def head_of(value, h):
            return masked(value, h, head_size)

        t = [mm_nt(head_of(part(at, col, 1), h), part(at, col, 0)) for at, col, h in heads]
        dp = [
            mm_nt(head_of(part(at, col, 2), h), do_ref[at, pl.ds(col, pair)])
            for at, col, h in heads
        ]
        turned = [part(at, col, 1).T for at, col in places]
        p = [soft(one, mask, scale) for one in t]
        dt = [
            (one * (grad - jnp.sum(one * grad, axis=0, keepdims=True)) * scale).astype(BF)
            for one, grad in zip(p, dp)
        ]
        dv = [
            mm(one.astype(BF), head_of(do_ref[at, pl.ds(col, pair)], h))
            for one, (at, col, h) in zip(p, heads)
        ]
        dk = [mm(one, head_of(part(at, col, 0), h)) for one, (at, col, h) in zip(dt, heads)]
        dq = [
            mm(turned[n // 2][h * head_size : (h + 1) * head_size], dt[n])
            for n, (_, _, h) in enumerate(heads)
        ]
        for n, (at, col) in enumerate(places):
            both = jnp.concatenate([dq[2 * n], dq[2 * n + 1]], axis=0)
            djoined_ref[at, pl.ds(col, pair)] = both.astype(BF).T
            djoined_ref[at, pl.ds(width + col, pair)] = (dk[2 * n] + dk[2 * n + 1]).astype(BF)
            djoined_ref[at, pl.ds(2 * width + col, pair)] = (dv[2 * n] + dv[2 * n + 1]).astype(BF)
        return 0

    lax.fori_loop(0, width // pair // many, step, 0)


def project_into(out_ref, low, w_ref, block=768):
    for at in range(0, w_ref.shape[1], block):
        out_ref[:, at : at + block] = mm(low, w_ref[:, at : at + block]).astype(BF)


def back_through(dy_ref, w_ref, block=768):
    total = None
    for at in range(0, w_ref.shape[1], block):
        term = mm_nt(dy_ref[:, at : at + block], w_ref[:, at : at + block])
        total = term if total is None else total + term
    return total


def hidden_forward(low, w_expand_ref, w_reduce_ref, m_ref, slope_ref, block=512):
    total = None
    for at in range(0, w_expand_ref.shape[1], block):
        u = mm(low, w_expand_ref[:, at : at + block]).astype(BF).astype(F32)
        m, slope = gelu_both(u)
        m = m.astype(BF)
        m_ref[:, at : at + block] = m
        slope_ref[:, at : at + block] = slope
        term = mm(m, w_reduce_ref[at : at + block, :])
        total = term if total is None else total + term
    return total


def hidden_backward(da, w_expand_ref, w_reduce_ref, slope_ref, du_ref, block=512):
    total = None
    for at in range(0, w_expand_ref.shape[1], block):
        dm = mm_nt(da, w_reduce_ref[at : at + block, :])
        du = (dm * slope_ref[:, at : at + block]).astype(BF)
        du_ref[:, at : at + block] = du
        term = mm_nt(du, w_expand_ref[:, at : at + block])
        total = term if total is None else total + term
    return total


def norm_into(z, gain, n_ref, r_ref):
    out, n, r = layer_norm(z, gain)
    n_ref[...] = n
    r_ref[...] = r
    return out


def window(t, own):
    low = t * own // 128 * 128
    return low, t * own - low


def put_blocks(out_ref, value):
    parts, _, wide = out_ref.shape
    own = value.shape[1] // parts
    for t in range(parts):
        low, _ = window(t, own)
        out_ref[t] = value[:, low : low + wide]


def take_blocks(in_ref, own):
    parts, _, wide = in_ref.shape
    pieces = []
    for low in range(0, parts * own, 128):
        piece = None
        for t in range(parts):
            first, _ = window(t, own)
            if first <= low < first + wide:
                part = in_ref[t, :, low - first : low - first + 128]
                piece = part if piece is None else piece + part
        pieces.append(piece)
    return jnp.concatenate(pieces, axis=1)


MESH = pl.DeviceIdType.MESH


def start(copies):
    for copy in copies:
        copy.start()


def wait(copies):
    for copy in copies:
        copy.wait()


def exchange_copies(source, target, sends, recvs):
    s, d = lax.axis_index("section"), lax.axis_index("dp")
    out = []
    for bit in range(1, lax.axis_size("section")):
        to = s ^ bit
        out.append(pltpu.make_async_remote_copy(
            src_ref=source.at[to], dst_ref=target.at[s], send_sem=sends.at[bit],
            recv_sem=recvs.at[bit], device_id=(to, d), device_id_type=MESH,
        ))
    out.append(pltpu.make_async_copy(source.at[s], target.at[s], sends.at[0]))
    return out


def greet_sections():
    s, d = lax.axis_index("section"), lax.axis_index("dp")
    barrier = pltpu.get_barrier_semaphore()
    parts = lax.axis_size("section")
    for bit in range(1, parts):
        pl.semaphore_signal(barrier, inc=1, device_id=(s ^ bit, d), device_id_type=MESH)
    pl.semaphore_wait(barrier, parts - 1)


def owner_copies(source, target, which, sends, recvs):
    s, d = lax.axis_index("section"), lax.axis_index("dp")
    out = []
    for i in range(2):
        to = 2 * which + i
        out.append((to != s, pltpu.make_async_remote_copy(
            src_ref=source, dst_ref=target.at[s], send_sem=sends.at[which, i],
            recv_sem=recvs.at[s], device_id=(to, d), device_id_type=MESH,
        )))
        out.append((to == s, pltpu.make_async_copy(source, target.at[s], sends.at[which, i])))
    return out


def start_if(pairs):
    for condition, copy in pairs:
        pl.when(condition)(copy.start)


def sent_if(pairs):
    for remote, local in zip(pairs[::2], pairs[1::2]):
        pl.when(remote[0])(remote[1].wait_send)
        pl.when(local[0])(local[1].wait)


def received(target, sends, recvs):
    s, d = lax.axis_index("section"), lax.axis_index("dp")
    for t in range(lax.axis_size("section")):
        copy = pltpu.make_async_remote_copy(
            src_ref=target.at[t], dst_ref=target.at[t], send_sem=sends.at[0, 0],
            recv_sem=recvs.at[t], device_id=(s ^ 1, d), device_id_type=MESH,
        )
        pl.when(t != s)(copy.wait_recv)


def front_kernel(
    query_count, head_size, own_heads,
    texts_ref, divisor_ref, g_ref, x_hbm, images_hbm, wp_hbm, wo_hbm, wq_hbm, pair_hbm,
    x_ref, h_ref, low_ref, n_ref, r_ref, joined_ref, mixed_ref, q_got, kv_ref, mixed1_ref,
    x_in, wp, wo, wq, w_pair, blocks, q_blocks, o_blocks, o_got,
    loads, image_sems, q_sends, q_recvs, o_sends, o_recvs,
):
    s, d = lax.axis_index("section"), lax.axis_index("dp")
    parts, rows, wide = q_got.shape
    images, patches, feat = images_hbm.shape
    width = x_ref.shape[1]
    own = width // parts
    items = x_in.shape[0]
    low_at = pl.multiple_of(s * own // 128 * 128, 128)
    copies = [
        pltpu.make_async_copy(source, target, loads.at[i])
        for i, (source, target) in enumerate((
            (x_hbm.at[pl.ds(s * items, items)], x_in),
            (wp_hbm, wp), (wo_hbm, wo), (wq_hbm, wq),
            (pair_hbm.at[:, pl.ds(low_at, wide)], w_pair.at[:, :wide]),
            (pair_hbm.at[:, pl.ds(pl.multiple_of(width + low_at, 128), wide)], w_pair.at[:, wide:]),
        ))
    ]
    start(copies)

    def image(j):
        return pltpu.make_async_copy(images_hbm.at[j], blocks.at[j % 4], image_sems.at[j % 4])

    for j in range(min(3, images)):
        image(j).start()
    greet_sections()
    copies[0].wait()
    x_ref[...] = x_in[...].reshape(rows, width)
    copies[1].wait()
    project_into(joined_ref, x_ref[...], wp)
    attend_self(joined_ref, mixed_ref, query_count, head_size)
    copies[2].wait()
    z = x_ref[...].astype(F32) + mm(mixed_ref[...], wo[...])
    h = norm_into(z, g_ref[0:1, :], n_ref, r_ref)
    h_ref[...] = h
    low_ref[...] = h.astype(BF)
    copies[3].wait()
    put_blocks(q_blocks, mm(low_ref[...], wq[...]).astype(BF))
    q_copies = exchange_copies(q_blocks, q_got, q_sends, q_recvs)
    start(q_copies)

    copies[4].wait()
    copies[5].wait()
    padded = kv_ref.shape[1]
    full = patches // 16 * 16
    for j in range(images):
        image(j).wait()
        if j + 3 < images:
            image(j + 3).start()
        kv_ref[j, full:, :] = jnp.zeros((padded - full, kv_ref.shape[2]), BF)
        kv_ref[j, :patches, :] = mm(blocks[j % 4], w_pair[...]).astype(BF)

    scales = column_scales(divisor_ref, own_heads, head_size, query_count)
    shift = s * own % 128 // head_size
    ends = caption_ends(texts_ref)
    mask = patch_rows(padded, patches)
    together = items

    for copy in q_copies[:-1]:
        copy.wait()
    q_copies[-1].wait()
    o_copies = []
    for bit in (1, 2, 3, 0):
        t = s ^ bit

        def step(i, _, t=t):
            group = [i * together + b for b in range(together)]

            def at(item):
                return pl.ds(pl.multiple_of(item * query_count, query_count), query_count)

            done = attend_image(
                lambda item: q_got[t, at(item), :], group, kv_ref,
                [image_at(ends, t * items + item) for item in group],
                mask, scales, own_heads, head_size, shift,
            )
            for item, rows in zip(group, done):
                o_blocks[t, at(item), :] = rows
            return 0

        lax.fori_loop(0, items // together, step, 0)
        if bit:
            copy = pltpu.make_async_remote_copy(
                src_ref=o_blocks.at[t], dst_ref=o_got.at[s], send_sem=o_sends.at[bit],
                recv_sem=o_recvs.at[bit], device_id=(t, d), device_id_type=MESH,
            )
        else:
            copy = pltpu.make_async_copy(o_blocks.at[t], o_got.at[t], o_sends.at[0])
        copy.start()
        o_copies.append(copy)
    wait(o_copies)
    mixed1_ref[...] = take_blocks(o_got, own)


def stacked(value, own_heads, head_size, shift):
    return jnp.concatenate(
        [masked(value, h + shift, head_size) for h in range(own_heads)], axis=0
    )


def unstacked(value, own_heads, head_size, shift):
    rows = value.shape[0] // own_heads
    total = None
    for h in range(own_heads):
        part = masked(value[h * rows : (h + 1) * rows], h + shift, head_size)
        total = part if total is None else total + part
    return total


def column_scales(divisor_ref, own_heads, head_size, query_count):
    first = lax.axis_index("section") * own_heads
    divisors = jnp.concatenate(
        [jnp.full((1, query_count), divisor_ref[first + h], F32) for h in range(own_heads)], axis=1
    )
    return 1.0 / math.sqrt(head_size) / jnp.clip(divisors, 0.5, 2.0)


def caption_ends(texts_ref):
    ends, total = [], 0
    for j in range(texts_ref.shape[1]):
        total = total + texts_ref[0, j]
        ends.append(total)
    return ends


def image_at(ends, item):
    j = 0
    for end in ends:
        j = j + jnp.where(end <= item, 1, 0)
    return jnp.minimum(j, len(ends) - 1)


def patch_rows(padded, patches):
    return lax.broadcasted_iota(jnp.int32, (padded, 1), 0) < patches


def attend_image(rows_of, items, kv_ref, images, mask, scales, own_heads, head_size, shift):
    q = [stacked(rows_of(item), own_heads, head_size, shift) for item in items]
    wide = q[0].shape[1]
    t = [mm_nt(kv_ref[j, :, :wide], one) for j, one in zip(images, q)]
    p = [soft(one, mask, scales).astype(BF) for one in t]
    o = [mm_tn(one, kv_ref[j, :, wide:]) for j, one in zip(images, p)]
    return [unstacked(one, own_heads, head_size, shift).astype(BF) for one in o]


def attend_image_back_kernel(
    patches, own_heads, head_size, query_count, together,
    texts_ref, divisor_ref, q_ref, do_ref, kv_ref, dq_ref, dkv_ref, temper_ref, total_ref,
):
    wide = q_ref.shape[1]
    items = q_ref.shape[0] // query_count
    mask = patch_rows(kv_ref.shape[1], patches)
    scales = column_scales(divisor_ref, own_heads, head_size, query_count)
    shift = lax.axis_index("section") * own_heads * head_size % 128 // head_size
    ends = caption_ends(texts_ref)
    total_ref[...] = jnp.zeros_like(total_ref)
    temper_ref[...] = jnp.zeros_like(temper_ref)

    def step(i, _):
        group = [i * together + b for b in range(together)]
        at = [pl.ds(pl.multiple_of(item * query_count, query_count), query_count) for item in group]
        images = [image_at(ends, item) for item in group]
        q = [stacked(q_ref[one, :], own_heads, head_size, shift) for one in at]
        do = [stacked(do_ref[one, :], own_heads, head_size, shift) for one in at]
        t = [mm_nt(kv_ref[j, :, :wide], one) for j, one in zip(images, q)]
        dp = [mm_nt(kv_ref[j, :, wide:], one) for j, one in zip(images, do)]
        p = [soft(one, mask, scales) for one in t]
        ds = [
            one * (grad - jnp.sum(one * grad, axis=0, keepdims=True)) for one, grad in zip(p, dp)
        ]
        dt = [(one * scales).astype(BF) for one in ds]
        temper = None
        for one, score in zip(ds, t):
            term = jnp.sum(one * score, axis=0, keepdims=True)
            temper = term if temper is None else temper + term
        dq = [mm_tn(one, kv_ref[j, :, :wide]) for one, j in zip(dt, images)]
        dk = [mm(one, rows) for one, rows in zip(dt, q)]
        dv = [mm(one.astype(BF), rows) for one, rows in zip(p, do)]
        for one, rows in zip(at, dq):
            dq_ref[one, :] = unstacked(rows, own_heads, head_size, shift).astype(BF)
        for j, key, val in zip(images, dk, dv):
            total_ref[j, :, :wide] += key
            total_ref[j, :, wide:] += val
        temper_ref[...] += temper
        return 0

    lax.fori_loop(0, items // together, step, 0)
    dkv_ref[...] = total_ref[...].astype(BF)


def pair_columns(total_ref, own):
    s = lax.axis_index("section")
    shift = s * own % 128
    halves = []
    for half in range(2):
        base = half * (total_ref.shape[0] // 2)
        out = total_ref[base : base + own, :]
        for offset in sorted({window(t, own)[1] for t in range(4)} - {0}):
            out = jnp.where(
                shift == offset, total_ref[base + offset : base + offset + own, :], out
            )
        halves.append(out.T.astype(BF))
    return jnp.concatenate(halves, axis=1)


def image_back_kernel(
    query_count, head_size, own_heads,
    texts_ref, divisor_ref, q_ref, do_blocks, da_own, da_other, kv_hbm, images_hbm,
    dq_blocks, da_got, temper_ref, pair_ref,
    do_got, kv, scores, shares, running, sums, blocks, total, last_x, last_kv,
    loads, image_sems, do_sends, do_recvs, da_sends, da_recvs,
):
    s, d = lax.axis_index("section"), lax.axis_index("dp")
    parts, rows, wide = q_ref.shape
    count, patches, feat = images_hbm.shape
    items = rows // query_count
    last = patches - 1
    own = parts * 0 + pair_ref.shape[4] // 2

    def image_pair(j):
        return pltpu.make_async_copy(
            images_hbm.at[pl.ds(2 * j, 2)], blocks.at[j % 2], image_sems.at[j % 2]
        )

    kv_copy = pltpu.make_async_copy(kv_hbm, kv, loads.at[0])
    kv_copy.start()
    image_pair(0).start()
    greet_sections()
    dos = exchange_copies(do_blocks, do_got, do_sends, do_recvs)
    start(dos)
    das = [pltpu.make_async_copy(da_own, da_got.at[s], da_sends.at[0])]
    for bit in range(1, parts):
        das.append(pltpu.make_async_remote_copy(
            src_ref=da_own if bit == 1 else da_other, dst_ref=da_got.at[s],
            send_sem=da_sends.at[bit], recv_sem=da_recvs.at[bit],
            device_id=(s ^ bit, d), device_id_type=MESH,
        ))
    start(das)

    scales = column_scales(divisor_ref, own_heads, head_size, query_count)
    shift = s * own % 128 // head_size
    ends = caption_ends(texts_ref)
    mask = patch_rows(kv.shape[1], patches)
    kv_copy.wait()

    def rows_of(i):
        return pl.ds(pl.multiple_of(i * query_count, query_count), query_count)

    def score(t, _):
        group = range(items)
        images = [image_at(ends, t * items + i) for i in group]
        q = [stacked(q_ref[t, rows_of(i), :], own_heads, head_size, shift) for i in group]
        got = [mm_nt(kv[j, :, :wide], one) for j, one in zip(images, q)]
        p = [soft(one, mask, scales) for one in got]
        for i in group:
            scores[t * items + i] = got[i]
            shares[t * items + i] = p[i]
        return 0

    lax.fori_loop(0, parts, score, 0)
    wait(dos)
    temper_ref[...] = jnp.zeros_like(temper_ref)
    sums[...] = jnp.zeros_like(sums)
    for t in range(parts):

        def back(g, _, t=t):
            group = [g * (items // 2) + i for i in range(items // 2)]
            place = [t * items + i for i in group]
            images = [image_at(ends, at) for at in place]
            same = [image_at(ends, at - 1) == j for at, j in zip(place, images)]
            q = [stacked(q_ref[t, rows_of(i), :], own_heads, head_size, shift) for i in group]
            do = [stacked(do_got[t, rows_of(i), :], own_heads, head_size, shift) for i in group]
            dp = [mm_nt(kv[j, :, wide:], one) for j, one in zip(images, do)]
            p = [shares[at] for at in place]
            ds = [
                one * (grad - jnp.sum(one * grad, axis=0, keepdims=True))
                for one, grad in zip(p, dp)
            ]
            dt = [(one * scales).astype(BF) for one in ds]
            temper = temper_ref[...]
            for one, at in zip(ds, place):
                temper = temper + jnp.sum(one * scores[at], axis=0, keepdims=True)
            temper_ref[...] = temper
            dq = [mm_tn(one, kv[j, :, :wide]) for one, j in zip(dt, images)]
            dk = [mm(one, rows) for one, rows in zip(dt, q)]
            dv = [mm(one.astype(BF), rows) for one, rows in zip(p, do)]
            for i, one in zip(group, dq):
                dq_blocks[t, rows_of(i), :] = unstacked(
                    one, own_heads, head_size, shift
                ).astype(BF)
            for at, again, key, val in zip(place, same, dk, dv):
                key = jnp.where(again, sums[:, :wide], 0.0) + key
                val = jnp.where(again, sums[:, wide:], 0.0) + val
                sums[:, :wide] = key
                sums[:, wide:] = val
                running[at, :, :wide] = key.astype(BF)
                running[at, :, wide:] = val.astype(BF)
            return 0

        lax.fori_loop(0, 2, back, 0)

    total[...] = jnp.zeros_like(total)
    last_x[...] = jnp.zeros_like(last_x)
    last_kv[...] = jnp.zeros_like(last_kv)
    for j in range(count // 2):
        image_pair(j).wait()
        if j + 1 < count // 2:
            image_pair(j + 1).start()
        at = [jnp.clip(ends[2 * j + i] - 1, 0, parts * items - 1) for i in range(2)]
        total[...] += mm_tn(
            jnp.concatenate([running[one, :last, :] for one in at], axis=0),
            blocks[j % 2, :, :last, :].reshape(2 * last, feat),
        )
        for i in range(2):
            row = 2 * j + i
            last_x[row : row + 1, :] = blocks[j % 2, i, last:, :].astype(F32)
            last_kv[row : row + 1, :] = running[at[i], last:patches, :].astype(F32)
    total[...] += mm_tn(last_kv[...].astype(BF), last_x[...].astype(BF))
    turned = pair_columns(total, own)
    r = pair_ref.shape[3]
    for i in range(2 * pair_ref.shape[1]):
        pair_ref[0, i // 2, i % 2] = turned[i * r : (i + 1) * r]

    wait(das)


def keyval_grad_kernel(x_ref, dkv_ref, out_ref, total_ref):
    @pl.when(pl.program_id(0) == 0)
    def _():
        total_ref[...] = jnp.zeros_like(total_ref)

    patches = x_ref.shape[1]
    total_ref[...] += mm_tn(dkv_ref[0, :patches, :], x_ref[0])

    @pl.when(pl.program_id(0) == pl.num_programs(0) - 1)
    def _():
        out_ref[...] = pair_columns(total_ref, out_ref.shape[1] // 2)


def middle_kernel(query_count, head_size, owners, *refs):
    refs = list(refs)

    def take(count):
        out = refs[:count]
        del refs[:count]
        return out

    h1_ref, mixed1_ref, g_ref, dout_hbm = take(4)
    hbm_weights = take(7)
    final_blocks, do_blocks, low3_ref, mixed2_ref, djoined_ref, da4_ref, da2_ref, dz2_ref, dg_ref = take(9)
    if owners:
        x_got, da_own, da_other = take(3)
        low2_ref, m1_ref, du1_ref, da3_ref, low4_ref, m2_ref, du2_ref, da5_ref = take(8)
    else:
        low2_ref, m1_ref, du1_ref, da3_ref, low4_ref, m2_ref, du2_ref, da5_ref = take(8)

    def sort_out(da_ref, which):
        if owners:
            own = lax.axis_index("section") // 2 == which

            @pl.when(own)
            def _():
                da_own[...] = da_ref[...]

            @pl.when(jnp.logical_not(own))
            def _():
                da_other[...] = da_ref[...]

    weights = take(7)
    wx, we1, wr1, wp, wo, we2, wr2 = weights
    dout, sems, owner_sends, owner_recvs = take(4)
    slope1, slope2, joined, do2, n2, r2, n3, r3, n4, r4, n5, r5 = refs
    given = []

    def give(source, which):
        if owners:
            pairs = owner_copies(source, x_got, which, owner_sends, owner_recvs)
            start_if(pairs)
            given.append(pairs)

    copies = [
        pltpu.make_async_copy(src, dst, sems.at[i])
        for i, (src, dst) in enumerate(zip(hbm_weights, weights))
    ]
    for copy in copies:
        copy.start()
    items = dout.shape[0]
    dout_copy = pltpu.make_async_copy(
        dout_hbm.at[pl.ds(lax.axis_index("section") * items, items)], dout, sems.at[len(copies)]
    )
    dout_copy.start()
    if owners:
        greet_sections()
    copies[0].wait()
    h2 = norm_into(h1_ref[...] + mm(mixed1_ref[...], wx[...]), g_ref[1:2, :], n2, r2)
    low2_ref[...] = h2.astype(BF)
    give(low2_ref, 0)
    copies[1].wait()
    copies[2].wait()
    a = hidden_forward(low2_ref[...], we1, wr1, m1_ref, slope1)
    h3 = norm_into(n2[...] * g_ref[1:2, :] + a, g_ref[2:3, :], n3, r3)
    low3_ref[...] = h3.astype(BF)
    copies[3].wait()
    project_into(joined, low3_ref[...], wp)
    attend_self(joined, mixed2_ref, query_count, head_size)
    copies[4].wait()
    a = mm(mixed2_ref[...], wo[...])
    h4 = norm_into(n3[...] * g_ref[2:3, :] + a, g_ref[3:4, :], n4, r4)
    low4_ref[...] = h4.astype(BF)
    give(low4_ref, 1)
    copies[5].wait()
    copies[6].wait()
    a = hidden_forward(low4_ref[...], we2, wr2, m2_ref, slope2)
    h5 = norm_into(n4[...] * g_ref[3:4, :] + a, g_ref[4:5, :], n5, r5)
    put_blocks(final_blocks, h5.astype(BF))
    dout_copy.wait()

    dz, dg4 = norm_back(
        dout[...].reshape(n5.shape).astype(F32), g_ref[4:5, :], n5[...], r5[...]
    )
    da5_ref[...] = dz.astype(BF)
    sort_out(da5_ref, 1)
    d4 = dz + hidden_backward(da5_ref[...], we2, wr2, slope2, du2_ref)

    dz, dg3 = norm_back(d4, g_ref[3:4, :], n4[...], r4[...])
    da4_ref[...] = dz.astype(BF)
    do2[...] = mm_nt(da4_ref[...], wo[...]).astype(BF)
    attend_self_back(joined, do2, djoined_ref, query_count, head_size)
    d3 = dz + back_through(djoined_ref, wp)

    dz, dg2 = norm_back(d3, g_ref[2:3, :], n3[...], r3[...])
    da3_ref[...] = dz.astype(BF)
    sort_out(da3_ref, 0)
    d2 = dz + hidden_backward(da3_ref[...], we1, wr1, slope1, du1_ref)

    dz, dg1 = norm_back(d2, g_ref[1:2, :], n2[...], r2[...])
    dz2_ref[...] = dz
    da2_ref[...] = dz.astype(BF)
    put_blocks(do_blocks, mm_nt(da2_ref[...], wx[...]).astype(BF))
    dg_ref[...] = jnp.concatenate([d[None, :] for d in (dg1, dg2, dg3, dg4)], axis=0)
    for pairs in given:
        sent_if(pairs)
    if owners:
        received(x_got, owner_sends, owner_recvs)


def last_kernel(
    query_count, head_size, dz2_ref, dq_ref, wq_ref, n_ref, r_ref, g_ref, wo_ref, joined_ref, wp_ref,
    dqr_ref, da_ref, djoined_ref, dx_ref, dg_ref, do,
):
    own = wq_ref.shape[1] // dq_ref.shape[0]
    dqr_ref[...] = take_blocks(dq_ref, own)
    d1 = dz2_ref[...] + mm_nt(dqr_ref[...], wq_ref[...])
    dz, dg = norm_back(d1, g_ref[0:1, :], n_ref[...], r_ref[...])
    dg_ref[...] = dg[None, :]
    da_ref[...] = dz.astype(BF)
    do[...] = mm_nt(da_ref[...], wo_ref[...]).astype(BF)
    attend_self_back(joined_ref, do, djoined_ref, query_count, head_size)
    put_blocks(dx_ref, (dz + back_through(djoined_ref, wp_ref)).astype(BF))


def weight_kernel(x_ref, dy_ref, out_ref):
    out_ref[0] = mm_tn(x_ref[...], dy_ref[...]).astype(BF)


def pair_weight_kernel(x_ref, dy_ref, y_ref, dz_ref, out_ref):
    parts = out_ref.shape[0]
    own_a, own_b = dy_ref.shape[1] // parts, dz_ref.shape[1] // parts
    for t in range(parts):
        a = mm_tn(x_ref[...], dy_ref[:, t * own_a : (t + 1) * own_a]).astype(BF)
        b = mm_tn(y_ref[...], dz_ref[:, t * own_b : (t + 1) * own_b]).astype(BF)
        out_ref[t] = jnp.concatenate([a, b], axis=1)


def turned_weight_kernel(dy_ref, x_ref, out_ref):
    _, dp, own, wide = out_ref.shape
    r = mm_tn(dy_ref[...], x_ref[...]).astype(BF)
    for d in range(dp):
        out_ref[0, d] = r[:, d * wide : (d + 1) * wide]


def deliver_kernel(own, *refs):
    count = len(refs) // 2
    given, out = refs[:count], refs[count:]
    shift = lax.axis_index("section") * own % 128
    parts, rows, _ = given[0].shape
    for source, target in zip(given[:2], out[:2]):
        for t in range(parts):
            block = source[t].astype(F32)
            cut = block[:, :own]
            for offset in sorted({window(i, own)[1] for i in range(parts)} - {0}):
                cut = jnp.where(shift == offset, block[:, offset : offset + own], cut)
            target[t * rows : (t + 1) * rows, :] = cut
    for source, target in zip(given[2:], out[2:]):
        target[...] = source[...] if source.shape == target.shape else source[...].T


def shape(dims, dtype):
    return jax.ShapeDtypeStruct(tuple(dims), dtype)


def call(kernel, outs, *args, in_specs=None, scratch=(), flops=0):
    return pl.pallas_call(
        kernel,
        out_shape=outs,
        in_specs=in_specs or [whole()] * len(args),
        out_specs=jax.tree.map(lambda _: whole(), outs),
        scratch_shapes=list(scratch),
        compiler_params=pltpu.CompilerParams(vmem_limit_bytes=LIMIT),
        cost_estimate=pl.CostEstimate(
            flops=flops, bytes_accessed=int(flops) // 400, transcendentals=0
        ),
    )(*args)


def expand_grad(low, du, parts):
    rows, width = low.shape
    own = du.shape[1] // parts
    return pl.pallas_call(
        weight_kernel,
        out_shape=shape((parts, width, own), BF),
        grid=(parts,),
        in_specs=[
            pl.BlockSpec((rows, width), lambda t: (0, 0)),
            pl.BlockSpec((rows, own), lambda t: (0, t)),
        ],
        out_specs=pl.BlockSpec((1, width, own), lambda t: (t, 0, 0)),
        compiler_params=pltpu.CompilerParams(vmem_limit_bytes=LIMIT),
    )(low, du)


def reduce_grad(da, m, parts, dp):
    rows, width = da.shape
    wide = m.shape[1] // dp
    own = width // parts
    per = 4 if dp % 4 == 0 and (dp // 4 * wide) % 128 == 0 else 1
    blocks = dp // per
    return pl.pallas_call(
        functools.partial(turned_weight_all_kernel, parts),
        out_shape=shape((parts, dp, own, wide), BF),
        grid=(per,),
        in_specs=[
            pl.BlockSpec((rows, width), lambda b: (0, 0)),
            pl.BlockSpec((rows, blocks * wide), lambda b: (0, b)),
        ],
        out_specs=pl.BlockSpec((parts, blocks, own, wide), lambda b: (0, b, 0, 0)),
        compiler_params=pltpu.CompilerParams(vmem_limit_bytes=LIMIT),
    )(da, m)


def turned_weight_all_kernel(parts, dy_ref, x_ref, out_ref):
    _, blocks, own, wide = out_ref.shape
    r = mm_tn(dy_ref[...], x_ref[...]).astype(BF)
    for t in range(parts):
        for d in range(blocks):
            out_ref[t, d] = r[t * own : (t + 1) * own, d * wide : (d + 1) * wide]


def device_of(section, z, core):
    return (section, z * 2 + core)


class Home:
    def __init__(self, unit, kept, from_x, from_y, then_x, then_y, from_z, sends, recvs):
        self.unit, self.kept = unit, kept
        self.from_x, self.from_y = from_x, from_y
        self.then_x, self.then_y = then_x, then_y
        self.from_z = from_z
        self.sends, self.recvs = sends, recvs
        self.s, d = lax.axis_index("section"), lax.axis_index("dp")
        self.sx, self.sy = self.s % 2, self.s // 2
        self.z, self.c = d // 2, d % 2
        self.half = kept.shape[2] // 2

    def copy(self, i, src, dst, device):
        return pltpu.make_async_remote_copy(
            src_ref=src, dst_ref=dst, send_sem=self.sends.at[i], recv_sem=self.recvs.at[i],
            device_id=device, device_id_type=MESH,
        )

    def mine(self):
        return self.s if self.kept.shape[0] > 1 else 0

    def cores(self):
        return [
            self.copy(
                0, self.unit.at[:, :, 1 - self.c], self.kept, device_of(self.s, self.z, 1 - self.c)
            )
        ]

    def first(self):
        s, sx, sy, z, c, half = self.s, self.sx, self.sy, self.z, self.c, self.half
        out = []
        for i in range(2):
            out.append(self.copy(
                1 + i, self.kept.at[2 * i + 1 - sx, :, :half], self.from_x.at[i],
                device_of(s + 1 - 2 * sx, z, c),
            ))
            out.append(self.copy(
                3 + i, self.kept.at[2 * (1 - sy) + i, :, half:], self.from_y.at[i],
                device_of(s + 2 - 4 * sy, z, c),
            ))
        return out

    def second(self):
        s, sx, sy, z, c, half = self.s, self.sx, self.sy, self.z, self.c, self.half
        return [
            self.copy(
                5, self.kept.at[2 * (1 - sy) + sx, :, :half], self.then_y,
                device_of(s + 2 - 4 * sy, z, c),
            ),
            self.copy(
                6, self.kept.at[2 * sy + 1 - sx, :, half:], self.then_x,
                device_of(s + 1 - 2 * sx, z, c),
            ),
        ]

    def pairs(self):
        out = []
        for i in range(2):
            at = 2 * i + 1 - self.z % 2
            out.append(self.copy(
                7 + i, self.kept.at[self.mine(), at], self.from_z.at[i],
                device_of(self.s, self.z + 1 - 2 * (self.z % 2), self.c),
            ))
        return out

    def across(self):
        at = (self.z + 2) % 4
        return [
            self.copy(
                9, self.kept.at[self.mine(), at], self.from_z.at[2],
                device_of(self.s, at, self.c),
            )
        ]

    def add_pairs(self):
        for i in range(2):
            at = 2 * i + self.z % 2
            self.kept[self.mine(), at] = self.kept[self.mine(), at] + self.from_z[i]

    def add_cores(self):
        n = self.kept.shape[1]

        def step(i, _):
            t, z = i // n, i % n
            self.kept[t, z] = self.kept[t, z] + self.unit[t, z, self.c]
            return 0

        lax.fori_loop(0, self.kept.shape[0] * n, step, 0)

    def add_first(self):
        n, half = self.kept.shape[1], self.half

        def step(i, _):
            t, z = i // n, i % n
            x, y = 2 * t + self.sx, 2 * self.sy + t
            self.kept[x, z, :half] = self.kept[x, z, :half] + self.from_x[t, z]
            self.kept[y, z, half:] = self.kept[y, z, half:] + self.from_y[t, z]
            return 0

        lax.fori_loop(0, 2 * n, step, 0)

    def add_second(self):
        n, half = self.kept.shape[1], self.half

        def step(z, _):
            self.kept[self.s, z, :half] = self.kept[self.s, z, :half] + self.then_y[z]
            self.kept[self.s, z, half:] = self.kept[self.s, z, half:] + self.then_x[z]
            return 0

        lax.fori_loop(0, n, step, 0)

    def total(self):
        return self.kept[self.mine(), self.z].astype(F32) + self.from_z[2].astype(F32)


def greet():
    s, d = lax.axis_index("section"), lax.axis_index("dp")
    sections, dp = lax.axis_size("section"), lax.axis_size("dp")
    n = dp // 2
    z, c = d // 2, d % 2
    barrier = pltpu.get_barrier_semaphore()
    near = [device_of(s, z, 1 - c)]
    for bit in range(1, sections):
        near.append(device_of(s ^ bit, z, c))
        near.append(device_of(s ^ bit, z, 1 - c))
    for k in range(1, n):
        near.append(device_of(s, (z + k) % n, c))
    for device in near:
        pl.semaphore_signal(barrier, inc=1, device_id=device, device_id_type=MESH)
    pl.semaphore_wait(barrier, len(near))


def fill_pair(unit, x, dy, y, dz):
    parts, n, two, r, w = unit.shape
    own_a, own_b = dy.shape[1] // parts, dz.shape[1] // parts
    for t in range(parts):
        a = mm_tn(x[...], dy[:, t * own_a : (t + 1) * own_a]).astype(BF)
        b = mm_tn(y[...], dz[:, t * own_b : (t + 1) * own_b]).astype(BF)
        g = jnp.concatenate([a, b], axis=1)
        for d in range(2 * n):
            unit[t, d // 2, d % 2] = g[d * r : (d + 1) * r]


class Owned:
    def __init__(self, refs, expand1, reduce1, expand2, reduce2):
        (self.e_unit, self.r_unit, self.e_kept, self.r_kept, self.e_pair, self.e_across,
         self.r_pair, self.r_across, self.e_low, self.r_low, self.e_got, self.r_got,
         self.loads, self.cores, self.e_z, self.r_z, self.homes) = refs
        self.out = (expand1, reduce1, expand2, reduce2)
        self.s, d = lax.axis_index("section"), lax.axis_index("dp")
        self.d, self.z, self.c = d, d // 2, d % 2
        self.h, self.p = self.s % 2, self.z % 2
        self.n = self.e_unit.shape[0]

    def load(self, x_got, da_got, we1, wr1, we2, wr2, held):
        self.x, self.da, self.xt, self.we, self.wr, self.m, self.du = held
        wide = self.we.shape[2]
        rows = [pltpu.make_async_copy(x_got, self.x, self.loads.at[0])]
        rows.append(pltpu.make_async_copy(da_got, self.da, self.loads.at[1]))
        start(rows)
        for which, (we, wr) in enumerate(((we1, wr1), (we2, wr2))):
            copies = []
            for i in range(self.n):
                at = pl.multiple_of((2 * i + self.h) * wide, 128)
                copies.append(
                    pltpu.make_async_copy(
                        we.at[:, pl.ds(at, wide)], self.we.at[i], self.loads.at[2 + 2 * i]
                    )
                )
                copies.append(
                    pltpu.make_async_copy(
                        wr.at[pl.ds(at, wide), :], self.wr.at[i], self.loads.at[3 + 2 * i]
                    )
                )

            @pl.when(self.s // 2 == which)
            def _(copies=copies):
                start(copies)

        self.copies = rows + copies

    def loaded(self):
        wait(self.copies)
        for t in range(self.x.shape[0]):
            rows = self.x.shape[1]
            self.xt[:, t * rows : (t + 1) * rows] = self.x[t].T

    def core_e(self, i):
        return pltpu.make_async_remote_copy(
            src_ref=self.e_unit.at[i, :, :, 1 - self.c], dst_ref=self.e_kept.at[i],
            send_sem=self.cores.at[0, i], recv_sem=self.cores.at[1, i],
            device_id=(self.s, self.z * 2 + 1 - self.c), device_id_type=MESH,
        )

    def core_r(self, i):
        rows = self.r_kept.shape[1]
        at = pl.ds(pl.multiple_of((1 - self.c) * rows, rows), rows)
        return pltpu.make_async_remote_copy(
            src_ref=self.r_unit.at[i, at], dst_ref=self.r_kept.at[i],
            send_sem=self.cores.at[2, i], recv_sem=self.cores.at[3, i],
            device_id=(self.s, self.z * 2 + 1 - self.c), device_id_type=MESH,
        )

    def pairs_e(self, i):
        return pltpu.make_async_remote_copy(
            src_ref=self.e_kept.at[i, :, 1 - self.p], dst_ref=self.e_pair.at[i],
            send_sem=self.e_z.at[0, i], recv_sem=self.e_z.at[1, i],
            device_id=(self.s, (self.z + 1 - 2 * self.p) * 2 + self.c), device_id_type=MESH,
        )

    def across_e(self, i):
        return pltpu.make_async_remote_copy(
            src_ref=self.e_kept.at[i, 1 - self.z // 2, self.p], dst_ref=self.e_across.at[i],
            send_sem=self.e_z.at[2, i], recv_sem=self.e_z.at[3, i],
            device_id=(self.s, (self.z + 2) % 4 * 2 + self.c), device_id_type=MESH,
        )

    def pairs_r(self, i):
        return pltpu.make_async_remote_copy(
            src_ref=self.r_kept.at[i], dst_ref=self.r_pair.at[i // 2],
            send_sem=self.r_z.at[0, i], recv_sem=self.r_z.at[1, i // 2],
            device_id=(self.s, (self.z + 1 - 2 * self.p) * 2 + self.c), device_id_type=MESH,
        )

    def across_r(self, i):
        return pltpu.make_async_remote_copy(
            src_ref=self.r_kept.at[i], dst_ref=self.r_across,
            send_sem=self.r_z.at[2, i // 2], recv_sem=self.r_z.at[3, 0],
            device_id=(self.s, (self.z + 2) % 4 * 2 + self.c), device_id_type=MESH,
        )

    def make(self, i):
        parts, rows, width = self.x.shape
        wide = self.we.shape[2]

        def rows_of(t, _):
            u = mm(self.x[t], self.we[i]).astype(BF).astype(F32)
            m, slope = gelu_both(u)
            at = pl.ds(pl.multiple_of(t * rows, rows), rows)
            self.m[at, :] = m.astype(BF)
            self.du[at, :] = (mm_nt(self.da[t], self.wr[i]) * slope).astype(BF)
            return 0

        lax.fori_loop(0, parts, rows_of, 0)
        r = self.e_unit.shape[4]

        def columns_of(z, _):
            at = pl.ds(pl.multiple_of(z * 2 * r, 2 * r), 2 * r)
            g = mm(self.xt[at, :], self.du[...]).astype(BF)
            for c in range(2):
                self.e_unit[i, z // 2, z % 2, c] = g[c * r : (c + 1) * r]
            return 0

        lax.fori_loop(0, self.n, columns_of, 0)
        self.core_e(i).start()
        for at in range(0, width, 256):
            self.r_unit[i, :, at : at + 256] = mm_tn(
                self.m[...], self.da[:, :, at : at + 256].reshape(parts * rows, 256)
            ).astype(BF)
        self.core_r(i).start()

    def over_cores(self, i):
        self.core_e(i).wait()

        def step(z, _):
            at = (i, z // 2, z % 2)
            self.e_kept[at] = self.e_kept[at] + self.e_unit[(*at, self.c)]
            return 0

        lax.fori_loop(0, self.n, step, 0)
        self.pairs_e(i).start()
        self.core_r(i).wait()
        rows = self.r_kept.shape[1]
        own = pl.ds(pl.multiple_of(self.c * rows, rows), rows)
        self.r_kept[i] = self.r_kept[i] + self.r_unit[i, own]
        pl.when(self.p != i % 2)(self.pairs_r(i).start)

    def over_pairs(self, i):
        self.pairs_e(i).wait()
        for t in range(2):
            self.e_kept[i, t, self.p] = self.e_kept[i, t, self.p] + self.e_pair[i, t]
        self.across_e(i).start()
        pl.when(self.p != i % 2)(self.pairs_r(i).wait_send)

        @pl.when(self.p == i % 2)
        def _():
            self.pairs_r(i).wait_recv()
            self.r_kept[i] = self.r_kept[i] + self.r_pair[i // 2]

        pl.when((self.p == i % 2) & (self.z != i))(self.across_r(i).start)

    def home_e(self, t):
        return pltpu.make_async_remote_copy(
            src_ref=self.e_low.at[t], dst_ref=self.e_got.at[self.s],
            send_sem=self.homes.at[0, t], recv_sem=self.homes.at[1, self.s],
            device_id=(t, self.d), device_id_type=MESH,
        )

    def home_r(self, t):
        return pltpu.make_async_remote_copy(
            src_ref=self.r_low.at[t], dst_ref=self.r_got.at[self.s // 2, self.c],
            send_sem=self.homes.at[2, t], recv_sem=self.homes.at[3, self.s // 2 * 2 + self.c],
            device_id=(t, self.z * 2 + self.h), device_id_type=MESH,
        )

    def over_z_e(self):
        for i in range(self.n):
            self.across_e(i).wait()
            total = self.e_kept[i, self.z // 2, self.p].astype(F32) + self.e_across[i].astype(F32)
            self.e_low[i] = total.astype(BF)

            @pl.when(self.s == i)
            def _(i=i):
                self.e_got[i] = self.e_low[i]

            pl.when(self.s != i)(self.home_e(i).start)

    def over_z_r(self):
        parts, rows, wide = self.r_low.shape
        own = self.r_kept.shape[2] // parts
        for i in range(self.n):
            pl.when((self.p == i % 2) & (self.z != i))(self.across_r(i).wait_send)
        self.across_r(0).wait_recv()
        step = rows // 2
        for at in range(0, rows, step):
            total = self.r_kept[self.z, at : at + step].astype(F32)
            total = (total + self.r_across[at : at + step].astype(F32)).astype(BF)
            for t in range(parts):
                low, _ = window(t, own)
                self.r_low[t, at : at + step] = total[:, low : low + wide]
        for t in range(parts):
            stays = (self.s == t) & (self.c == self.h)
            pl.when(jnp.logical_not(stays))(self.home_r(t).start)

            @pl.when(stays)
            def _(t=t):
                self.r_got[self.s // 2, self.c] = self.r_low[t]

    def finish(self):
        parts = self.e_low.shape[0]
        for t in range(parts):
            pl.when(self.s != t)(self.home_e(t).wait_send)
            stays = (self.s == t) & (self.c == self.h)
            pl.when(jnp.logical_not(stays))(self.home_r(t).wait_send)
        for t in range(parts):
            copy = pltpu.make_async_remote_copy(
                src_ref=self.e_low.at[0], dst_ref=self.e_got.at[t],
                send_sem=self.homes.at[0, 0], recv_sem=self.homes.at[1, t],
                device_id=(self.s ^ 1, self.d), device_id_type=MESH,
            )
            pl.when(self.s != t)(copy.wait_recv)
        for which in range(2):
            for core in range(2):
                copy = pltpu.make_async_remote_copy(
                    src_ref=self.r_low.at[0], dst_ref=self.r_got.at[which, core],
                    send_sem=self.homes.at[2, 0], recv_sem=self.homes.at[3, 2 * which + core],
                    device_id=(self.s ^ 1, self.d), device_id_type=MESH,
                )
                stays = (self.s == 2 * which + self.c) & (self.c == core)
                pl.when(jnp.logical_not(stays))(copy.wait_recv)
        wide = self.e_got.shape[2]
        own = self.out[1].shape[1]
        shift = self.s * own % 128
        for which in range(2):
            expand, reduce = self.out[2 * which : 2 * which + 2]
            for h in range(2):
                expand[:, h * wide : (h + 1) * wide] = self.e_got[2 * which + h].astype(F32)
            for core in range(2):
                block = self.r_got[which, core].astype(F32)
                out = block[:, :own]
                for offset in sorted({window(t, own)[1] for t in range(parts)} - {0}):
                    out = jnp.where(shift == offset, block[:, offset : offset + own], out)
                reduce[core * block.shape[0] : (core + 1) * block.shape[0], :] = out


def tail_kernel(query_count, head_size, *refs):
    refs = list(refs)

    def take(count):
        out = refs[:count]
        del refs[:count]
        return out

    final_blocks, dq_blocks = take(2)
    x_got, da_got, we1, wr1, we2, wr2 = take(6)
    low3, djoined2, mixed2, da4 = take(4)
    low1, mixed1, da2, x0, mixed_self1 = take(5)
    wq_hbm, wo_hbm, wp_hbm = take(3)
    pair_unit, dz2, n1, r1, gains, joined1, dg_mid, temper_rows = take(8)
    final_got, dx_got, small = take(3)
    expand2, reduce2, project2, out2, expand1, reduce1, asker, image_out, project1, out1 = take(10)
    pair_out = take(1)[0]
    units = ("self2", "self1", "image")
    buffers = {name: take(6) for name in units}
    pair_kept, pair_from_z, pair_low, pair_got = take(4)
    wide, sends, recvs, slots_a, slots_b, slots_c, slots_d, loads = take(8)
    slots = (slots_a, slots_b, slots_c, slots_d)
    dq_got, dqr, da1, djoined1, dx_blocks, sums, state_sends, state_recvs, local = take(9)
    owned = Owned(refs, expand1, reduce1, expand2, reduce2)
    own_heads = temper_rows.shape[1] // query_count

    s, d = lax.axis_index("section"), lax.axis_index("dp")
    z, c = d // 2, d % 2

    homes = {}
    for i, name in enumerate(units):
        unit = wide.at[:, :, :, :, : buffers[name][0].shape[3]]
        homes[name] = Home(unit, *buffers[name], sends.at[i], recvs.at[i])
    homes["pair"] = Home(
        pair_unit, pair_kept, None, None, None, None, pair_from_z,
        sends.at[len(units)], recvs.at[len(units)],
    )
    factors = {
        "self2": (low3, djoined2, mixed2, da4), "self1": (x0, djoined1, mixed_self1, da1),
        "image": (low1, dqr, mixed1, da2),
    }
    results = {
        "self2": (project2, out2), "self1": (project1, out1), "image": (asker, image_out),
    }

    def held(name):
        return [
            slots[j].at[:, : source.shape[1]] for j, source in enumerate(factors[name])
        ]

    def fetch(name):
        return [
            pltpu.make_async_copy(source, target, loads.at[units.index(name), j])
            for j, (source, target) in enumerate(zip(factors[name], held(name)))
        ]

    def make(name):
        wait(fetch(name))
        fill_pair(homes[name].unit, *held(name))
        start(homes[name].cores())

    def finish(name):
        wait(homes[name].across())
        total = homes[name].total()
        out = results[name]
        own = out[0].shape[1]
        out[0][...] = total[:, :own]
        out[1][...] = total[:, own:]

    steps = [("dp", 1), ("section", 1), ("section", 2)]
    bit = 2
    while bit < lax.axis_size("dp"):
        steps.append(("dp", bit))
        bit *= 2

    def small_copy(k):
        axis, bit = steps[k]
        to = (s ^ bit, d) if axis == "section" else (s, d ^ bit)
        return [pltpu.make_async_remote_copy(
            src_ref=small, dst_ref=sums.at[k], send_sem=state_sends.at[8 + k],
            recv_sem=state_recvs.at[8 + k], device_id=to, device_id_type=MESH,
        )]

    def small_step(k):
        if k > 0:
            wait(small_copy(k - 1))
            small[...] = small[...] + sums[k - 1]
        if k < len(steps):
            start(small_copy(k))

    finals = exchange_copies(
        final_blocks, final_got, state_sends.at[pl.ds(0, 4)], state_recvs.at[pl.ds(0, 4)]
    )
    dqs = exchange_copies(
        dq_blocks, dq_got, state_sends.at[pl.ds(4, 4)], state_recvs.at[pl.ds(4, 4)]
    )
    dxs = exchange_copies(dx_blocks, dx_got, state_sends.at[pl.ds(16, 4)], state_recvs.at[pl.ds(16, 4)])

    def rest_of_states(wq, wo, wp, do):
        own = wq.shape[1] // dq_got.shape[0]
        wait(dqs)
        wait([pltpu.make_async_copy(*one) for one in
              ((wq_hbm, wq, local.at[0]), (wo_hbm, wo, local.at[1]), (wp_hbm, wp, local.at[2]))])
        dqr[...] = take_blocks(dq_got, own)
        d1 = dz2[...] + mm_nt(dqr[...], wq[...])
        dz, dg = norm_back(d1, gains[0:1, :], n1[...], r1[...])
        da1[...] = dz.astype(BF)
        do[...] = mm_nt(da1[...], wo[...]).astype(BF)
        attend_self_back(joined1, do, djoined1, query_count, head_size)
        put_blocks(dx_blocks, (dz + back_through(djoined1, wp)).astype(BF))
        width = small.shape[1]
        lane = lax.broadcasted_iota(jnp.int32, (1, width), 1)
        row = jnp.zeros((1, width), F32)
        for h in range(own_heads):
            one = jnp.sum(
                jnp.where(head_lanes(temper_rows.shape, h, query_count), temper_rows[...], 0.0),
                keepdims=True,
            )
            row = row + jnp.where(lane == s * own_heads + h, one, 0.0)
        small[...] = jnp.concatenate(
            [dg[None, :], dg_mid[...], row, jnp.zeros((2, width), F32)], axis=0
        )

    def pair_copy(half):
        to = 2 * half + s // 2
        return to, pltpu.make_async_remote_copy(
            src_ref=pair_low.at[half], dst_ref=pair_got.at[s % 2],
            send_sem=state_sends.at[20 + half], recv_sem=state_recvs.at[20 + s % 2],
            device_id=(to, d), device_id_type=MESH,
        )

    def send_pair():
        wait(homes["pair"].across())
        total = homes["pair"].total().astype(BF)
        own = total.shape[1] // 2
        for half in range(2):
            pair_low[half] = total[:, half * own : (half + 1) * own]
            to, copy = pair_copy(half)

            @pl.when(to != s)
            def _(copy=copy):
                copy.start()

            @pl.when(to == s)
            def _(half=half):
                pair_got[s % 2] = pair_low[half]

    def finish_pair():
        for half in range(2):
            to, copy = pair_copy(half)

            @pl.when(to != s)
            def _(copy=copy):
                copy.wait_send()

        for j in range(2):
            source = 2 * (s % 2) + j

            @pl.when(source != s)
            def _(j=j):
                pltpu.make_async_remote_copy(
                    src_ref=pair_low.at[0], dst_ref=pair_got.at[j],
                    send_sem=state_sends.at[20], recv_sem=state_recvs.at[20 + j],
                    device_id=(s ^ 1, d), device_id_type=MESH,
                ).wait_recv()

        own = pair_got.shape[2]
        for j in range(2):
            pair_out[:, j * own : (j + 1) * own] = pair_got[j].astype(F32)

    def over_cores(name):
        wait(homes[name].cores())
        homes[name].add_cores()
        start(homes[name].first())

    def over_first(name):
        wait(homes[name].first())
        homes[name].add_first()
        start(homes[name].second())

    def over_second(name):
        wait(homes[name].second())
        homes[name].add_second()
        start(homes[name].pairs())

    def over_pairs(name):
        wait(homes[name].pairs())
        homes[name].add_pairs()
        start(homes[name].across())

    parts, rows, width = x_got.shape
    block = we1.shape[1] // lax.axis_size("dp")
    n = owned.n
    start(fetch("self2"))

    def first_part(wq, wo, wp, do, *held):
        owned.load(x_got, da_got, we1, wr1, we2, wr2, held)
        start([pltpu.make_async_copy(*one) for one in
               ((wq_hbm, wq, local.at[0]), (wo_hbm, wo, local.at[1]), (wp_hbm, wp, local.at[2]))])
        greet()
        owned.loaded()
        start(homes["pair"].cores())
        start(finals)
        owned.make(0)
        start(dqs)
        wait(homes["pair"].cores())
        homes["pair"].add_cores()
        start(homes["pair"].pairs())
        make("self2")
        owned.make(1)
        owned.over_cores(0)
        over_pairs("pair")
        over_cores("self2")
        owned.make(2)
        owned.over_cores(1)
        rest_of_states(wq, wo, wp, do)
        start(fetch("self1"))
        owned.over_cores(2)
        small_step(0)
        over_first("self2")
        make("self1")
        start(fetch("image"))
        send_pair()
        owned.over_pairs(1)
        owned.over_pairs(2)
        over_second("self2")
        small_step(1)
        over_cores("self1")
        owned.make(3)
        wait(finals)
        make("image")
        owned.over_cores(3)
        over_cores("image")
        owned.over_pairs(0)
        over_pairs("self2")
        over_first("self1")
        over_first("image")
        owned.over_pairs(3)
        owned.over_z_r()
        small_step(2)
        over_second("self1")
        over_second("image")
        owned.over_z_e()
        finish("self2")
        small_step(3)
        over_pairs("self1")
        start(dxs)
        over_pairs("image")
        small_step(4)
        finish_pair()
        owned.finish()
        finish("self1")
        small_step(5)
        finish("image")
        wait(dxs)

    pl.run_scoped(
        first_part, *[pltpu.VMEM(w.shape, BF) for w in (wq_hbm, wo_hbm, wp_hbm)],
        pltpu.VMEM(da1.shape, BF),
        *[
            pltpu.VMEM(dims, BF)
            for dims in (
                (parts, rows, width), (parts, rows, width), (width, parts * rows),
                (n, width, block), (n, block, width),
                (parts * rows, block), (parts * rows, block),
            )
        ],
    )


def tail(operands, sections, dp, width, hidden, feat, query_count, head_size):
    n = dp // 2
    rows, most = operands[8].shape[0], operands[9].shape[1]
    r, own, wide_own = width // dp, width // sections, hidden // sections
    lanes = operands[0].shape[2]
    pair_r, pair_w = feat // dp, 2 * own

    def buffers(w):
        return [
            pltpu.VMEM((sections, n, r, w), BF),
            pltpu.VMEM((2, n, r // 2, w), BF), pltpu.VMEM((2, n, r // 2, w), BF),
            pltpu.VMEM((n, r // 2, w), BF), pltpu.VMEM((n, r // 2, w), BF),
            pltpu.VMEM((n - 1, r, w), BF),
        ]

    results = [
        shape((sections, rows, lanes), BF), shape((sections, rows, lanes), BF),
        shape((8, width), F32),
        shape((r, wide_own), F32), shape((hidden // dp, own), F32),
        shape((r, 3 * own), F32), shape((r, own), F32),
        shape((r, wide_own), F32), shape((hidden // dp, own), F32),
        shape((r, own), F32), shape((r, own), F32),
        shape((r, 3 * own), F32), shape((r, own), F32),
        shape((pair_r, pair_w), F32),
    ]
    scratch = []
    for w in (4 * own,) * 2 + (2 * own,):
        scratch += buffers(w)
    scratch += [
        pltpu.VMEM((1, n, pair_r, pair_w), BF),
        pltpu.VMEM((n - 1, pair_r, pair_w), BF),
        pltpu.VMEM((2, pair_r, own), BF), pltpu.VMEM((2, pair_r, own), BF),
        pltpu.VMEM((sections, n, 2, r, 4 * own), BF),
        pltpu.SemaphoreType.DMA((8, 10)), pltpu.SemaphoreType.DMA((8, 10)),
        pltpu.VMEM((rows, width), BF), pltpu.VMEM((rows, most), BF),
        pltpu.VMEM((rows, width), BF), pltpu.VMEM((rows, width), BF),
        pltpu.SemaphoreType.DMA((8, 4)),
        pltpu.VMEM((sections, rows, lanes), BF),
        pltpu.VMEM((rows, width), BF), pltpu.VMEM((rows, width), BF),
        pltpu.VMEM((rows, 3 * width), BF), pltpu.VMEM((sections, rows, lanes), BF),
        pltpu.VMEM((8, 8, width), F32),
        pltpu.SemaphoreType.DMA((24,)), pltpu.SemaphoreType.DMA((24,)),
        pltpu.SemaphoreType.DMA((6,)),
    ]
    block = hidden // dp
    scratch += [
        pltpu.VMEM((n, 2, 2, 2, r, block), BF), pltpu.VMEM((n, block, width), BF),
        pltpu.VMEM((n, 2, 2, r, block), BF), pltpu.VMEM((n, block // 2, width), BF),
        pltpu.VMEM((n, 2, r, block), BF), pltpu.VMEM((n, r, block), BF),
        pltpu.VMEM((2, block // 2, width), BF), pltpu.VMEM((block // 2, width), BF),
        pltpu.VMEM((n, r, block), BF), pltpu.VMEM((sections, block // 2, lanes), BF),
        pltpu.VMEM((sections, r, block), BF), pltpu.VMEM((2, 2, block // 2, lanes), BF),
        pltpu.SemaphoreType.DMA((2 + 2 * n + sections,)), pltpu.SemaphoreType.DMA((4, n)),
        pltpu.SemaphoreType.DMA((4, n)), pltpu.SemaphoreType.DMA((4, n)),
        pltpu.SemaphoreType.DMA((4, sections)),
    ]
    return pl.pallas_call(
        functools.partial(tail_kernel, query_count, head_size),
        out_shape=results,
        in_specs=[whole(pl.ANY)] * 20 + [whole()] * 8,
        out_specs=[whole(pl.ANY)] * 2 + [whole()] * 12,
        scratch_shapes=scratch,
        compiler_params=pltpu.CompilerParams(
            vmem_limit_bytes=LIMIT, collective_id=2, has_side_effects=True
        ),
    )(*operands)


def body(
    starting_learned_vectors,
    frozen_picture_vectors,
    texts_per_picture,
    early_triple_matrix,
    early_mixing_exit_matrix,
    picture_asker_matrix,
    picture_pair_matrix,
    picture_exit_matrix,
    early_widen_matrix,
    early_narrow_matrix,
    later_triple_matrix,
    later_mixing_exit_matrix,
    later_widen_matrix,
    later_narrow_matrix,
    standardizer_factors,
    picture_divisors,
    closing_cotangent,
):
    sections = lax.axis_size("section")
    dp = lax.axis_size("dp")
    me = lax.axis_index("section")
    item_count, query_count, width = starting_learned_vectors.shape
    heads = picture_divisors.shape[0]
    images, patches, feat = frozen_picture_vectors.shape
    own_items = item_count // sections
    rows = own_items * query_count
    own_heads = heads // sections
    head_size = width // heads
    own_width = width // sections
    wide = -(-own_width // 128) * 128
    padded = -(-patches // 16) * 16
    hidden = early_widen_matrix.shape[1]
    gains = standardizer_factors

    clamped = jnp.clip(picture_divisors, 0.5, 2.0)
    scale_all = 1.0 / math.sqrt(head_size) / clamped

    def act(*dims, dtype=BF):
        return shape((rows,) + dims, dtype)

    def blocks():
        return (sections, rows, wide)

    def comm(kernel, outs, args, specs, out_specs, scratch, identity):
        params = pltpu.CompilerParams(vmem_limit_bytes=LIMIT)
        if identity is not None:
            params = pltpu.CompilerParams(
                vmem_limit_bytes=LIMIT, collective_id=identity, has_side_effects=True
            )
        return pl.pallas_call(
            kernel, out_shape=outs, in_specs=specs, out_specs=out_specs, scratch_shapes=scratch,
            compiler_params=params,
        )(*args)

    sems = pltpu.SemaphoreType.DMA
    x0, h1, low1, n1, r1, joined1, mixed_self1, q_got, keyval, mixed1_rows = comm(
        functools.partial(front_kernel, query_count, head_size, own_heads),
        (
            act(width), act(width, dtype=F32), act(width), act(width, dtype=F32), act(1, dtype=F32),
            act(3 * width), act(width), shape(blocks(), BF),
            shape((images, padded, 2 * wide), BF), act(width),
        ),
        (
            texts_per_picture, picture_divisors, gains, starting_learned_vectors,
            frozen_picture_vectors, early_triple_matrix, early_mixing_exit_matrix,
            picture_asker_matrix, picture_pair_matrix,
        ),
        [whole(SMEM), whole(SMEM), whole()] + [whole(pl.ANY)] * 6,
        [whole()] * 10,
        [
            pltpu.VMEM((own_items, query_count, width), BF),
            pltpu.VMEM(early_triple_matrix.shape, BF), pltpu.VMEM((width, width), BF),
            pltpu.VMEM((width, width), BF), pltpu.VMEM((feat, 2 * wide), BF),
            pltpu.VMEM((4, patches, feat), BF),
            pltpu.VMEM(blocks(), BF), pltpu.VMEM(blocks(), BF), pltpu.VMEM(blocks(), BF),
            sems((6,)), sems((4,)), sems((4,)), sems((4,)), sems((4,)), sems((4,)),
        ],
        0,
    )

    weights = (
        picture_exit_matrix, early_widen_matrix, early_narrow_matrix, later_triple_matrix,
        later_mixing_exit_matrix, later_widen_matrix, later_narrow_matrix,
    )
    owners = width // dp % 32 == 0 and feat // dp % 16 == 0 and hidden // dp % 128 == 0
    factors = (
        act(width), act(hidden), act(hidden), act(width),
        act(width), act(hidden), act(hidden), act(width),
    )
    everywhere = shape((sections, rows, width), BF)
    final_blocks, do_blocks, low3, mixed2, djoined2, da4, da2, dz2, dg_mid, *given = comm(
        functools.partial(middle_kernel, query_count, head_size, owners),
        (
            shape(blocks(), BF), shape(blocks(), BF),
            act(width), act(width), act(3 * width), act(width),
            act(width), act(width, dtype=F32), shape((4, width), F32),
        ) + ((everywhere, act(width), act(width)) if owners else factors),
        (h1, mixed1_rows, gains, closing_cotangent) + weights,
        [whole()] * 3 + [whole(pl.ANY)] * (1 + len(weights)),
        [whole()] * 9
        + ([whole(pl.ANY)] + [whole()] * 2 if owners else [whole()] * len(factors)),
        ([pltpu.VMEM(f.shape, BF) for f in factors] if owners else [])
        + [pltpu.VMEM(w.shape, BF) for w in weights]
        + [pltpu.VMEM((own_items, query_count, width), BF)]
        + [sems((len(weights) + 1,)), sems((2, 2)), sems((sections,))]
        + [pltpu.VMEM((rows, hidden), F32)] * 2
        + [pltpu.VMEM((rows, 3 * width), BF), pltpu.VMEM((rows, width), BF)]
        + [pltpu.VMEM((rows, width), F32), pltpu.VMEM((rows, 1), F32)] * 4,
        1 if owners else None,
    )

    if owners:
        x_got, da_own, da_other = given
        pair_block_rows = feat // dp
        dq_blocks, da_got, temper_rows, pair_unit = comm(
            functools.partial(image_back_kernel, query_count, head_size, own_heads),
            (
                shape(blocks(), BF), everywhere, shape((1, own_heads * query_count), F32),
                shape((1, dp // 2, 2, pair_block_rows, 2 * own_width), BF),
            ),
            (
                texts_per_picture, picture_divisors, q_got, do_blocks, da_own, da_other, keyval,
                frozen_picture_vectors,
            ),
            [whole(SMEM), whole(SMEM), whole()] + [whole(pl.ANY)] * 5,
            [whole(), whole(pl.ANY), whole(), whole()],
            [
                pltpu.VMEM(blocks(), BF),
                pltpu.VMEM((images, padded, 2 * wide), BF),
                pltpu.VMEM((item_count, padded, own_heads * query_count), F32),
                pltpu.VMEM((item_count, padded, own_heads * query_count), F32),
                pltpu.VMEM((item_count, padded, 2 * wide), BF),
                pltpu.VMEM((padded, 2 * wide), F32),
                pltpu.VMEM((2, 2, patches, feat), BF),
                pltpu.VMEM((2 * wide, feat), F32),
                pltpu.VMEM((16, feat), F32), pltpu.VMEM((16, 2 * wide), F32),
                sems((1,)), sems((2,)), sems((4,)), sems((4,)), sems((4,)), sems((4,)),
            ],
            3,
        )
    else:
        do_got, final_got = exchange(do_blocks), exchange(final_blocks)
        dq, dkv, temper_rows = call(
            functools.partial(
                attend_image_back_kernel, patches, own_heads, head_size, query_count, 8
            ),
            (
                shape((sections * rows, wide), BF),
                shape((images, padded, 2 * wide), BF),
                shape((1, own_heads * query_count), F32),
            ),
            texts_per_picture, picture_divisors, q_got.reshape(sections * rows, wide),
            do_got.reshape(sections * rows, wide), keyval,
            in_specs=[whole(SMEM), whole(SMEM), whole(), whole(), whole()],
            scratch=[pltpu.VMEM((images, padded, 2 * wide), F32)],
        )

    interior = ((picture_divisors > 0.5) & (picture_divisors < 2.0)).astype(F32)
    temper_factor = (-scale_all / clamped) * interior
    if owners:
        (
            final_got, dx_got, small, expand2, reduce2, project2, out2, expand1, reduce1,
            asker, image_out, project1, out1, pair_part,
        ) = tail(
            (
                final_blocks, dq_blocks, x_got, da_got, early_widen_matrix, early_narrow_matrix,
                later_widen_matrix, later_narrow_matrix, low3, djoined2, mixed2, da4,
                low1, mixed1_rows, da2, x0, mixed_self1,
                picture_asker_matrix, early_mixing_exit_matrix, early_triple_matrix,
                pair_unit, dz2, n1, r1, gains, joined1, dg_mid, temper_rows,
            ),
            sections, dp, width, hidden, feat, query_count, head_size,
        )
        gains_grad = small[:5]
        temper_grad = small[5, :heads] * temper_factor
    else:
        low2, m1, du1, da3, low4, m2, du2, da5 = given
        dq_blocks = exchange(dq.reshape(sections, rows, wide))
        d_pair = pl.pallas_call(
            keyval_grad_kernel,
            out_shape=shape((feat, 2 * own_width), BF),
            grid=(images,),
            in_specs=[
                pl.BlockSpec((1, patches, feat), lambda j: (j, 0, 0)),
                pl.BlockSpec((1, padded, 2 * wide), lambda j: (j, 0, 0)),
            ],
            out_specs=pl.BlockSpec((feat, 2 * own_width), lambda j: (0, 0)),
            scratch_shapes=[pltpu.VMEM((2 * wide, feat), F32)],
            compiler_params=pltpu.CompilerParams(vmem_limit_bytes=LIMIT),
        )(frozen_picture_vectors, dkv)

        dq_rows, da1, djoined1, dx_blocks, dg0 = call(
            functools.partial(last_kernel, query_count, head_size),
            (
                act(width), act(width), act(3 * width),
                shape((sections, rows, wide), BF), shape((1, width), F32),
            ),
            dz2, dq_blocks, picture_asker_matrix, n1, r1, gains, early_mixing_exit_matrix, joined1,
            early_triple_matrix,
            scratch=[pltpu.VMEM((rows, width), BF)],
        )

        def block_unit(grad):
            parts, k, own = grad.shape
            return grad.reshape(parts, dp, k // dp, own)

        def pair_grad(x, dy, y, dz):
            own = (dy.shape[1] + dz.shape[1]) // sections
            return block_unit(
                call(pair_weight_kernel, shape((sections, x.shape[1], own), BF), x, dy, y, dz)
            )

        expand2 = home(block_unit(expand_grad(low4, du2, sections)))
        reduce2 = home(reduce_grad(da5, m2, sections, dp)).T
        self2 = home(pair_grad(low3, djoined2, mixed2, da4))
        expand1 = home(block_unit(expand_grad(low2, du1, sections)))
        reduce1 = home(reduce_grad(da3, m1, sections, dp)).T
        pair_block = line_sum(
            core_sum(d_pair.reshape(1, dp, feat // dp, 2 * own_width))[0]
        )
        image_units = home(pair_grad(low1, dq_rows, mixed1_rows, da2))
        self1 = home(pair_grad(x0, djoined1, mixed_self1, da1))
        third = 3 * own_width
        project2, out2 = self2[:, :third], self2[:, third:]
        project1, out1 = self1[:, :third], self1[:, third:]
        asker, image_out = image_units[:, :own_width], image_units[:, own_width:]

        pair_rows = pair_block.shape[0]
        half = sections // 2
        pair_halves = pair_block.astype(BF).reshape(pair_rows, 2, own_width).transpose(1, 0, 2)
        key_home, val_home = me // 2, half + me // 2
        sent = jnp.zeros((sections, pair_rows, own_width), BF)
        sent = lax.dynamic_update_index_in_dim(sent, pair_halves[0], key_home, 0)
        sent = lax.dynamic_update_index_in_dim(sent, pair_halves[1], val_home, 0)
        got = exchange(sent)
        first = (me % half) * 2
        pair_part = lax.dynamic_slice_in_dim(got, first, 2, 0)
        pair_part = pair_part.transpose(1, 0, 2).reshape(pair_rows, 2 * own_width).astype(F32)

        dx_got = exchange(dx_blocks)
        d_temper = jnp.sum(temper_rows.reshape(own_heads, query_count), axis=1)
        spread = jnp.zeros((heads,), F32)
        spread = lax.dynamic_update_slice_in_dim(spread, d_temper, me * own_heads, 0)
        small = all_sum(jnp.concatenate([dg0.reshape(-1), dg_mid.reshape(-1), spread]))
        gains_grad = small[: 5 * width].reshape(5, width)
        temper_grad = small[5 * width :] * temper_factor

    grads = (
        project1, out1, asker, pair_part, image_out, expand1, reduce1,
        project2, out2, expand2, reduce2, gains_grad,
    )
    grads = [grad.astype(F32) for grad in grads]
    states = [shape((item_count * query_count, own_width), F32)] * 2
    turned = [grad.shape[0] > grad.shape[1] for grad in grads]
    results = states + [
        shape(grad.shape[::-1] if turn else grad.shape, F32) for grad, turn in zip(grads, turned)
    ]
    final_part, grad_part, *grads = pl.pallas_call(
        functools.partial(deliver_kernel, own_width),
        out_shape=results,
        in_specs=[whole()] * (2 + len(grads)),
        out_specs=[whole()] * (2 + len(grads)),
        compiler_params=pltpu.CompilerParams(vmem_limit_bytes=LIMIT),
    )(final_got, dx_got, *grads)
    grads = [grad.T if turn else grad for grad, turn in zip(grads, turned)]
    states = (item_count, query_count, own_width)
    return (
        final_part.reshape(states),
        grad_part.reshape(states),
        *grads,
        temper_grad,
    )


def solution(mesh):
    return jax.shard_map(
        body,
        mesh=mesh,
        in_specs=(P("dp", None, None), P("dp", None, None), P("dp", None))
        + (P(),) * 13
        + (P("dp", None, None),),
        out_specs=(P("dp", None, "section"),) * 2 + (P("dp", "section"),) * 11 + (P(), P()),
        check_vma=False,
    )
```

```python
import functools
import math

import jax
import jax.numpy as jnp
from jax import lax
from jax.experimental import pallas as pl
from jax.experimental.pallas import tpu as pltpu
from jax.sharding import PartitionSpec as P

EPSILON = 1e-06
BF = jnp.bfloat16
F32 = jnp.float32


def mm(left, right):
    return jnp.dot(left, right, preferred_element_type=F32)


def mm_tn(left, right):
    return lax.dot_general(left, right, (((0,), (0,)), ((), ())), preferred_element_type=F32)


def mm_nt(left, right):
    return lax.dot_general(left, right, (((1,), (1,)), ((), ())), preferred_element_type=F32)


def layer_norm(z, gain):
    centred = z - jnp.mean(z, axis=-1, keepdims=True)
    inverse = lax.rsqrt(jnp.mean(centred * centred, axis=-1, keepdims=True) + EPSILON)
    normed = centred * inverse
    return normed * gain, normed, inverse


def norm_back(dout, gain, normed, inverse):
    dn = dout * gain
    dgain = jnp.sum(dout * normed, axis=0)
    dz = inverse * (
        dn
        - jnp.mean(dn, axis=-1, keepdims=True)
        - normed * jnp.mean(dn * normed, axis=-1, keepdims=True)
    )
    return dz, dgain


def gelu_both(u):
    cdf = 0.5 * (1.0 + lax.erf(u * (0.5**0.5)))
    return u * cdf, cdf + u * jnp.exp(-0.5 * u * u) * (1.0 / math.sqrt(2.0 * math.pi))


def swap(value, axis, bit):
    size = lax.axis_size(axis)
    return lax.ppermute(value, axis, [(i, i ^ bit) for i in range(size)])


def pick(value, index, axis):
    return lax.dynamic_index_in_dim(value, index, axis, keepdims=False)


def add_low(left, right):
    return (left.astype(F32) + right.astype(F32)).astype(BF)


def section_blocks(value):
    rows, width = value.shape
    parts = lax.axis_size("section")
    return value.reshape(rows, parts, width // parts).transpose(1, 0, 2)


def exchange(blocks):
    me = lax.axis_index("section")
    parts = lax.axis_size("section")
    out = blocks
    for bit in range(1, parts):
        got = swap(pick(blocks, me ^ bit, 0), "section", bit)
        out = lax.dynamic_update_index_in_dim(out, got, me ^ bit, 0)
    return out


def cols_to_section(value):
    return exchange(section_blocks(value))


def rows_from_section(blocks):
    got = exchange(blocks)
    parts, rows, width = got.shape
    return got.transpose(1, 0, 2).reshape(rows, parts * width)


def line_sum(blocks):
    n = blocks.shape[0]
    p = lax.axis_index("dp") // 2
    size = lax.axis_size("dp")
    kept = blocks
    for k in range(n - 1):
        up_at = jnp.clip(n - 1 - k + p, 0, n - 1)
        down_at = jnp.clip(p - (n - 1 - k), 0, n - 1)
        up_pairs = [(2 * q + c, 2 * q + 2 + c) for q in range(min(k, n - 2) + 1) for c in (0, 1)]
        down_pairs = [
            (2 * q + c, 2 * q - 2 + c) for q in range(max(n - 1 - k, 1), n) for c in (0, 1)
        ]
        up = lax.ppermute(pick(kept, up_at, 0), "dp", up_pairs)
        down = lax.ppermute(pick(kept, down_at, 0), "dp", down_pairs)
        up_to = jnp.clip(n - 2 - k + p, 0, n - 1)
        down_to = jnp.clip(p + 1 - (n - 1 - k), 0, n - 1)
        kept = lax.dynamic_update_index_in_dim(kept, add_low(pick(kept, up_to, 0), up), up_to, 0)
        kept = lax.dynamic_update_index_in_dim(
            kept, add_low(pick(kept, down_to, 0), down), down_to, 0
        )
    del size
    return pick(kept, p, 0)


def core_sum(unit):
    parts, dp, r, w = unit.shape
    c = lax.axis_index("dp") % 2
    pairs = unit.reshape(parts, dp // 2, 2, r, w)
    return add_low(pick(pairs, c, 2), swap(pick(pairs, 1 - c, 2), "dp", 1))


def plane_sum(unit):
    parts, n, r, w = unit.shape
    me = lax.axis_index("section")
    low, high = me % 2, me // 2
    square = unit.reshape(2, 2, n, r, w)
    a, b = square[:, :, :, : r // 2], square[:, :, :, r // 2 :]
    a = add_low(pick(a, low, 1), swap(pick(a, 1 - low, 1), "section", 1))
    b = add_low(pick(b, high, 0), swap(pick(b, 1 - high, 0), "section", 2))
    a = add_low(pick(a, high, 0), swap(pick(a, 1 - high, 0), "section", 2))
    b = add_low(pick(b, low, 0), swap(pick(b, 1 - low, 0), "section", 1))
    return jnp.concatenate([a, b], axis=1)


def home(unit):
    return line_sum(plane_sum(core_sum(unit)))


def unit_of(grad, dp, sections):
    rows, cols = grad.shape
    return (
        grad.astype(BF)
        .reshape(dp, rows // dp, sections, cols // sections)
        .transpose(2, 0, 1, 3)
    )


def all_sum(value):
    for axis in ("dp", "section"):
        bit = 1
        while bit < lax.axis_size(axis):
            value = value + swap(value, axis, bit)
            bit *= 2
    return value


VMEM = pltpu.MemorySpace.VMEM
SMEM = pltpu.MemorySpace.SMEM
LIMIT = 60 * 1024 * 1024
GROUP = 128


def whole(space=VMEM):
    return pl.BlockSpec(memory_space=space)


def head_lanes(shape, head, head_size):
    return lax.broadcasted_iota(jnp.int32, shape, len(shape) - 1) // head_size == head


def same_item(query_count):
    shape = (GROUP, GROUP)
    left = lax.broadcasted_iota(jnp.int32, shape, 0) // query_count
    right = lax.broadcasted_iota(jnp.int32, shape, 1) // query_count
    return left == right


def soft(t, mask, scale):
    t = jnp.where(mask, t * scale, -1e30)
    e = jnp.exp(t - jnp.max(t, axis=0, keepdims=True))
    return e * (1.0 / jnp.sum(e, axis=0, keepdims=True))


def masked(value, head, head_size):
    return jnp.where(head_lanes(value.shape, head, head_size), value, jnp.zeros_like(value))


def pairs_at_once(pairs):
    return 3 if pairs % 3 == 0 else 1


def attend_self(joined_ref, mixed_ref, query_count, head_size):
    rows, width = mixed_ref.shape
    pair = 2 * head_size
    scale = 1.0 / math.sqrt(head_size)
    mask = same_item(query_count)
    many = pairs_at_once(width // pair)

    def step(i, _):
        places = [
            (pl.ds(g * GROUP, GROUP), pl.multiple_of((i * many + j) * pair, pair))
            for j in range(many)
            for g in range(rows // GROUP)
        ]
        heads = [(at, col, h) for at, col in places for h in range(2)]
        t = [
            mm_nt(
                masked(joined_ref[at, pl.ds(width + col, pair)], h, head_size),
                joined_ref[at, pl.ds(col, pair)],
            )
            for at, col, h in heads
        ]
        turned = [joined_ref[at, pl.ds(2 * width + col, pair)].T for at, col in places]
        p = [soft(one, mask, scale).astype(BF) for one in t]
        o = [
            mm(turned[n // 2][h * head_size : (h + 1) * head_size], p[n])
            for n, (_, _, h) in enumerate(heads)
        ]
        for n, (at, col) in enumerate(places):
            both = jnp.concatenate([o[2 * n], o[2 * n + 1]], axis=0)
            mixed_ref[at, pl.ds(col, pair)] = both.astype(BF).T
        return 0

    lax.fori_loop(0, width // pair // many, step, 0)


def attend_self_back(joined_ref, do_ref, djoined_ref, query_count, head_size, many=None):
    rows, width = do_ref.shape
    pair = 2 * head_size
    scale = 1.0 / math.sqrt(head_size)
    mask = same_item(query_count)
    many = many or pairs_at_once(width // pair)

    def step(i, _):
        places = [
            (pl.ds(g * GROUP, GROUP), pl.multiple_of((i * many + j) * pair, pair))
            for j in range(many)
            for g in range(rows // GROUP)
        ]
        heads = [(at, col, h) for at, col in places for h in range(2)]

        def part(at, col, which):
            return joined_ref[at, pl.ds(which * width + col, pair)]

        def head_of(value, h):
            return masked(value, h, head_size)

        t = [mm_nt(head_of(part(at, col, 1), h), part(at, col, 0)) for at, col, h in heads]
        dp = [
            mm_nt(head_of(part(at, col, 2), h), do_ref[at, pl.ds(col, pair)])
            for at, col, h in heads
        ]
        turned = [part(at, col, 1).T for at, col in places]
        p = [soft(one, mask, scale) for one in t]
        dt = [
            (one * (grad - jnp.sum(one * grad, axis=0, keepdims=True)) * scale).astype(BF)
            for one, grad in zip(p, dp)
        ]
        dv = [
            mm(one.astype(BF), head_of(do_ref[at, pl.ds(col, pair)], h))
            for one, (at, col, h) in zip(p, heads)
        ]
        dk = [mm(one, head_of(part(at, col, 0), h)) for one, (at, col, h) in zip(dt, heads)]
        dq = [
            mm(turned[n // 2][h * head_size : (h + 1) * head_size], dt[n])
            for n, (_, _, h) in enumerate(heads)
        ]
        for n, (at, col) in enumerate(places):
            both = jnp.concatenate([dq[2 * n], dq[2 * n + 1]], axis=0)
            djoined_ref[at, pl.ds(col, pair)] = both.astype(BF).T
            djoined_ref[at, pl.ds(width + col, pair)] = (dk[2 * n] + dk[2 * n + 1]).astype(BF)
            djoined_ref[at, pl.ds(2 * width + col, pair)] = (dv[2 * n] + dv[2 * n + 1]).astype(BF)
        return 0

    lax.fori_loop(0, width // pair // many, step, 0)


def project_into(out_ref, low, w_ref, block=768):
    for at in range(0, w_ref.shape[1], block):
        out_ref[:, at : at + block] = mm(low, w_ref[:, at : at + block]).astype(BF)


def back_through(dy_ref, w_ref, block=768):
    total = None
    for at in range(0, w_ref.shape[1], block):
        term = mm_nt(dy_ref[:, at : at + block], w_ref[:, at : at + block])
        total = term if total is None else total + term
    return total


def hidden_forward(low, w_expand_ref, w_reduce_ref, m_ref, slope_ref, block=768):
    starts = list(range(0, w_expand_ref.shape[1], block))

    def expand(at):
        return mm(low, w_expand_ref[:, at : at + block]).astype(BF)

    total = None
    ahead = expand(starts[0])
    for i, at in enumerate(starts):
        u = ahead
        if i + 1 < len(starts):
            ahead = expand(starts[i + 1])
        m, slope = gelu_both(u.astype(F32))
        m = m.astype(BF)
        m_ref[:, at : at + block] = m
        slope_ref[:, at : at + block] = slope
        term = mm(m, w_reduce_ref[at : at + block, :])
        total = term if total is None else total + term
    return total


def hidden_backward(da, w_expand_ref, w_reduce_ref, slope_ref, du_ref, block=1024):
    for at in range(0, w_expand_ref.shape[1], block):
        dm = mm_nt(da, w_reduce_ref[at : at + block, :])
        du_ref[:, at : at + block] = (dm * slope_ref[:, at : at + block]).astype(BF)
    return mm_nt(du_ref[...], w_expand_ref[...])


def norm_into(z, gain, n_ref, r_ref):
    out, n, r = layer_norm(z, gain)
    n_ref[...] = n
    r_ref[...] = r
    return out


def window(t, own):
    low = t * own // 128 * 128
    return low, t * own - low


def put_blocks(out_ref, value):
    parts, _, wide = out_ref.shape
    own = value.shape[1] // parts
    for t in range(parts):
        low, _ = window(t, own)
        out_ref[t] = value[:, low : low + wide]


def take_blocks(in_ref, own):
    parts, _, wide = in_ref.shape
    pieces = []
    for low in range(0, parts * own, 128):
        piece = None
        for t in range(parts):
            first, _ = window(t, own)
            if first <= low < first + wide:
                part = in_ref[t, :, low - first : low - first + 128]
                piece = part if piece is None else piece + part
        pieces.append(piece)
    return jnp.concatenate(pieces, axis=1)


MESH = pl.DeviceIdType.MESH


def start(copies):
    for copy in copies:
        copy.start()


def wait(copies):
    for copy in copies:
        copy.wait()


def exchange_copies(source, target, sends, recvs):
    s, d = lax.axis_index("section"), lax.axis_index("dp")
    out = []
    for bit in range(1, lax.axis_size("section")):
        to = s ^ bit
        out.append(pltpu.make_async_remote_copy(
            src_ref=source.at[to], dst_ref=target.at[s], send_sem=sends.at[bit],
            recv_sem=recvs.at[bit], device_id=(to, d), device_id_type=MESH,
        ))
    out.append(pltpu.make_async_copy(source.at[s], target.at[s], sends.at[0]))
    return out


def greet_sections():
    s, d = lax.axis_index("section"), lax.axis_index("dp")
    barrier = pltpu.get_barrier_semaphore()
    parts = lax.axis_size("section")
    for bit in range(1, parts):
        pl.semaphore_signal(barrier, inc=1, device_id=(s ^ bit, d), device_id_type=MESH)
    pl.semaphore_wait(barrier, parts - 1)


def owner_copies(source, target, which, sends, recvs):
    s, d = lax.axis_index("section"), lax.axis_index("dp")
    out = []
    for i in range(2):
        to = 2 * which + i
        out.append((to != s, pltpu.make_async_remote_copy(
            src_ref=source, dst_ref=target.at[s], send_sem=sends.at[which, i],
            recv_sem=recvs.at[s], device_id=(to, d), device_id_type=MESH,
        )))
        out.append((to == s, pltpu.make_async_copy(source, target.at[s], sends.at[which, i])))
    return out


def start_if(pairs):
    for condition, copy in pairs:
        pl.when(condition)(copy.start)


def sent_if(pairs):
    for remote, local in zip(pairs[::2], pairs[1::2]):
        pl.when(remote[0])(remote[1].wait_send)
        pl.when(local[0])(local[1].wait)


def received(target, sends, recvs):
    s, d = lax.axis_index("section"), lax.axis_index("dp")
    for t in range(lax.axis_size("section")):
        copy = pltpu.make_async_remote_copy(
            src_ref=target.at[t], dst_ref=target.at[t], send_sem=sends.at[0, 0],
            recv_sem=recvs.at[t], device_id=(s ^ 1, d), device_id_type=MESH,
        )
        pl.when(t != s)(copy.wait_recv)


def front_kernel(
    query_count, head_size, own_heads,
    texts_ref, divisor_ref, g_ref, x_hbm, images_hbm, wp_hbm, wo_hbm, wq_hbm, pair_hbm,
    x_out, h_out, low_out, n_out, joined_out, mixed_out, q_out, kv_out, r_ref, mixed1_ref,
    x_ref, h_ref, low_ref, n_ref, joined_ref, mixed_ref, q_got, kv_ref,
    x_in, wp, wo, wq, w_pair, blocks, q_blocks, o_blocks, o_got,
    loads, image_sems, q_sends, q_recvs, o_sends, o_recvs, stores,
):
    s, d = lax.axis_index("section"), lax.axis_index("dp")
    parts, rows, wide = q_got.shape
    images, patches, feat = images_hbm.shape
    width = x_ref.shape[1]
    own = width // parts
    items = x_in.shape[0]
    low_at = pl.multiple_of(s * own // 128 * 128, 128)
    copies = [
        pltpu.make_async_copy(source, target, loads.at[i])
        for i, (source, target) in enumerate((
            (x_hbm.at[pl.ds(s * items, items)], x_in),
            (wp_hbm, wp), (wo_hbm, wo), (wq_hbm, wq),
            (pair_hbm.at[:, pl.ds(low_at, wide)], w_pair.at[:, :wide]),
            (pair_hbm.at[:, pl.ds(pl.multiple_of(width + low_at, 128), wide)], w_pair.at[:, wide:]),
        ))
    ]
    start(copies)

    results = (
        (x_ref, x_out), (h_ref, h_out), (low_ref, low_out), (n_ref, n_out), (joined_ref, joined_out),
        (mixed_ref, mixed_out), (q_got, q_out), (kv_ref, kv_out),
    )
    stored = [
        pltpu.make_async_copy(source, target, stores.at[i])
        for i, (source, target) in enumerate(results)
    ]

    def image(j):
        return pltpu.make_async_copy(images_hbm.at[j], blocks.at[j % 4], image_sems.at[j % 4])

    for j in range(min(3, images)):
        image(j).start()
    copies[0].wait()
    x_ref[...] = x_in[...].reshape(rows, width)
    copies[1].wait()
    project_into(joined_ref, x_ref[...], wp)
    attend_self(joined_ref, mixed_ref, query_count, head_size)
    copies[2].wait()
    z = x_ref[...].astype(F32) + mm(mixed_ref[...], wo[...])
    h = norm_into(z, g_ref[0:1, :], n_ref, r_ref)
    h_ref[...] = h
    low_ref[...] = h.astype(BF)
    copies[3].wait()
    put_blocks(q_blocks, mm(low_ref[...], wq[...]).astype(BF))
    greet_sections()
    q_copies = exchange_copies(q_blocks, q_got, q_sends, q_recvs)
    start(q_copies)
    start(stored[:6])

    copies[4].wait()
    copies[5].wait()
    padded = kv_ref.shape[1]
    full = patches // 16 * 16
    for j in range(images):
        image(j).wait()
        if j + 3 < images:
            image(j + 3).start()
        kv_ref[j, full:, :] = jnp.zeros((padded - full, kv_ref.shape[2]), BF)
        kv_ref[j, :patches, :] = mm(blocks[j % 4], w_pair[...]).astype(BF)

    scales = column_scales(divisor_ref, own_heads, head_size, query_count)
    shift = s * own % 128 // head_size
    ends = caption_ends(texts_ref)
    mask = patch_rows(padded, patches)
    together = items

    for copy in q_copies[:-1]:
        copy.wait()
    q_copies[-1].wait()
    start(stored[6:])
    o_copies = []
    for bit in (1, 2, 3, 0):
        t = s ^ bit

        def step(i, _, t=t):
            group = [i * together + b for b in range(together)]

            def at(item):
                return pl.ds(pl.multiple_of(item * query_count, query_count), query_count)

            done = attend_image(
                lambda item: q_got[t, at(item), :], group, kv_ref,
                [image_at(ends, t * items + item) for item in group],
                mask, scales, own_heads, head_size, shift,
            )
            for item, rows in zip(group, done):
                o_blocks[t, at(item), :] = rows
            return 0

        lax.fori_loop(0, items // together, step, 0)
        if bit:
            copy = pltpu.make_async_remote_copy(
                src_ref=o_blocks.at[t], dst_ref=o_got.at[s], send_sem=o_sends.at[bit],
                recv_sem=o_recvs.at[bit], device_id=(t, d), device_id_type=MESH,
            )
        else:
            copy = pltpu.make_async_copy(o_blocks.at[t], o_got.at[t], o_sends.at[0])
        copy.start()
        o_copies.append(copy)
    wait(o_copies)
    mixed1_ref[...] = take_blocks(o_got, own)
    wait(stored)


def stacked(value, own_heads, head_size, shift):
    return jnp.concatenate(
        [masked(value, h + shift, head_size) for h in range(own_heads)], axis=0
    )


def unstacked(value, own_heads, head_size, shift):
    rows = value.shape[0] // own_heads
    total = None
    for h in range(own_heads):
        part = masked(value[h * rows : (h + 1) * rows], h + shift, head_size)
        total = part if total is None else total + part
    return total


def column_scales(divisor_ref, own_heads, head_size, query_count):
    first = lax.axis_index("section") * own_heads
    divisors = jnp.concatenate(
        [jnp.full((1, query_count), divisor_ref[first + h], F32) for h in range(own_heads)], axis=1
    )
    return 1.0 / math.sqrt(head_size) / jnp.clip(divisors, 0.5, 2.0)


def caption_ends(texts_ref):
    ends, total = [], 0
    for j in range(texts_ref.shape[1]):
        total = total + texts_ref[0, j]
        ends.append(total)
    return ends


def image_at(ends, item):
    j = 0
    for end in ends:
        j = j + jnp.where(end <= item, 1, 0)
    return jnp.minimum(j, len(ends) - 1)


def patch_rows(padded, patches):
    return lax.broadcasted_iota(jnp.int32, (padded, 1), 0) < patches


def attend_image(rows_of, items, kv_ref, images, mask, scales, own_heads, head_size, shift):
    q = [stacked(rows_of(item), own_heads, head_size, shift) for item in items]
    wide = q[0].shape[1]
    t = [mm_nt(kv_ref[j, :, :wide], one) for j, one in zip(images, q)]
    p = [soft(one, mask, scales).astype(BF) for one in t]
    o = [mm_tn(one, kv_ref[j, :, wide:]) for j, one in zip(images, p)]
    return [unstacked(one, own_heads, head_size, shift).astype(BF) for one in o]


def attend_image_back_kernel(
    patches, own_heads, head_size, query_count, together,
    texts_ref, divisor_ref, q_ref, do_ref, kv_ref, dq_ref, dkv_ref, temper_ref, total_ref,
):
    wide = q_ref.shape[1]
    items = q_ref.shape[0] // query_count
    mask = patch_rows(kv_ref.shape[1], patches)
    scales = column_scales(divisor_ref, own_heads, head_size, query_count)
    shift = lax.axis_index("section") * own_heads * head_size % 128 // head_size
    ends = caption_ends(texts_ref)
    total_ref[...] = jnp.zeros_like(total_ref)
    temper_ref[...] = jnp.zeros_like(temper_ref)

    def step(i, _):
        group = [i * together + b for b in range(together)]
        at = [pl.ds(pl.multiple_of(item * query_count, query_count), query_count) for item in group]
        images = [image_at(ends, item) for item in group]
        q = [stacked(q_ref[one, :], own_heads, head_size, shift) for one in at]
        do = [stacked(do_ref[one, :], own_heads, head_size, shift) for one in at]
        t = [mm_nt(kv_ref[j, :, :wide], one) for j, one in zip(images, q)]
        dp = [mm_nt(kv_ref[j, :, wide:], one) for j, one in zip(images, do)]
        p = [soft(one, mask, scales) for one in t]
        ds = [
            one * (grad - jnp.sum(one * grad, axis=0, keepdims=True)) for one, grad in zip(p, dp)
        ]
        dt = [(one * scales).astype(BF) for one in ds]
        temper = None
        for one, score in zip(ds, t):
            term = jnp.sum(one * score, axis=0, keepdims=True)
            temper = term if temper is None else temper + term
        dq = [mm_tn(one, kv_ref[j, :, :wide]) for one, j in zip(dt, images)]
        dk = [mm(one, rows) for one, rows in zip(dt, q)]
        dv = [mm(one.astype(BF), rows) for one, rows in zip(p, do)]
        for one, rows in zip(at, dq):
            dq_ref[one, :] = unstacked(rows, own_heads, head_size, shift).astype(BF)
        for j, key, val in zip(images, dk, dv):
            total_ref[j, :, :wide] += key
            total_ref[j, :, wide:] += val
        temper_ref[...] += temper
        return 0

    lax.fori_loop(0, items // together, step, 0)
    dkv_ref[...] = total_ref[...].astype(BF)


def pair_columns(total_ref, own):
    s = lax.axis_index("section")
    shift = s * own % 128
    halves = []
    for half in range(2):
        base = half * (total_ref.shape[0] // 2)
        out = total_ref[base : base + own, :]
        for offset in sorted({window(t, own)[1] for t in range(4)} - {0}):
            out = jnp.where(
                shift == offset, total_ref[base + offset : base + offset + own, :], out
            )
        halves.append(out.T.astype(BF))
    return jnp.concatenate(halves, axis=1)


def image_back_kernel(
    query_count, head_size, own_heads,
    texts_ref, divisor_ref, q_ref, do_blocks, da_own, da_other, kv_hbm, images_hbm,
    dq_blocks, da_got, temper_ref, pair_ref,
    do_got, kv, scores, shares, running, sums, blocks, total, last_x, last_kv,
    loads, image_sems, do_sends, do_recvs, da_sends, da_recvs,
):
    s, d = lax.axis_index("section"), lax.axis_index("dp")
    parts, rows, wide = q_ref.shape
    count, patches, feat = images_hbm.shape
    items = rows // query_count
    last = patches - 1
    own = parts * 0 + pair_ref.shape[4] // 2

    def image_pair(j):
        return pltpu.make_async_copy(
            images_hbm.at[pl.ds(2 * j, 2)], blocks.at[j % 2], image_sems.at[j % 2]
        )

    kv_copy = pltpu.make_async_copy(kv_hbm, kv, loads.at[0])
    kv_copy.start()
    image_pair(0).start()
    greet_sections()
    dos = exchange_copies(do_blocks, do_got, do_sends, do_recvs)
    start(dos)
    das = [pltpu.make_async_copy(da_own, da_got.at[s], da_sends.at[0])]
    for bit in range(1, parts):
        das.append(pltpu.make_async_remote_copy(
            src_ref=da_own if bit == 1 else da_other, dst_ref=da_got.at[s],
            send_sem=da_sends.at[bit], recv_sem=da_recvs.at[bit],
            device_id=(s ^ bit, d), device_id_type=MESH,
        ))
    start(das)

    scales = column_scales(divisor_ref, own_heads, head_size, query_count)
    shift = s * own % 128 // head_size
    ends = caption_ends(texts_ref)
    mask = patch_rows(kv.shape[1], patches)
    kv_copy.wait()

    def rows_of(i):
        return pl.ds(pl.multiple_of(i * query_count, query_count), query_count)

    def score(t, _):
        group = range(items)
        images = [image_at(ends, t * items + i) for i in group]
        q = [stacked(q_ref[t, rows_of(i), :], own_heads, head_size, shift) for i in group]
        got = [mm_nt(kv[j, :, :wide], one) for j, one in zip(images, q)]
        p = [soft(one, mask, scales) for one in got]
        for i in group:
            scores[t * items + i] = got[i]
            shares[t * items + i] = p[i]
        return 0

    lax.fori_loop(0, parts, score, 0)
    wait(dos)
    temper_ref[...] = jnp.zeros_like(temper_ref)
    sums[...] = jnp.zeros_like(sums)
    for t in range(parts):

        def back(g, _, t=t):
            group = [g * (items // 2) + i for i in range(items // 2)]
            place = [t * items + i for i in group]
            images = [image_at(ends, at) for at in place]
            same = [image_at(ends, at - 1) == j for at, j in zip(place, images)]
            q = [stacked(q_ref[t, rows_of(i), :], own_heads, head_size, shift) for i in group]
            do = [stacked(do_got[t, rows_of(i), :], own_heads, head_size, shift) for i in group]
            dp = [mm_nt(kv[j, :, wide:], one) for j, one in zip(images, do)]
            p = [shares[at] for at in place]
            ds = [
                one * (grad - jnp.sum(one * grad, axis=0, keepdims=True))
                for one, grad in zip(p, dp)
            ]
            dt = [(one * scales).astype(BF) for one in ds]
            temper = temper_ref[...]
            for one, at in zip(ds, place):
                temper = temper + jnp.sum(one * scores[at], axis=0, keepdims=True)
            temper_ref[...] = temper
            dq = [mm_tn(one, kv[j, :, :wide]) for one, j in zip(dt, images)]
            dk = [mm(one, rows) for one, rows in zip(dt, q)]
            dv = [mm(one.astype(BF), rows) for one, rows in zip(p, do)]
            for i, one in zip(group, dq):
                dq_blocks[t, rows_of(i), :] = unstacked(
                    one, own_heads, head_size, shift
                ).astype(BF)
            for at, again, key, val in zip(place, same, dk, dv):
                key = jnp.where(again, sums[:, :wide], 0.0) + key
                val = jnp.where(again, sums[:, wide:], 0.0) + val
                sums[:, :wide] = key
                sums[:, wide:] = val
                running[at, :, :wide] = key.astype(BF)
                running[at, :, wide:] = val.astype(BF)
            return 0

        lax.fori_loop(0, 2, back, 0)

    total[...] = jnp.zeros_like(total)
    last_x[...] = jnp.zeros_like(last_x)
    last_kv[...] = jnp.zeros_like(last_kv)
    for j in range(count // 2):
        image_pair(j).wait()
        if j + 1 < count // 2:
            image_pair(j + 1).start()
        at = [jnp.clip(ends[2 * j + i] - 1, 0, parts * items - 1) for i in range(2)]
        total[...] += mm_tn(
            jnp.concatenate([running[one, :last, :] for one in at], axis=0),
            blocks[j % 2, :, :last, :].reshape(2 * last, feat),
        )
        for i in range(2):
            row = 2 * j + i
            last_x[row : row + 1, :] = blocks[j % 2, i, last:, :].astype(F32)
            last_kv[row : row + 1, :] = running[at[i], last:patches, :].astype(F32)
    total[...] += mm_tn(last_kv[...].astype(BF), last_x[...].astype(BF))
    turned = pair_columns(total, own)
    r = pair_ref.shape[3]
    for i in range(2 * pair_ref.shape[1]):
        pair_ref[0, i // 2, i % 2] = turned[i * r : (i + 1) * r]

    wait(das)


def keyval_grad_kernel(x_ref, dkv_ref, out_ref, total_ref):
    @pl.when(pl.program_id(0) == 0)
    def _():
        total_ref[...] = jnp.zeros_like(total_ref)

    patches = x_ref.shape[1]
    total_ref[...] += mm_tn(dkv_ref[0, :patches, :], x_ref[0])

    @pl.when(pl.program_id(0) == pl.num_programs(0) - 1)
    def _():
        out_ref[...] = pair_columns(total_ref, out_ref.shape[1] // 2)


def middle_kernel(query_count, head_size, owners, *refs):
    refs = list(refs)

    def take(count):
        out = refs[:count]
        del refs[:count]
        return out

    h1_ref, mixed1_ref, g_ref, dout_hbm = take(4)
    hbm_weights = take(7)
    outs = take(5)
    do_blocks, da2_ref, dz2_ref, dg_ref = take(4)
    if owners:
        x_got, da_own, da_other = take(3)
        low2_ref, m1_ref, du1_ref, da3_ref, low4_ref, m2_ref, du2_ref, da5_ref = take(8)
    else:
        low2_ref, m1_ref, du1_ref, da3_ref, low4_ref, m2_ref, du2_ref, da5_ref = take(8)

    def sort_out(da_ref, which):
        if owners:
            own = lax.axis_index("section") // 2 == which

            @pl.when(own)
            def _():
                da_own[...] = da_ref[...]

            @pl.when(jnp.logical_not(own))
            def _():
                da_other[...] = da_ref[...]

    weights = take(7)
    wx, we1, wr1, wp, wo, we2, wr2 = weights
    dout, sems, owner_sends, owner_recvs = take(4)
    early = take(5)
    final_blocks, low3_ref, mixed2_ref, djoined_ref, da4_ref = early
    stores = take(1)[0]
    stored = [
        pltpu.make_async_copy(source, target, stores.at[i])
        for i, (source, target) in enumerate(zip(early, outs))
    ]
    slope1, slope2, joined, do2, n2, r2, n3, r3, n4, r4, n5, r5 = refs
    given = []

    def give(source, which):
        if owners:
            pairs = owner_copies(source, x_got, which, owner_sends, owner_recvs)
            start_if(pairs)
            given.append(pairs)

    copies = [
        pltpu.make_async_copy(src, dst, sems.at[i])
        for i, (src, dst) in enumerate(zip(hbm_weights, weights))
    ]
    for copy in copies:
        copy.start()
    items = dout.shape[0]
    dout_copy = pltpu.make_async_copy(
        dout_hbm.at[pl.ds(lax.axis_index("section") * items, items)], dout, sems.at[len(copies)]
    )
    dout_copy.start()
    copies[0].wait()
    h2 = norm_into(h1_ref[...] + mm(mixed1_ref[...], wx[...]), g_ref[1:2, :], n2, r2)
    low2_ref[...] = h2.astype(BF)
    if owners:
        greet_sections()
    give(low2_ref, 0)
    copies[1].wait()
    copies[2].wait()
    a = hidden_forward(low2_ref[...], we1, wr1, m1_ref, slope1)
    h3 = norm_into(n2[...] * g_ref[1:2, :] + a, g_ref[2:3, :], n3, r3)
    low3_ref[...] = h3.astype(BF)
    copies[3].wait()
    project_into(joined, low3_ref[...], wp)
    attend_self(joined, mixed2_ref, query_count, head_size)
    copies[4].wait()
    a = mm(mixed2_ref[...], wo[...])
    h4 = norm_into(n3[...] * g_ref[2:3, :] + a, g_ref[3:4, :], n4, r4)
    low4_ref[...] = h4.astype(BF)
    give(low4_ref, 1)
    copies[5].wait()
    copies[6].wait()
    a = hidden_forward(low4_ref[...], we2, wr2, m2_ref, slope2)
    h5 = norm_into(n4[...] * g_ref[3:4, :] + a, g_ref[4:5, :], n5, r5)
    put_blocks(final_blocks, h5.astype(BF))
    start(stored[:3])
    dout_copy.wait()

    dz, dg4 = norm_back(
        dout[...].reshape(n5.shape).astype(F32), g_ref[4:5, :], n5[...], r5[...]
    )
    da5_ref[...] = dz.astype(BF)
    sort_out(da5_ref, 1)
    d4 = dz + hidden_backward(da5_ref[...], we2, wr2, slope2, du2_ref)

    dz, dg3 = norm_back(d4, g_ref[3:4, :], n4[...], r4[...])
    da4_ref[...] = dz.astype(BF)
    do2[...] = mm_nt(da4_ref[...], wo[...]).astype(BF)
    attend_self_back(joined, do2, djoined_ref, query_count, head_size)
    start(stored[3:])
    d3 = dz + back_through(djoined_ref, wp)

    dz, dg2 = norm_back(d3, g_ref[2:3, :], n3[...], r3[...])
    da3_ref[...] = dz.astype(BF)
    sort_out(da3_ref, 0)
    d2 = dz + hidden_backward(da3_ref[...], we1, wr1, slope1, du1_ref)

    dz, dg1 = norm_back(d2, g_ref[1:2, :], n2[...], r2[...])
    dz2_ref[...] = dz
    da2_ref[...] = dz.astype(BF)
    put_blocks(do_blocks, mm_nt(da2_ref[...], wx[...]).astype(BF))
    dg_ref[...] = jnp.concatenate([d[None, :] for d in (dg1, dg2, dg3, dg4)], axis=0)
    wait(stored)
    for pairs in given:
        sent_if(pairs)
    if owners:
        received(x_got, owner_sends, owner_recvs)


def last_kernel(
    query_count, head_size, dz2_ref, dq_ref, wq_ref, n_ref, r_ref, g_ref, wo_ref, joined_ref, wp_ref,
    dqr_ref, da_ref, djoined_ref, dx_ref, dg_ref, do,
):
    own = wq_ref.shape[1] // dq_ref.shape[0]
    dqr_ref[...] = take_blocks(dq_ref, own)
    d1 = dz2_ref[...] + mm_nt(dqr_ref[...], wq_ref[...])
    dz, dg = norm_back(d1, g_ref[0:1, :], n_ref[...], r_ref[...])
    dg_ref[...] = dg[None, :]
    da_ref[...] = dz.astype(BF)
    do[...] = mm_nt(da_ref[...], wo_ref[...]).astype(BF)
    attend_self_back(joined_ref, do, djoined_ref, query_count, head_size)
    put_blocks(dx_ref, (dz + back_through(djoined_ref, wp_ref)).astype(BF))


def weight_kernel(x_ref, dy_ref, out_ref):
    out_ref[0] = mm_tn(x_ref[...], dy_ref[...]).astype(BF)


def pair_weight_kernel(x_ref, dy_ref, y_ref, dz_ref, out_ref):
    parts = out_ref.shape[0]
    own_a, own_b = dy_ref.shape[1] // parts, dz_ref.shape[1] // parts
    for t in range(parts):
        a = mm_tn(x_ref[...], dy_ref[:, t * own_a : (t + 1) * own_a]).astype(BF)
        b = mm_tn(y_ref[...], dz_ref[:, t * own_b : (t + 1) * own_b]).astype(BF)
        out_ref[t] = jnp.concatenate([a, b], axis=1)


def turned_weight_kernel(dy_ref, x_ref, out_ref):
    _, dp, own, wide = out_ref.shape
    r = mm_tn(dy_ref[...], x_ref[...]).astype(BF)
    for d in range(dp):
        out_ref[0, d] = r[:, d * wide : (d + 1) * wide]


def deliver_kernel(own, *refs):
    count = len(refs) // 2
    given, out = refs[:count], refs[count:]
    shift = lax.axis_index("section") * own % 128
    parts, rows, _ = given[0].shape
    for source, target in zip(given[:2], out[:2]):
        for t in range(parts):
            block = source[t].astype(F32)
            cut = block[:, :own]
            for offset in sorted({window(i, own)[1] for i in range(parts)} - {0}):
                cut = jnp.where(shift == offset, block[:, offset : offset + own], cut)
            target[t * rows : (t + 1) * rows, :] = cut
    for source, target in zip(given[2:], out[2:]):
        target[...] = source[...] if source.shape == target.shape else source[...].T


def shape(dims, dtype):
    return jax.ShapeDtypeStruct(tuple(dims), dtype)


def call(kernel, outs, *args, in_specs=None, scratch=(), flops=0):
    return pl.pallas_call(
        kernel,
        out_shape=outs,
        in_specs=in_specs or [whole()] * len(args),
        out_specs=jax.tree.map(lambda _: whole(), outs),
        scratch_shapes=list(scratch),
        compiler_params=pltpu.CompilerParams(vmem_limit_bytes=LIMIT),
        cost_estimate=pl.CostEstimate(
            flops=flops, bytes_accessed=int(flops) // 400, transcendentals=0
        ),
    )(*args)


def expand_grad(low, du, parts):
    rows, width = low.shape
    own = du.shape[1] // parts
    return pl.pallas_call(
        weight_kernel,
        out_shape=shape((parts, width, own), BF),
        grid=(parts,),
        in_specs=[
            pl.BlockSpec((rows, width), lambda t: (0, 0)),
            pl.BlockSpec((rows, own), lambda t: (0, t)),
        ],
        out_specs=pl.BlockSpec((1, width, own), lambda t: (t, 0, 0)),
        compiler_params=pltpu.CompilerParams(vmem_limit_bytes=LIMIT),
    )(low, du)


def reduce_grad(da, m, parts, dp):
    rows, width = da.shape
    wide = m.shape[1] // dp
    own = width // parts
    per = 4 if dp % 4 == 0 and (dp // 4 * wide) % 128 == 0 else 1
    blocks = dp // per
    return pl.pallas_call(
        functools.partial(turned_weight_all_kernel, parts),
        out_shape=shape((parts, dp, own, wide), BF),
        grid=(per,),
        in_specs=[
            pl.BlockSpec((rows, width), lambda b: (0, 0)),
            pl.BlockSpec((rows, blocks * wide), lambda b: (0, b)),
        ],
        out_specs=pl.BlockSpec((parts, blocks, own, wide), lambda b: (0, b, 0, 0)),
        compiler_params=pltpu.CompilerParams(vmem_limit_bytes=LIMIT),
    )(da, m)


def turned_weight_all_kernel(parts, dy_ref, x_ref, out_ref):
    _, blocks, own, wide = out_ref.shape
    r = mm_tn(dy_ref[...], x_ref[...]).astype(BF)
    for t in range(parts):
        for d in range(blocks):
            out_ref[t, d] = r[t * own : (t + 1) * own, d * wide : (d + 1) * wide]


def device_of(section, z, core):
    return (section, z * 2 + core)


class Home:
    def __init__(self, unit, kept, from_x, from_y, then_x, then_y, from_z, sends, recvs):
        self.unit, self.kept = unit, kept
        self.from_x, self.from_y = from_x, from_y
        self.then_x, self.then_y = then_x, then_y
        self.from_z = from_z
        self.sends, self.recvs = sends, recvs
        self.s, d = lax.axis_index("section"), lax.axis_index("dp")
        self.sx, self.sy = self.s % 2, self.s // 2
        self.z, self.c = d // 2, d % 2
        self.half = kept.shape[2] // 2

    def copy(self, i, src, dst, device):
        return pltpu.make_async_remote_copy(
            src_ref=src, dst_ref=dst, send_sem=self.sends.at[i], recv_sem=self.recvs.at[i],
            device_id=device, device_id_type=MESH,
        )

    def mine(self):
        return self.s if self.kept.shape[0] > 1 else 0

    def cores(self):
        return [
            self.copy(
                0, self.unit.at[:, :, 1 - self.c], self.kept, device_of(self.s, self.z, 1 - self.c)
            )
        ]

    def first(self):
        s, sx, sy, z, c, half = self.s, self.sx, self.sy, self.z, self.c, self.half
        out = []
        for i in range(2):
            out.append(self.copy(
                1 + i, self.kept.at[2 * i + 1 - sx, :, :half], self.from_x.at[i],
                device_of(s + 1 - 2 * sx, z, c),
            ))
            out.append(self.copy(
                3 + i, self.kept.at[2 * (1 - sy) + i, :, half:], self.from_y.at[i],
                device_of(s + 2 - 4 * sy, z, c),
            ))
        return out

    def second(self):
        s, sx, sy, z, c, half = self.s, self.sx, self.sy, self.z, self.c, self.half
        return [
            self.copy(
                5, self.kept.at[2 * (1 - sy) + sx, :, :half], self.then_y,
                device_of(s + 2 - 4 * sy, z, c),
            ),
            self.copy(
                6, self.kept.at[2 * sy + 1 - sx, :, half:], self.then_x,
                device_of(s + 1 - 2 * sx, z, c),
            ),
        ]

    def pairs(self):
        out = []
        for i in range(2):
            at = 2 * i + 1 - self.z % 2
            out.append(self.copy(
                7 + i, self.kept.at[self.mine(), at], self.from_z.at[i],
                device_of(self.s, self.z + 1 - 2 * (self.z % 2), self.c),
            ))
        return out

    def across(self):
        at = (self.z + 2) % 4
        return [
            self.copy(
                9, self.kept.at[self.mine(), at], self.from_z.at[2],
                device_of(self.s, at, self.c),
            )
        ]

    def direct(self):
        out = []
        for k in range(1, 4):
            to = (self.z + k) % 4
            out.append(self.copy(
                6 + k, self.kept.at[self.mine(), to], self.from_z.at[k - 1],
                device_of(self.s, to, self.c),
            ))
        return out

    def add_pairs(self):
        for i in range(2):
            at = 2 * i + self.z % 2
            self.kept[self.mine(), at] = self.kept[self.mine(), at] + self.from_z[i]

    def add_cores(self):
        n = self.kept.shape[1]

        def step(i, _):
            t, z = i // n, i % n
            self.kept[t, z] = self.kept[t, z] + self.unit[t, z, self.c]
            return 0

        lax.fori_loop(0, self.kept.shape[0] * n, step, 0)

    def add_first(self):
        n, half = self.kept.shape[1], self.half

        def step(i, _):
            t, z = i // n, i % n
            x, y = 2 * t + self.sx, 2 * self.sy + t
            self.kept[x, z, :half] = self.kept[x, z, :half] + self.from_x[t, z]
            self.kept[y, z, half:] = self.kept[y, z, half:] + self.from_y[t, z]
            return 0

        lax.fori_loop(0, 2 * n, step, 0)

    def add_second(self):
        n, half = self.kept.shape[1], self.half

        def step(z, _):
            self.kept[self.s, z, :half] = self.kept[self.s, z, :half] + self.then_y[z]
            self.kept[self.s, z, half:] = self.kept[self.s, z, half:] + self.then_x[z]
            return 0

        lax.fori_loop(0, n, step, 0)

    def total(self, terms):
        total = self.kept[self.mine(), self.z].astype(F32)
        for i in terms:
            total = total + self.from_z[i].astype(F32)
        return total


def greet():
    s, d = lax.axis_index("section"), lax.axis_index("dp")
    sections, dp = lax.axis_size("section"), lax.axis_size("dp")
    n = dp // 2
    z, c = d // 2, d % 2
    barrier = pltpu.get_barrier_semaphore()
    near = [device_of(s, z, 1 - c)]
    for bit in range(1, sections):
        near.append(device_of(s ^ bit, z, c))
        near.append(device_of(s ^ bit, z, 1 - c))
    for k in range(1, n):
        near.append(device_of(s, (z + k) % n, c))
    for device in near:
        pl.semaphore_signal(barrier, inc=1, device_id=device, device_id_type=MESH)
    pl.semaphore_wait(barrier, len(near))


def fill_pair(unit, x, dy, y, dz):
    parts, n, two, r, w = unit.shape
    own_a, own_b = dy.shape[1] // parts, dz.shape[1] // parts
    for t in range(parts):
        a = mm_tn(x[...], dy[:, t * own_a : (t + 1) * own_a]).astype(BF)
        b = mm_tn(y[...], dz[:, t * own_b : (t + 1) * own_b]).astype(BF)
        g = jnp.concatenate([a, b], axis=1)
        for d in range(2 * n):
            unit[t, d // 2, d % 2] = g[d * r : (d + 1) * r]


class Owned:
    def __init__(self, refs, expand1, reduce1, expand2, reduce2):
        (self.e_unit, self.r_unit, self.e_kept, self.r_kept, self.e_pair, self.e_across,
         self.r_from, self.e_low, self.r_low, self.e_got, self.r_got,
         self.loads, self.cores, self.e_z, self.r_z, self.homes) = refs
        self.out = (expand1, reduce1, expand2, reduce2)
        self.s, d = lax.axis_index("section"), lax.axis_index("dp")
        self.d, self.z, self.c = d, d // 2, d % 2
        self.h, self.p = self.s % 2, self.z % 2
        self.n = self.e_unit.shape[0]

    def load(self, x_got, da_got, we1, wr1, we2, wr2, held):
        self.x, self.da, self.xt, self.we, self.wr, self.m, self.du = held
        wide = self.we.shape[2]
        rows = [pltpu.make_async_copy(x_got, self.x, self.loads.at[0])]
        rows.append(pltpu.make_async_copy(da_got, self.da, self.loads.at[1]))
        start(rows)
        for which, (we, wr) in enumerate(((we1, wr1), (we2, wr2))):
            copies = []
            for i in range(self.n):
                at = pl.multiple_of((2 * i + self.h) * wide, 128)
                copies.append(
                    pltpu.make_async_copy(
                        we.at[:, pl.ds(at, wide)], self.we.at[i], self.loads.at[2 + 2 * i]
                    )
                )
                copies.append(
                    pltpu.make_async_copy(
                        wr.at[pl.ds(at, wide), :], self.wr.at[i], self.loads.at[3 + 2 * i]
                    )
                )

            @pl.when(self.s // 2 == which)
            def _(copies=copies):
                start(copies)

        self.copies = rows + copies

    def loaded(self):
        wait(self.copies)
        for t in range(self.x.shape[0]):
            rows = self.x.shape[1]
            self.xt[:, t * rows : (t + 1) * rows] = self.x[t].T

    def core_e(self, i):
        return pltpu.make_async_remote_copy(
            src_ref=self.e_unit.at[i, :, :, 1 - self.c], dst_ref=self.e_kept.at[i],
            send_sem=self.cores.at[0, i], recv_sem=self.cores.at[1, i],
            device_id=(self.s, self.z * 2 + 1 - self.c), device_id_type=MESH,
        )

    def core_r(self, i):
        rows = self.r_kept.shape[1]
        at = pl.ds(pl.multiple_of((1 - self.c) * rows, rows), rows)
        return pltpu.make_async_remote_copy(
            src_ref=self.r_unit.at[i, at], dst_ref=self.r_kept.at[i],
            send_sem=self.cores.at[2, i], recv_sem=self.cores.at[3, i],
            device_id=(self.s, self.z * 2 + 1 - self.c), device_id_type=MESH,
        )

    def pairs_e(self, i):
        return pltpu.make_async_remote_copy(
            src_ref=self.e_kept.at[i, :, 1 - self.p], dst_ref=self.e_pair.at[i],
            send_sem=self.e_z.at[0, i], recv_sem=self.e_z.at[1, i],
            device_id=(self.s, (self.z + 1 - 2 * self.p) * 2 + self.c), device_id_type=MESH,
        )

    def across_e(self, i):
        return pltpu.make_async_remote_copy(
            src_ref=self.e_kept.at[i, 1 - self.z // 2, self.p], dst_ref=self.e_across.at[i],
            send_sem=self.e_z.at[2, i], recv_sem=self.e_z.at[3, i],
            device_id=(self.s, (self.z + 2) % 4 * 2 + self.c), device_id_type=MESH,
        )

    def straight_r(self, i):
        slot = jnp.maximum((self.z - i + self.n) % self.n - 1, 0)
        return pltpu.make_async_remote_copy(
            src_ref=self.r_kept.at[i], dst_ref=self.r_from.at[slot],
            send_sem=self.r_z.at[0, i], recv_sem=self.r_z.at[1, slot],
            device_id=(self.s, i * 2 + self.c), device_id_type=MESH,
        )

    def make(self, i):
        parts, rows, width = self.x.shape
        wide = self.we.shape[2]

        u = [mm(self.x[t], self.we[i]).astype(BF) for t in range(parts)]
        dm = [mm_nt(self.da[t], self.wr[i]) for t in range(parts)]
        for t in range(parts):
            m, slope = gelu_both(u[t].astype(F32))
            self.m[t * rows : (t + 1) * rows, :] = m.astype(BF)
            self.du[t * rows : (t + 1) * rows, :] = (dm[t] * slope).astype(BF)
        r = self.e_unit.shape[4]

        def columns_of(z, _):
            at = pl.ds(pl.multiple_of(z * 2 * r, 2 * r), 2 * r)
            g = mm(self.xt[at, :], self.du[...]).astype(BF)
            for c in range(2):
                self.e_unit[i, z // 2, z % 2, c] = g[c * r : (c + 1) * r]
            return 0

        lax.fori_loop(0, self.n, columns_of, 0)
        self.core_e(i).start()
        for at in range(0, width, 256):
            self.r_unit[i, :, at : at + 256] = mm_tn(
                self.m[...], self.da[:, :, at : at + 256].reshape(parts * rows, 256)
            ).astype(BF)
        self.core_r(i).start()

    def over_cores(self, i):
        self.core_e(i).wait()

        def step(z, _):
            at = (i, z // 2, z % 2)
            self.e_kept[at] = self.e_kept[at] + self.e_unit[(*at, self.c)]
            return 0

        lax.fori_loop(0, self.n, step, 0)
        self.pairs_e(i).start()
        self.core_r(i).wait()
        rows = self.r_kept.shape[1]
        own = pl.ds(pl.multiple_of(self.c * rows, rows), rows)
        self.r_kept[i] = self.r_kept[i] + self.r_unit[i, own]
        pl.when(self.z != i)(self.straight_r(i).start)

    def over_pairs(self, i):
        self.pairs_e(i).wait()
        for t in range(2):
            self.e_kept[i, t, self.p] = self.e_kept[i, t, self.p] + self.e_pair[i, t]
        self.across_e(i).start()

    def home_e(self, t):
        return pltpu.make_async_remote_copy(
            src_ref=self.e_low.at[t], dst_ref=self.e_got.at[self.s],
            send_sem=self.homes.at[0, t], recv_sem=self.homes.at[1, self.s],
            device_id=(t, self.d), device_id_type=MESH,
        )

    def home_r(self, t):
        return pltpu.make_async_remote_copy(
            src_ref=self.r_low.at[t], dst_ref=self.r_got.at[self.s // 2, self.c],
            send_sem=self.homes.at[2, t], recv_sem=self.homes.at[3, self.s // 2 * 2 + self.c],
            device_id=(t, self.z * 2 + self.h), device_id_type=MESH,
        )

    def over_z_e(self):
        for i in range(self.n):
            self.across_e(i).wait()
            total = self.e_kept[i, self.z // 2, self.p].astype(F32) + self.e_across[i].astype(F32)
            self.e_low[i] = total.astype(BF)

            @pl.when(self.s == i)
            def _(i=i):
                self.e_got[i] = self.e_low[i]

            pl.when(self.s != i)(self.home_e(i).start)

    def over_z_r(self):
        parts, rows, wide = self.r_low.shape
        own = self.r_kept.shape[2] // parts
        for i in range(self.n):
            pl.when(self.z != i)(self.straight_r(i).wait_send)
        for k in range(1, self.n):
            pltpu.make_async_remote_copy(
                src_ref=self.r_kept.at[0], dst_ref=self.r_from.at[k - 1],
                send_sem=self.r_z.at[0, 0], recv_sem=self.r_z.at[1, k - 1],
                device_id=(self.s, (self.z + k) % self.n * 2 + self.c), device_id_type=MESH,
            ).wait_recv()
        step = rows // 2
        for at in range(0, rows, step):
            total = self.r_kept[self.z, at : at + step].astype(F32)
            for k in range(self.n - 1):
                total = total + self.r_from[k, at : at + step].astype(F32)
            total = total.astype(BF)
            for t in range(parts):
                low, _ = window(t, own)
                self.r_low[t, at : at + step] = total[:, low : low + wide]
        for t in range(parts):
            stays = (self.s == t) & (self.c == self.h)
            pl.when(jnp.logical_not(stays))(self.home_r(t).start)

            @pl.when(stays)
            def _(t=t):
                self.r_got[self.s // 2, self.c] = self.r_low[t]

    def finish(self):
        parts = self.e_low.shape[0]
        for t in range(parts):
            pl.when(self.s != t)(self.home_e(t).wait_send)
            stays = (self.s == t) & (self.c == self.h)
            pl.when(jnp.logical_not(stays))(self.home_r(t).wait_send)
        for t in range(parts):
            copy = pltpu.make_async_remote_copy(
                src_ref=self.e_low.at[0], dst_ref=self.e_got.at[t],
                send_sem=self.homes.at[0, 0], recv_sem=self.homes.at[1, t],
                device_id=(self.s ^ 1, self.d), device_id_type=MESH,
            )
            pl.when(self.s != t)(copy.wait_recv)
        for which in range(2):
            for core in range(2):
                copy = pltpu.make_async_remote_copy(
                    src_ref=self.r_low.at[0], dst_ref=self.r_got.at[which, core],
                    send_sem=self.homes.at[2, 0], recv_sem=self.homes.at[3, 2 * which + core],
                    device_id=(self.s ^ 1, self.d), device_id_type=MESH,
                )
                stays = (self.s == 2 * which + self.c) & (self.c == core)
                pl.when(jnp.logical_not(stays))(copy.wait_recv)
        wide = self.e_got.shape[2]
        own = self.out[1].shape[1]
        shift = self.s * own % 128
        for which in range(2):
            expand, reduce = self.out[2 * which : 2 * which + 2]
            for h in range(2):
                expand[:, h * wide : (h + 1) * wide] = self.e_got[2 * which + h].astype(F32)
            for core in range(2):
                block = self.r_got[which, core].astype(F32)
                out = block[:, :own]
                for offset in sorted({window(t, own)[1] for t in range(parts)} - {0}):
                    out = jnp.where(shift == offset, block[:, offset : offset + own], out)
                reduce[core * block.shape[0] : (core + 1) * block.shape[0], :] = out


def tail_kernel(query_count, head_size, *refs):
    refs = list(refs)

    def take(count):
        out = refs[:count]
        del refs[:count]
        return out

    final_blocks, dq_blocks = take(2)
    x_got, da_got, we1, wr1, we2, wr2 = take(6)
    low3, djoined2, mixed2, da4 = take(4)
    low1, mixed1, da2, x0, mixed_self1 = take(5)
    wq_hbm, wo_hbm, wp_hbm = take(3)
    dz2_hbm, n1_hbm, joined1_hbm = take(3)
    pair_unit, r1, gains, dg_mid, temper_rows = take(5)
    final_got, dx_got, small = take(3)
    expand2, reduce2, project2, out2, expand1, reduce1, asker, image_out, project1, out1 = take(10)
    pair_out = take(1)[0]
    units = ("self2", "self1", "image")
    straight = ("image",)
    buffers = {name: take(6) for name in units}
    pair_kept, pair_from_z, pair_low, pair_got = take(4)
    wide, sends, recvs, slots_a, slots_b, slots_c, slots_d, loads = take(8)
    slots = (slots_a, slots_b, slots_c, slots_d)
    dq_got, dqr, da1, djoined1, dx_blocks, sums, state_sends, state_recvs, local = take(9)
    dz2, n1, joined1 = take(3)
    owned = Owned(refs, expand1, reduce1, expand2, reduce2)
    own_heads = temper_rows.shape[1] // query_count

    s, d = lax.axis_index("section"), lax.axis_index("dp")
    z, c = d // 2, d % 2

    homes = {}
    for i, name in enumerate(units):
        unit = wide.at[:, :, :, :, : buffers[name][0].shape[3]]
        homes[name] = Home(unit, *buffers[name], sends.at[i], recvs.at[i])
    homes["pair"] = Home(
        pair_unit, pair_kept, None, None, None, None, pair_from_z,
        sends.at[len(units)], recvs.at[len(units)],
    )
    factors = {
        "self2": (low3, djoined2, mixed2, da4), "self1": (x0, djoined1, mixed_self1, da1),
        "image": (low1, dqr, mixed1, da2),
    }
    results = {
        "self2": (project2, out2), "self1": (project1, out1), "image": (asker, image_out),
    }

    def held(name):
        return [
            slots[j].at[:, : source.shape[1]] for j, source in enumerate(factors[name])
        ]

    def fetch(name):
        return [
            pltpu.make_async_copy(source, target, loads.at[units.index(name), j])
            for j, (source, target) in enumerate(zip(factors[name], held(name)))
        ]

    def make(name):
        wait(fetch(name))
        fill_pair(homes[name].unit, *held(name))
        start(homes[name].cores())

    def finish(name):
        home = homes[name]
        wait(home.direct() if name in straight else home.across())
        total = home.total((0, 1, 2) if name in straight else (2,))
        out = results[name]
        own = out[0].shape[1]
        out[0][...] = total[:, :own]
        out[1][...] = total[:, own:]

    steps = [("dp", 1), ("section", 1), ("section", 2)]
    bit = 2
    while bit < lax.axis_size("dp"):
        steps.append(("dp", bit))
        bit *= 2

    def small_copy(k):
        axis, bit = steps[k]
        to = (s ^ bit, d) if axis == "section" else (s, d ^ bit)
        return [pltpu.make_async_remote_copy(
            src_ref=small, dst_ref=sums.at[k], send_sem=state_sends.at[8 + k],
            recv_sem=state_recvs.at[8 + k], device_id=to, device_id_type=MESH,
        )]

    def small_step(k):
        if k > 0:
            wait(small_copy(k - 1))
            small[...] = small[...] + sums[k - 1]
        if k < len(steps):
            start(small_copy(k))

    finals = exchange_copies(
        final_blocks, final_got, state_sends.at[pl.ds(0, 4)], state_recvs.at[pl.ds(0, 4)]
    )
    dqs = exchange_copies(
        dq_blocks, dq_got, state_sends.at[pl.ds(4, 4)], state_recvs.at[pl.ds(4, 4)]
    )
    dxs = exchange_copies(dx_blocks, dx_got, state_sends.at[pl.ds(16, 4)], state_recvs.at[pl.ds(16, 4)])

    saved = [
        pltpu.make_async_copy(source, target, local.at[3 + i])
        for i, (source, target) in enumerate(
            ((dz2_hbm, dz2), (n1_hbm, n1), (joined1_hbm, joined1))
        )
    ]

    def rest_of_states(wq, wo, wp, do):
        own = wq.shape[1] // dq_got.shape[0]
        wait(dqs)
        wait(saved)
        wait([pltpu.make_async_copy(*one) for one in
              ((wq_hbm, wq, local.at[0]), (wo_hbm, wo, local.at[1]), (wp_hbm, wp, local.at[2]))])
        dqr[...] = take_blocks(dq_got, own)
        d1 = dz2[...] + mm_nt(dqr[...], wq[...])
        dz, dg = norm_back(d1, gains[0:1, :], n1[...], r1[...])
        da1[...] = dz.astype(BF)
        do[...] = mm_nt(da1[...], wo[...]).astype(BF)
        attend_self_back(joined1, do, djoined1, query_count, head_size)
        put_blocks(dx_blocks, (dz + back_through(djoined1, wp)).astype(BF))
        width = small.shape[1]
        lane = lax.broadcasted_iota(jnp.int32, (1, width), 1)
        row = jnp.zeros((1, width), F32)
        for h in range(own_heads):
            one = jnp.sum(
                jnp.where(head_lanes(temper_rows.shape, h, query_count), temper_rows[...], 0.0),
                keepdims=True,
            )
            row = row + jnp.where(lane == s * own_heads + h, one, 0.0)
        small[...] = jnp.concatenate(
            [dg[None, :], dg_mid[...], row, jnp.zeros((2, width), F32)], axis=0
        )

    def pair_copy(half):
        to = 2 * half + s // 2
        return to, pltpu.make_async_remote_copy(
            src_ref=pair_low.at[half], dst_ref=pair_got.at[s % 2],
            send_sem=state_sends.at[20 + half], recv_sem=state_recvs.at[20 + s % 2],
            device_id=(to, d), device_id_type=MESH,
        )

    def send_pair():
        wait(homes["pair"].direct())
        total = homes["pair"].total((0, 1, 2)).astype(BF)
        own = total.shape[1] // 2
        for half in range(2):
            pair_low[half] = total[:, half * own : (half + 1) * own]
            to, copy = pair_copy(half)

            @pl.when(to != s)
            def _(copy=copy):
                copy.start()

            @pl.when(to == s)
            def _(half=half):
                pair_got[s % 2] = pair_low[half]

    def finish_pair():
        for half in range(2):
            to, copy = pair_copy(half)

            @pl.when(to != s)
            def _(copy=copy):
                copy.wait_send()

        for j in range(2):
            source = 2 * (s % 2) + j

            @pl.when(source != s)
            def _(j=j):
                pltpu.make_async_remote_copy(
                    src_ref=pair_low.at[0], dst_ref=pair_got.at[j],
                    send_sem=state_sends.at[20], recv_sem=state_recvs.at[20 + j],
                    device_id=(s ^ 1, d), device_id_type=MESH,
                ).wait_recv()

        own = pair_got.shape[2]
        for j in range(2):
            pair_out[:, j * own : (j + 1) * own] = pair_got[j].astype(F32)

    def over_cores(name):
        wait(homes[name].cores())
        homes[name].add_cores()
        start(homes[name].first())

    def over_first(name):
        wait(homes[name].first())
        homes[name].add_first()
        start(homes[name].second())

    def over_second(name):
        wait(homes[name].second())
        homes[name].add_second()
        start(homes[name].direct() if name in straight else homes[name].pairs())

    def over_pairs(name):
        wait(homes[name].pairs())
        homes[name].add_pairs()
        start(homes[name].across())

    parts, rows, width = x_got.shape
    block = we1.shape[1] // lax.axis_size("dp")
    n = owned.n
    start(fetch("self2"))

    def first_part(wq, wo, wp, do, *held):
        owned.load(x_got, da_got, we1, wr1, we2, wr2, held)
        start([pltpu.make_async_copy(*one) for one in
               ((wq_hbm, wq, local.at[0]), (wo_hbm, wo, local.at[1]), (wp_hbm, wp, local.at[2]))])
        start(saved)
        greet()
        start(homes["pair"].cores())
        make("self2")
        start(dqs)
        owned.loaded()
        wait(homes["pair"].cores())
        homes["pair"].add_cores()
        start(homes["pair"].direct())
        start(finals)
        owned.make(0)
        owned.make(1)
        owned.over_cores(0)
        over_cores("self2")
        owned.make(2)
        owned.over_cores(1)
        rest_of_states(wq, wo, wp, do)
        start(fetch("self1"))
        start(dxs)
        small_step(0)
        owned.over_pairs(1)
        owned.over_cores(2)
        over_first("self2")
        make("self1")
        start(fetch("image"))
        small_step(1)
        owned.make(3)
        over_cores("self1")
        owned.over_pairs(2)
        owned.over_cores(3)
        make("image")
        send_pair()
        over_second("self2")
        owned.over_pairs(3)
        owned.over_pairs(0)
        over_first("self1")
        over_pairs("self2")
        over_cores("image")
        small_step(2)
        wait(finals)
        small_step(3)
        over_second("self1")
        owned.over_z_e()
        over_first("image")
        wait(dxs)
        finish_pair()
        over_pairs("self1")
        small_step(4)
        owned.over_z_r()
        over_second("image")
        finish("self2")
        owned.finish()
        finish("self1")
        small_step(5)
        finish("image")

    pl.run_scoped(
        first_part, *[pltpu.VMEM(w.shape, BF) for w in (wq_hbm, wo_hbm, wp_hbm)],
        pltpu.VMEM(da1.shape, BF),
        *[
            pltpu.VMEM(dims, BF)
            for dims in (
                (parts, rows, width), (parts, rows, width), (width, parts * rows),
                (n, width, block), (n, block, width),
                (parts * rows, block), (parts * rows, block),
            )
        ],
    )


def tail(operands, sections, dp, width, hidden, feat, query_count, head_size):
    n = dp // 2
    rows, most = operands[8].shape[0], operands[9].shape[1]
    r, own, wide_own = width // dp, width // sections, hidden // sections
    lanes = operands[0].shape[2]
    pair_r, pair_w = feat // dp, 2 * own

    def buffers(w):
        return [
            pltpu.VMEM((sections, n, r, w), BF),
            pltpu.VMEM((2, n, r // 2, w), BF), pltpu.VMEM((2, n, r // 2, w), BF),
            pltpu.VMEM((n, r // 2, w), BF), pltpu.VMEM((n, r // 2, w), BF),
            pltpu.VMEM((n - 1, r, w), BF),
        ]

    results = [
        shape((sections, rows, lanes), BF), shape((sections, rows, lanes), BF),
        shape((8, width), F32),
        shape((r, wide_own), F32), shape((hidden // dp, own), F32),
        shape((r, 3 * own), F32), shape((r, own), F32),
        shape((r, wide_own), F32), shape((hidden // dp, own), F32),
        shape((r, own), F32), shape((r, own), F32),
        shape((r, 3 * own), F32), shape((r, own), F32),
        shape((pair_r, pair_w), F32),
    ]
    scratch = []
    for w in (4 * own,) * 2 + (2 * own,):
        scratch += buffers(w)
    scratch += [
        pltpu.VMEM((1, n, pair_r, pair_w), BF),
        pltpu.VMEM((n - 1, pair_r, pair_w), BF),
        pltpu.VMEM((2, pair_r, own), BF), pltpu.VMEM((2, pair_r, own), BF),
        pltpu.VMEM((sections, n, 2, r, 4 * own), BF),
        pltpu.SemaphoreType.DMA((8, 10)), pltpu.SemaphoreType.DMA((8, 10)),
        pltpu.VMEM((rows, width), BF), pltpu.VMEM((rows, most), BF),
        pltpu.VMEM((rows, width), BF), pltpu.VMEM((rows, width), BF),
        pltpu.SemaphoreType.DMA((8, 4)),
        pltpu.VMEM((sections, rows, lanes), BF),
        pltpu.VMEM((rows, width), BF), pltpu.VMEM((rows, width), BF),
        pltpu.VMEM((rows, 3 * width), BF), pltpu.VMEM((sections, rows, lanes), BF),
        pltpu.VMEM((8, 8, width), F32),
        pltpu.SemaphoreType.DMA((24,)), pltpu.SemaphoreType.DMA((24,)),
        pltpu.SemaphoreType.DMA((6,)),
        pltpu.VMEM((rows, width), F32), pltpu.VMEM((rows, width), F32),
        pltpu.VMEM((rows, 3 * width), BF),
    ]
    block = hidden // dp
    scratch += [
        pltpu.VMEM((n, 2, 2, 2, r, block), BF), pltpu.VMEM((n, block, width), BF),
        pltpu.VMEM((n, 2, 2, r, block), BF), pltpu.VMEM((n, block // 2, width), BF),
        pltpu.VMEM((n, 2, r, block), BF), pltpu.VMEM((n, r, block), BF),
        pltpu.VMEM((n - 1, block // 2, width), BF),
        pltpu.VMEM((n, r, block), BF), pltpu.VMEM((sections, block // 2, lanes), BF),
        pltpu.VMEM((sections, r, block), BF), pltpu.VMEM((2, 2, block // 2, lanes), BF),
        pltpu.SemaphoreType.DMA((2 + 2 * n + sections,)), pltpu.SemaphoreType.DMA((4, n)),
        pltpu.SemaphoreType.DMA((4, n)), pltpu.SemaphoreType.DMA((4, n)),
        pltpu.SemaphoreType.DMA((4, sections)),
    ]
    return pl.pallas_call(
        functools.partial(tail_kernel, query_count, head_size),
        out_shape=results,
        in_specs=[whole(pl.ANY)] * 23 + [whole()] * 5,
        out_specs=[whole(pl.ANY)] * 2 + [whole()] * 12,
        scratch_shapes=scratch,
        compiler_params=pltpu.CompilerParams(
            vmem_limit_bytes=LIMIT, collective_id=2, has_side_effects=True
        ),
    )(*operands)


def body(
    starting_learned_vectors,
    frozen_picture_vectors,
    texts_per_picture,
    early_triple_matrix,
    early_mixing_exit_matrix,
    picture_asker_matrix,
    picture_pair_matrix,
    picture_exit_matrix,
    early_widen_matrix,
    early_narrow_matrix,
    later_triple_matrix,
    later_mixing_exit_matrix,
    later_widen_matrix,
    later_narrow_matrix,
    standardizer_factors,
    picture_divisors,
    closing_cotangent,
):
    sections = lax.axis_size("section")
    dp = lax.axis_size("dp")
    me = lax.axis_index("section")
    item_count, query_count, width = starting_learned_vectors.shape
    heads = picture_divisors.shape[0]
    images, patches, feat = frozen_picture_vectors.shape
    own_items = item_count // sections
    rows = own_items * query_count
    own_heads = heads // sections
    head_size = width // heads
    own_width = width // sections
    wide = -(-own_width // 128) * 128
    padded = -(-patches // 16) * 16
    hidden = early_widen_matrix.shape[1]
    gains = standardizer_factors

    clamped = jnp.clip(picture_divisors, 0.5, 2.0)
    scale_all = 1.0 / math.sqrt(head_size) / clamped

    def act(*dims, dtype=BF):
        return shape((rows,) + dims, dtype)

    def blocks():
        return (sections, rows, wide)

    def comm(kernel, outs, args, specs, out_specs, scratch, identity):
        params = pltpu.CompilerParams(vmem_limit_bytes=LIMIT)
        if identity is not None:
            params = pltpu.CompilerParams(
                vmem_limit_bytes=LIMIT, collective_id=identity, has_side_effects=True
            )
        return pl.pallas_call(
            kernel, out_shape=outs, in_specs=specs, out_specs=out_specs, scratch_shapes=scratch,
            compiler_params=params,
        )(*args)

    sems = pltpu.SemaphoreType.DMA
    stored = (
        act(width), act(width, dtype=F32), act(width), act(width, dtype=F32),
        act(3 * width), act(width), shape(blocks(), BF), shape((images, padded, 2 * wide), BF),
    )
    x0, h1, low1, n1, joined1, mixed_self1, q_got, keyval, r1, mixed1_rows = comm(
        functools.partial(front_kernel, query_count, head_size, own_heads),
        stored + (act(1, dtype=F32), act(width)),
        (
            texts_per_picture, picture_divisors, gains, starting_learned_vectors,
            frozen_picture_vectors, early_triple_matrix, early_mixing_exit_matrix,
            picture_asker_matrix, picture_pair_matrix,
        ),
        [whole(SMEM), whole(SMEM), whole()] + [whole(pl.ANY)] * 6,
        [whole(pl.ANY)] * len(stored) + [whole()] * 2,
        [pltpu.VMEM(one.shape, one.dtype) for one in stored]
        + [
            pltpu.VMEM((own_items, query_count, width), BF),
            pltpu.VMEM(early_triple_matrix.shape, BF), pltpu.VMEM((width, width), BF),
            pltpu.VMEM((width, width), BF), pltpu.VMEM((feat, 2 * wide), BF),
            pltpu.VMEM((4, patches, feat), BF),
            pltpu.VMEM(blocks(), BF), pltpu.VMEM(blocks(), BF), pltpu.VMEM(blocks(), BF),
            sems((6,)), sems((4,)), sems((4,)), sems((4,)), sems((4,)), sems((4,)),
            sems((len(stored),)),
        ],
        0,
    )

    weights = (
        picture_exit_matrix, early_widen_matrix, early_narrow_matrix, later_triple_matrix,
        later_mixing_exit_matrix, later_widen_matrix, later_narrow_matrix,
    )
    owners = width // dp % 32 == 0 and feat // dp % 16 == 0 and hidden // dp % 128 == 0
    factors = (
        act(width), act(hidden), act(hidden), act(width),
        act(width), act(hidden), act(hidden), act(width),
    )
    everywhere = shape((sections, rows, width), BF)
    early = (shape(blocks(), BF), act(width), act(width), act(3 * width), act(width))
    final_blocks, low3, mixed2, djoined2, da4, do_blocks, da2, dz2, dg_mid, *given = comm(
        functools.partial(middle_kernel, query_count, head_size, owners),
        early
        + (shape(blocks(), BF), act(width), act(width, dtype=F32), shape((4, width), F32))
        + ((everywhere, act(width), act(width)) if owners else factors),
        (h1, mixed1_rows, gains, closing_cotangent) + weights,
        [whole()] * 3 + [whole(pl.ANY)] * (1 + len(weights)),
        [whole(pl.ANY)] * len(early) + [whole()] * 4
        + ([whole(pl.ANY)] + [whole()] * 2 if owners else [whole()] * len(factors)),
        ([pltpu.VMEM(f.shape, BF) for f in factors] if owners else [])
        + [pltpu.VMEM(w.shape, BF) for w in weights]
        + [pltpu.VMEM((own_items, query_count, width), BF)]
        + [sems((len(weights) + 1,)), sems((2, 2)), sems((sections,))]
        + [pltpu.VMEM(one.shape, BF) for one in early]
        + [sems((len(early),))]
        + [pltpu.VMEM((rows, hidden), F32)] * 2
        + [pltpu.VMEM((rows, 3 * width), BF), pltpu.VMEM((rows, width), BF)]
        + [pltpu.VMEM((rows, width), F32), pltpu.VMEM((rows, 1), F32)] * 4,
        1 if owners else None,
    )

    if owners:
        x_got, da_own, da_other = given
        pair_block_rows = feat // dp
        dq_blocks, da_got, temper_rows, pair_unit = comm(
            functools.partial(image_back_kernel, query_count, head_size, own_heads),
            (
                shape(blocks(), BF), everywhere, shape((1, own_heads * query_count), F32),
                shape((1, dp // 2, 2, pair_block_rows, 2 * own_width), BF),
            ),
            (
                texts_per_picture, picture_divisors, q_got, do_blocks, da_own, da_other, keyval,
                frozen_picture_vectors,
            ),
            [whole(SMEM), whole(SMEM), whole()] + [whole(pl.ANY)] * 5,
            [whole(), whole(pl.ANY), whole(), whole()],
            [
                pltpu.VMEM(blocks(), BF),
                pltpu.VMEM((images, padded, 2 * wide), BF),
                pltpu.VMEM((item_count, padded, own_heads * query_count), F32),
                pltpu.VMEM((item_count, padded, own_heads * query_count), F32),
                pltpu.VMEM((item_count, padded, 2 * wide), BF),
                pltpu.VMEM((padded, 2 * wide), F32),
                pltpu.VMEM((2, 2, patches, feat), BF),
                pltpu.VMEM((2 * wide, feat), F32),
                pltpu.VMEM((16, feat), F32), pltpu.VMEM((16, 2 * wide), F32),
                sems((1,)), sems((2,)), sems((4,)), sems((4,)), sems((4,)), sems((4,)),
            ],
            3,
        )
    else:
        do_got, final_got = exchange(do_blocks), exchange(final_blocks)
        dq, dkv, temper_rows = call(
            functools.partial(
                attend_image_back_kernel, patches, own_heads, head_size, query_count, 8
            ),
            (
                shape((sections * rows, wide), BF),
                shape((images, padded, 2 * wide), BF),
                shape((1, own_heads * query_count), F32),
            ),
            texts_per_picture, picture_divisors, q_got.reshape(sections * rows, wide),
            do_got.reshape(sections * rows, wide), keyval,
            in_specs=[whole(SMEM), whole(SMEM), whole(), whole(), whole()],
            scratch=[pltpu.VMEM((images, padded, 2 * wide), F32)],
        )

    interior = ((picture_divisors > 0.5) & (picture_divisors < 2.0)).astype(F32)
    temper_factor = (-scale_all / clamped) * interior
    if owners:
        (
            final_got, dx_got, small, expand2, reduce2, project2, out2, expand1, reduce1,
            asker, image_out, project1, out1, pair_part,
        ) = tail(
            (
                final_blocks, dq_blocks, x_got, da_got, early_widen_matrix, early_narrow_matrix,
                later_widen_matrix, later_narrow_matrix, low3, djoined2, mixed2, da4,
                low1, mixed1_rows, da2, x0, mixed_self1,
                picture_asker_matrix, early_mixing_exit_matrix, early_triple_matrix,
                dz2, n1, joined1, pair_unit, r1, gains, dg_mid, temper_rows,
            ),
            sections, dp, width, hidden, feat, query_count, head_size,
        )
        gains_grad = small[:5]
        temper_grad = small[5, :heads] * temper_factor
    else:
        low2, m1, du1, da3, low4, m2, du2, da5 = given
        dq_blocks = exchange(dq.reshape(sections, rows, wide))
        d_pair = pl.pallas_call(
            keyval_grad_kernel,
            out_shape=shape((feat, 2 * own_width), BF),
            grid=(images,),
            in_specs=[
                pl.BlockSpec((1, patches, feat), lambda j: (j, 0, 0)),
                pl.BlockSpec((1, padded, 2 * wide), lambda j: (j, 0, 0)),
            ],
            out_specs=pl.BlockSpec((feat, 2 * own_width), lambda j: (0, 0)),
            scratch_shapes=[pltpu.VMEM((2 * wide, feat), F32)],
            compiler_params=pltpu.CompilerParams(vmem_limit_bytes=LIMIT),
        )(frozen_picture_vectors, dkv)

        dq_rows, da1, djoined1, dx_blocks, dg0 = call(
            functools.partial(last_kernel, query_count, head_size),
            (
                act(width), act(width), act(3 * width),
                shape((sections, rows, wide), BF), shape((1, width), F32),
            ),
            dz2, dq_blocks, picture_asker_matrix, n1, r1, gains, early_mixing_exit_matrix, joined1,
            early_triple_matrix,
            scratch=[pltpu.VMEM((rows, width), BF)],
        )

        def block_unit(grad):
            parts, k, own = grad.shape
            return grad.reshape(parts, dp, k // dp, own)

        def pair_grad(x, dy, y, dz):
            own = (dy.shape[1] + dz.shape[1]) // sections
            return block_unit(
                call(pair_weight_kernel, shape((sections, x.shape[1], own), BF), x, dy, y, dz)
            )

        expand2 = home(block_unit(expand_grad(low4, du2, sections)))
        reduce2 = home(reduce_grad(da5, m2, sections, dp)).T
        self2 = home(pair_grad(low3, djoined2, mixed2, da4))
        expand1 = home(block_unit(expand_grad(low2, du1, sections)))
        reduce1 = home(reduce_grad(da3, m1, sections, dp)).T
        pair_block = line_sum(
            core_sum(d_pair.reshape(1, dp, feat // dp, 2 * own_width))[0]
        )
        image_units = home(pair_grad(low1, dq_rows, mixed1_rows, da2))
        self1 = home(pair_grad(x0, djoined1, mixed_self1, da1))
        third = 3 * own_width
        project2, out2 = self2[:, :third], self2[:, third:]
        project1, out1 = self1[:, :third], self1[:, third:]
        asker, image_out = image_units[:, :own_width], image_units[:, own_width:]

        pair_rows = pair_block.shape[0]
        half = sections // 2
        pair_halves = pair_block.astype(BF).reshape(pair_rows, 2, own_width).transpose(1, 0, 2)
        key_home, val_home = me // 2, half + me // 2
        sent = jnp.zeros((sections, pair_rows, own_width), BF)
        sent = lax.dynamic_update_index_in_dim(sent, pair_halves[0], key_home, 0)
        sent = lax.dynamic_update_index_in_dim(sent, pair_halves[1], val_home, 0)
        got = exchange(sent)
        first = (me % half) * 2
        pair_part = lax.dynamic_slice_in_dim(got, first, 2, 0)
        pair_part = pair_part.transpose(1, 0, 2).reshape(pair_rows, 2 * own_width).astype(F32)

        dx_got = exchange(dx_blocks)
        d_temper = jnp.sum(temper_rows.reshape(own_heads, query_count), axis=1)
        spread = jnp.zeros((heads,), F32)
        spread = lax.dynamic_update_slice_in_dim(spread, d_temper, me * own_heads, 0)
        small = all_sum(jnp.concatenate([dg0.reshape(-1), dg_mid.reshape(-1), spread]))
        gains_grad = small[: 5 * width].reshape(5, width)
        temper_grad = small[5 * width :] * temper_factor

    grads = (
        project1, out1, asker, pair_part, image_out, expand1, reduce1,
        project2, out2, expand2, reduce2, gains_grad,
    )
    grads = [grad.astype(F32) for grad in grads]
    states = [shape((item_count * query_count, own_width), F32)] * 2
    turned = [grad.shape[0] > grad.shape[1] for grad in grads]
    results = states + [
        shape(grad.shape[::-1] if turn else grad.shape, F32) for grad, turn in zip(grads, turned)
    ]
    final_part, grad_part, *grads = pl.pallas_call(
        functools.partial(deliver_kernel, own_width),
        out_shape=results,
        in_specs=[whole()] * (2 + len(grads)),
        out_specs=[whole()] * (2 + len(grads)),
        compiler_params=pltpu.CompilerParams(vmem_limit_bytes=LIMIT),
    )(final_got, dx_got, *grads)
    grads = [grad.T if turn else grad for grad, turn in zip(grads, turned)]
    states = (item_count, query_count, own_width)
    return (
        final_part.reshape(states),
        grad_part.reshape(states),
        *grads,
        temper_grad,
    )


def solution(mesh):
    return jax.shard_map(
        body,
        mesh=mesh,
        in_specs=(P("dp", None, None), P("dp", None, None), P("dp", None))
        + (P(),) * 13
        + (P("dp", None, None),),
        out_specs=(P("dp", None, "section"),) * 2 + (P("dp", "section"),) * 11 + (P(), P()),
        check_vma=False,
    )
```
